32 devices in a mesh: ctx: 4 (over z), ch: 8 (over y, x, core).
Axes of the slice: x: 2, y: 2, z: 4, core: 2. Of those that a mesh axis runs over, the one named last changes fastest.
Arguments:
- features: bfloat16 [2, 4, 128, 3, 4096], P(None, 'ctx', None, None, 'ch'), may hold values from -6 to 6
- short_weight: bfloat16 [7, 3, 4096], P(None, None, 'ch'), may hold values from -2 to 2
- long_filter: bfloat16 [2, 4, 128, 4096], P(None, 'ctx', None, 'ch'), may hold values from -0.25 to 0.25
- skip_gain: float32 [4096], P('ch'), may hold values from -4 to 4
- out_weight: bfloat16 [4096, 4096], P('ch'), may hold values from -0.125 to 0.125
Outputs:
- mixed: bfloat16 [2, 4, 128, 4096], P(None, 'ctx', None, 'ch')
The draws below stay inside these ranges and needn't reach their ends.
All inputs are finite; a program needn't handle non-finite values.
Results may differ from the reference program's by a relative error of at most 0.015.
Values may be sent and summed in bfloat16 or wider, within the bound.
A program may use at most 128 MiB of HBM per device.

```python
import jax
import jax.numpy as jnp

D = 4096
BLOCK = 128
TAPS = 7
PAIRS = 4
SEQ = 1024


def strengthened(values, key, source, target, blocks, factor):
    def block_of(position):
        return (jnp.arange(values.shape[position]) // (values.shape[position] // blocks)).reshape((-1,) + (1,) * (values.ndim - 1 - position))

    first = jax.random.permutation(key, blocks)[block_of(target)]
    other_side = (block_of(target) + blocks // 2) % blocks
    return jnp.where((block_of(source) == first) | (block_of(source) == other_side), factor * values, values)


def block_levels(own_key, extent, split, low, high):
    def one(dim, parts):
        heights = jax.random.uniform(jax.random.fold_in(jax.random.fold_in(own_key, 6), dim), (parts,), jnp.float32, low / len(split), high / len(split))
        return jnp.repeat(jnp.exp(heights), extent[dim] // parts).reshape((-1,) + (1,) * (len(extent) - dim - 1))

    factor_of = one(*split[0])
    for cut in split[1:]:
        factor_of = factor_of * one(*cut)
    return factor_of


def gaussian(stream_key, shape, width, bound, shards=(), held_as=jnp.bfloat16):
    entries = width * jax.random.normal(stream_key, shape, jnp.float32)
    if shards:
        entries = entries * block_levels(stream_key, shape, shards, -0.22, 0.18)
    return jnp.clip(entries, -bound, bound).astype(held_as)


def bell_draw_with(key, extent, deviation, most, shards, heavy, kind=jnp.bfloat16):
    result = deviation * jax.random.normal(key, extent, jnp.float32)
    if shards:
        result = result * block_levels(key, extent, shards, -0.22, 0.18)
    return jnp.clip(strengthened(result, jax.random.fold_in(key, 3), *heavy), -most, most).astype(kind)


def setup_inputs(seed: int = 0) -> dict:
    seeds = jax.random.split(jax.random.key(seed), 6)
    return {
        "features": gaussian(seeds[0], (2, PAIRS, BLOCK, 3, D), 1.0, 6.0, ((1, 4), (4, 8))),
        "short_weight": gaussian(seeds[1], (TAPS, 3, D), TAPS ** -0.5, 2.0, ((2, 8),)),
        "long_filter": gaussian(seeds[2], (2, PAIRS, BLOCK, D), (SEQ // 2) ** -0.5, 0.25, ((1, 4), (3, 8))),
        "skip_gain": gaussian(seeds[3], (D,), 1.0, 4.0, ((0, 8),), jnp.float32),
        "out_weight": bell_draw_with(seeds[4], (D, D), D ** -0.5, 0.125, ((0, 8),), (0, 1, 8, 2.0)),
    }


def ordered(blocks):
    return jnp.concatenate([blocks[0], jnp.flip(blocks[1], axis=0)], axis=0)


def reference(features, short_weight, long_filter, skip_gain, out_weight):
    sequence = ordered(features).reshape((SEQ, 3, D)).astype(jnp.float32)
    margin_rows = TAPS - 1
    padded = jnp.pad(sequence, ((margin_rows, 0), (0, 0), (0, 0)))
    kernel = short_weight.astype(jnp.float32)
    featured = jnp.zeros_like(sequence)
    for offset in range(TAPS):
        featured = featured + kernel[offset] * padded[margin_rows - offset: margin_rows - offset + SEQ]
    queries = featured[:, 0]
    gated_keys = (featured[:, 1] * featured[:, 2]).astype(jnp.bfloat16)
    signal = gated_keys.astype(jnp.float32)
    response = ordered(long_filter).reshape((SEQ, D)).astype(jnp.float32)
    product = jnp.fft.rfft(signal, n=2 * SEQ, axis=0) * jnp.fft.rfft(response, n=2 * SEQ, axis=0)
    convolved = jnp.fft.irfft(product, n=2 * SEQ, axis=0)[:SEQ]
    activated = (queries * (convolved + skip_gain.astype(jnp.float32) * signal)).astype(jnp.bfloat16)
    mixed = jnp.dot(activated, out_weight, preferred_element_type=jnp.float32).astype(jnp.bfloat16)
    blocks = mixed.reshape((2 * PAIRS, BLOCK, D))
    return jnp.stack([blocks[:PAIRS], jnp.flip(blocks[PAIRS:], axis=0)], axis=0)
```

```python
import math

import jax
import jax.numpy as jnp
import ml_dtypes
import numpy as np
from jax import lax
from jax.experimental import pallas as pl
from jax.experimental.pallas import tpu as pltpu
from jax.sharding import PartitionSpec as P

F32 = jnp.float32
BF16 = jnp.bfloat16
MESH = pl.DeviceIdType.MESH
RIM = 16
LANES = 128
PAIRS = 4


def halves(values):
    high = values.astype(ml_dtypes.bfloat16)
    low = (values - high.astype(np.float64)).astype(ml_dtypes.bfloat16)
    return np.stack([high, low])


def odd_tables(length):
    k = np.arange(length)[:, None]
    t = np.arange(length)[None, :]
    angles = ((2 * k + 1) * t % (4 * length)) * (np.pi / (2 * length))
    forward = np.concatenate([np.cos(angles), -np.sin(angles)], axis=0)
    return halves(forward), halves(forward.T / length)


def dot(a, b):
    return jnp.dot(a, b, preferred_element_type=F32)


def kernel(
    x_ref,
    taps_ref,
    filter_ref,
    skip_ref,
    weight_hbm,
    forward_hbm,
    inverse_hbm,
    out_ref,
    weight,
    forward,
    inverse,
    halo,
    wide,
    gated,
    queries,
    moved,
    convolved,
    back,
    filter_spec,
    key_spec,
    own,
    act,
    pair_out,
    pair_in,
    first_out,
    first_in,
    second_out,
    second_in,
    local_sem,
    halo_send,
    halo_recv,
    move_send,
    move_recv,
    pair_send,
    pair_recv,
    first_send,
    first_recv,
    second_send,
    second_recv,
):
    rows, channels = gated.shape[1:]
    taps = taps_ref.shape[0]
    middle = forward.shape[2]
    z = lax.axis_index("ctx")
    ch = lax.axis_index("ch")
    core, x, y = ch % 2, ch // 2 % 2, ch // 4

    def ch_of(yy, xx, cc):
        return yy * 4 + xx * 2 + cc

    partner = (z, ch_of(y, x, 1 - core))
    beside_x = (z, ch_of(y, 1 - x, core))
    beside_y = (z, ch_of(1 - y, x, core))

    loads = [
        pltpu.make_async_copy(forward_hbm, forward, local_sem.at[0]),
        pltpu.make_async_copy(inverse_hbm, inverse, local_sem.at[1]),
        pltpu.make_async_copy(weight_hbm, weight, local_sem.at[2]),
    ]
    for load in loads:
        load.start()

    barrier = pltpu.get_barrier_semaphore()
    peers = [((z + o) % PAIRS, ch) for o in range(1, PAIRS)] + [partner, beside_x, beside_y]
    for peer in peers:
        pl.semaphore_signal(barrier, inc=1, device_id=peer, device_id_type=MESH)
    pl.semaphore_wait(barrier, len(peers))

    pending = []

    def remote(src, dst, send, recv, device):
        return pltpu.make_async_remote_copy(
            src_ref=src, dst_ref=dst, send_sem=send, recv_sem=recv, device_id=device, device_id_type=MESH
        )

    last = pl.ds(rows - RIM, RIM)
    up = remote(x_ref.at[0, :, last], halo.at[0], halo_send.at[0], halo_recv.at[0], ((z + 1) % PAIRS, ch))
    down = remote(x_ref.at[1, :, last], halo.at[1], halo_send.at[1], halo_recv.at[1], ((z + 3) % PAIRS, ch))

    @pl.when(z < PAIRS - 1)
    def _():
        up.start()

    @pl.when(z > 0)
    def _():
        down.start()

    def place(h, owner):
        block = owner if h == 0 else PAIRS - 1 - owner
        return (
            pl.ds(pl.multiple_of(block % 2 * rows, rows), rows),
            pl.ds(pl.multiple_of(block // 2 * LANES, LANES), LANES),
        )

    def lane_slice(owner):
        return pl.ds(pl.multiple_of(owner * LANES, LANES), LANES)

    def scatter(kind, source, h):
        mine_rows, mine_lanes = place(h, z)
        copies = []
        for o in (2, 1, 3):
            target = (z + o) % PAIRS
            copy = remote(
                source.at[h, :, lane_slice(target)],
                moved.at[kind, h, mine_rows, mine_lanes],
                move_send.at[kind, h, o - 1],
                move_recv.at[kind, h, o - 1],
                (target, ch),
            )
            copy.start()
            copies.append(copy)
        moved[kind, h, mine_rows, mine_lanes] = source[h, :, lane_slice(z)]
        pending.extend(copies)
        return copies

    def widen(h):
        for s in range(3):
            wide[h, s, RIM:] = x_ref[h, s].astype(F32)

    def taps_of(h, s, cols):
        total = None
        for i in range(taps):
            tap = taps_ref[i].astype(F32)[s : s + 1, cols]
            term = tap * wide[h, s, pl.ds(RIM - i, rows), cols]
            total = term if total is None else total + term
        return total

    columns = [slice(a, a + LANES) for a in range(0, channels, LANES)]

    def make_keys(h):
        for cols in columns:
            gated[h, :, cols] = (taps_of(h, 1, cols) * taps_of(h, 2, cols)).astype(BF16)

    def make_queries(h):
        for cols in columns:
            queries[h, :, cols] = taps_of(h, 0, cols)

    filter_copies, key_copies = [None, None], [None, None]
    filter_copies[0] = scatter(0, filter_ref, 0)
    widen(0)
    widen(1)

    @pl.when(z > 0)
    def _():
        up.wait_recv()

    @pl.when(z == 0)
    def _():
        halo[0] = jnp.zeros(halo.shape[1:], BF16)

    for s in range(3):
        wide[0, s, :RIM] = halo[0, s].astype(F32)
    make_keys(0)
    key_copies[0] = scatter(1, gated, 0)
    filter_copies[1] = scatter(0, filter_ref, 1)

    @pl.when(z < PAIRS - 1)
    def _():
        down.wait_recv()

    @pl.when(z == PAIRS - 1)
    def _():
        halo[1] = x_ref[0, :, rows - RIM :]

    for s in range(3):
        wide[1, s, :RIM] = halo[1, s].astype(F32)
    make_keys(1)
    key_copies[1] = scatter(1, gated, 1)
    loads[0].wait()

    signs = (1 - 2 * (lax.broadcasted_iota(jnp.int32, (middle, LANES), 0) % 2)).astype(F32)

    def spectrum(kind, h):
        data = moved[kind, h]
        return dot(forward[0], data) + dot(forward[1], data)

    def filter_spectra(h):
        for copy in filter_copies[h]:
            copy.wait_recv()
        both = spectrum(0, h)
        for m in range(2):
            filter_spec[0, 2 * h + m] = both[:, m * LANES : (m + 1) * LANES]
        for b in (2 * h, 2 * h + 1):
            if b == 0:
                filter_spec[1, 0] = filter_spec[0, 0]
            else:
                filter_spec[1, b, :middle] = filter_spec[0, b, :middle] - signs * filter_spec[0, b - 1, middle:]
                filter_spec[1, b, middle:] = filter_spec[0, b, middle:] + signs * filter_spec[0, b - 1, :middle]

    def key_spectra(h):
        for copy in key_copies[h]:
            copy.wait_recv()
        both = spectrum(1, h)
        for m in range(2):
            key_spec[2 * h + m] = both[:, m * LANES : (m + 1) * LANES]

    def products(i):
        real, imag = None, None
        for j in range(i + 1):
            ra, ia = filter_spec[1, i - j, :middle], filter_spec[1, i - j, middle:]
            rb, ib = key_spec[j, :middle], key_spec[j, middle:]
            re, im = ra * rb - ia * ib, ra * ib + ia * rb
            real = re if real is None else real + re
            imag = im if imag is None else imag + im
        return jnp.concatenate([real, imag], axis=0)

    back_copies = [None, None]

    def convolve(h):
        both = jnp.concatenate([products(2 * h), products(2 * h + 1)], axis=1)
        high = both.astype(BF16)
        low = (both - high.astype(F32)).astype(BF16)
        result = dot(inverse[0], high) + dot(inverse[0], low) + dot(inverse[1], high)
        convolved[h] = result.astype(BF16)
        copies = []
        for o in (2, 1, 3):
            target = (z + o) % PAIRS
            its_rows, its_lanes = place(h, target)
            copy = remote(
                convolved.at[h, its_rows, its_lanes],
                back.at[h, :, lane_slice(z)],
                move_send.at[2, h, o - 1],
                move_recv.at[2, h, o - 1],
                (target, ch),
            )
            copy.start()
            copies.append(copy)
        mine_rows, mine_lanes = place(h, z)
        back[h, :, lane_slice(z)] = convolved[h, mine_rows, mine_lanes]
        pending.extend(copies)
        back_copies[h] = copies

    filter_spectra(0)
    key_spectra(0)
    loads[1].wait()
    convolve(0)
    make_queries(0)
    filter_spectra(1)
    key_spectra(1)
    convolve(1)
    make_queries(1)
    loads[2].wait()

    steps = [(1, 1), (0, 1), (1, 0), (0, 0)]
    pair_copies = {}
    half = rows // 2
    parts = (slice(0, half), slice(half, rows))

    def weights_for(step, cc):
        yy = 1 - y if step[0] else y
        xx = 1 - x if step[1] else x
        return weight[:, pl.ds(pl.multiple_of(ch_of(yy, xx, cc) * channels, channels), channels)]

    def project(h):
        for copy in back_copies[h]:
            copy.wait_recv()
        for cols in columns:
            summed = back[h, :, cols].astype(F32) + skip_ref[:, cols] * gated[h, :, cols].astype(F32)
            act[h, :, cols] = (queries[h, :, cols] * summed).astype(BF16)
        rows_in = act[h]
        for t, step in enumerate(steps):
            pair_out[h, t] = dot(rows_in, weights_for(step, 1 - core)).astype(BF16)
            copy = remote(pair_out.at[h, t], pair_in.at[h, t], pair_send.at[h, t], pair_recv.at[h, t], partner)
            copy.start()
            pair_copies[h, t] = copy
            pending.append(copy)
        for t, step in enumerate(steps):
            own[h, t] = dot(rows_in, weights_for(step, core))

    first_copies, second_copies = {}, {}

    def pair_sum(h, t, part):
        return own[h, t, part] + pair_in[h, t, part].astype(F32)

    def first(h):
        for t, way, slot in ((0, 0, 0), (0, 1, 0), (1, 0, 1), (2, 1, 1)):
            if way == 0:
                pair_copies[h, t].wait_recv()
            elif t == 2:
                pair_copies[h, t].wait_recv()
            first_out[h, way, slot] = pair_sum(h, t, parts[way]).astype(BF16)
            copy = remote(
                first_out.at[h, way, slot],
                first_in.at[h, way, slot],
                first_send.at[h, way, slot],
                first_recv.at[h, way, slot],
                beside_y if way else beside_x,
            )
            copy.start()
            first_copies[h, way, slot] = copy
            pending.append(copy)

    def second(h):
        for way in range(2):
            first_copies[h, way, 0].wait_recv()
            t = 1 if way else 2
            total = pair_sum(h, t, parts[way]) + first_in[h, way, 0].astype(F32)
            second_out[h, way] = total.astype(BF16)
            copy = remote(
                second_out.at[h, way],
                second_in.at[h, way],
                second_send.at[h, way],
                second_recv.at[h, way],
                beside_x if way else beside_y,
            )
            copy.start()
            second_copies[h, way] = copy
            pending.append(copy)

    def finish(h):
        pair_copies[h, 3].wait_recv()
        for way in range(2):
            first_copies[h, way, 1].wait_recv()
            total = pair_sum(h, 3, parts[way]) + first_in[h, way, 1].astype(F32)
            second_copies[h, way].wait_recv()
            out_ref[h, parts[way]] = (total + second_in[h, way].astype(F32)).astype(BF16)

    project(0)
    first(0)
    project(1)
    second(0)
    first(1)
    finish(0)
    second(1)
    finish(1)

    @pl.when(z < PAIRS - 1)
    def _():
        up.wait_send()

    @pl.when(z > 0)
    def _():
        down.wait_send()

    for copy in pending:
        copy.wait_send()


def fused(features, short_weight, long_filter, skip_gain, out_weight):
    rows, channels = long_filter.shape[2:]
    middle = 2 * rows
    streams = jnp.transpose(features[:, 0], (0, 2, 1, 3))
    forward, inverse = odd_tables(middle)
    in_vmem = pl.BlockSpec(memory_space=pltpu.VMEM)
    in_hbm = pl.BlockSpec(memory_space=pl.ANY)
    vmem = pltpu.VMEM
    dma = pltpu.SemaphoreType.DMA
    out = pl.pallas_call(
        kernel,
        out_shape=jax.ShapeDtypeStruct((2, rows, channels), BF16),
        in_specs=[in_vmem] * 4 + [in_hbm] * 3,
        out_specs=in_vmem,
        scratch_shapes=[
            vmem(out_weight.shape, BF16),
            vmem(forward.shape, BF16),
            vmem(inverse.shape, BF16),
            vmem((2, 3, RIM, channels), BF16),
            vmem((2, 3, RIM + rows, channels), F32),
            vmem((2, rows, channels), BF16),
            vmem((2, rows, channels), F32),
            vmem((2, 2, middle, 2 * LANES), BF16),
            vmem((2, middle, 2 * LANES), BF16),
            vmem((2, rows, channels), BF16),
            vmem((2, 4, 2 * middle, LANES), F32),
            vmem((4, 2 * middle, LANES), F32),
            vmem((2, 4, rows, channels), F32),
            vmem((2, rows, channels), BF16),
            vmem((2, 4, rows, channels), BF16),
            vmem((2, 4, rows, channels), BF16),
            vmem((2, 2, 2, rows // 2, channels), BF16),
            vmem((2, 2, 2, rows // 2, channels), BF16),
            vmem((2, 2, rows // 2, channels), BF16),
            vmem((2, 2, rows // 2, channels), BF16),
            dma((3,)),
            dma((2,)),
            dma((2,)),
            dma((3, 2, 3)),
            dma((3, 2, 3)),
            dma((2, 4)),
            dma((2, 4)),
            dma((2, 2, 2)),
            dma((2, 2, 2)),
            dma((2, 2)),
            dma((2, 2)),
        ],
        compiler_params=pltpu.CompilerParams(
            collective_id=0, has_side_effects=True, vmem_limit_bytes=48 * 1024 * 1024
        ),
        name="hyena",
    )(
        streams,
        short_weight,
        long_filter[:, 0],
        skip_gain.reshape(1, channels),
        out_weight,
        jnp.asarray(forward),
        jnp.asarray(inverse),
    )
    return out[:, None]


def from_behind(value, axis, steps):
    count = lax.axis_size(axis)
    initial, last = (max(0, -steps), min(count, count - steps))
    return lax.ppermute(value, axis, [(source, source + steps) for source in range(initial, last)])


def transform_tables(length):
    period = 2 * length
    indices = jnp.arange(period, dtype=jnp.int32)
    phases = indices[:, None] * indices[None, :] % period
    angles = phases.astype(jnp.float32) * (2.0 * math.pi / period)
    cosine = jnp.cos(angles)
    sine_table = jnp.sin(angles)
    forward_full = jnp.concatenate([cosine, -sine_table], axis=0)
    forward_data = forward_full[:, :length]
    inverse = jnp.concatenate([cosine[:length], -sine_table[:length]], axis=1) / period
    return (forward_full, forward_data, inverse)


def complex_product(first, second):
    middle = first.shape[-2] // 2
    real_a = first[..., :middle, :]
    imag_a = first[..., middle:, :]
    real_b = second[..., :middle, :]
    imag_b = second[..., middle:, :]
    return jnp.concatenate(
        [real_a * real_b - imag_a * imag_b, real_a * imag_b + imag_a * real_b], axis=-2
    )


def featurize(tokens, before, kernel):
    extended = jnp.concatenate([before, tokens], axis=0).astype(jnp.float32)
    length = tokens.shape[0]
    margin_rows = kernel.shape[0] - 1
    summed = jnp.zeros(tokens.shape, jnp.float32)
    for offset in range(kernel.shape[0]):
        summed = (
            summed
            + kernel[offset].astype(jnp.float32)
            * extended[margin_rows - offset : margin_rows - offset + length]
        )
    return summed


def ordered(blocks):
    return jnp.concatenate([blocks[0], jnp.flip(blocks[1], axis=0)], axis=0)


def local(features, short_weight, long_filter, skip_gain, out_weight):
    pair_count = lax.axis_size("ctx")
    blocks_all = 2 * pair_count
    position = lax.axis_index("ctx")
    length = features.shape[2]
    margin_rows = short_weight.shape[0] - 1
    trailing = features[:, 0, length - margin_rows :]
    from_before = from_behind(trailing[0], "ctx", 1)
    from_after = from_behind(trailing[1], "ctx", -1)
    second_rim = jnp.where(position == pair_count - 1, trailing[0], from_after)
    first_feat = featurize(features[0, 0], from_before, short_weight)
    second_feat = featurize(features[1, 0], second_rim, short_weight)
    featured = jnp.stack([first_feat, second_feat], axis=0)
    queries = featured[:, :, 0]
    gated_keys = (featured[:, :, 1] * featured[:, :, 2]).astype(jnp.bfloat16)
    forward_full, forward_data, inverse = transform_tables(length)
    precise = lax.Precision.HIGHEST
    moved_gated, moved_filter = (
        lax.all_to_all(gated_keys[:, None], "ctx", split_axis=3, concat_axis=1, tiled=True),
        lax.all_to_all(long_filter, "ctx", split_axis=3, concat_axis=1, tiled=True),
    )
    ordered_gated = ordered(moved_gated).astype(jnp.float32)
    lag_order = ordered(moved_filter)
    padded = jnp.concatenate(
        [jnp.zeros((1,) + lag_order.shape[1:], lag_order.dtype), lag_order], axis=0
    )
    segments = jnp.concatenate([padded[1:], padded[:-1]], axis=1).astype(jnp.float32)
    responses = jnp.einsum("fm,kmc->kfc", forward_full, segments, precision=precise)
    spectra = jnp.einsum("fn,knc->kfc", forward_data, ordered_gated, precision=precise)
    sources = jnp.arange(blocks_all, dtype=jnp.int32)

    def one_target(target):
        distance = target - sources
        picked = jnp.take(responses, jnp.maximum(distance, 0), axis=0)
        products = complex_product(picked, spectra)
        summed = jnp.sum(jnp.where((distance >= 0)[:, None, None], products, 0.0), axis=0)
        return jnp.dot(inverse, summed, precision=precise)

    group_size = math.gcd(blocks_all, 8)
    grouped = sources.reshape(blocks_all // group_size, group_size)
    outputs = lax.map(jax.vmap(one_target), grouped).reshape(
        (blocks_all, length, responses.shape[-1])
    )
    blocks = jnp.stack([outputs[:pair_count], jnp.flip(outputs[pair_count:], axis=0)], axis=0)
    returned = lax.all_to_all(blocks, "ctx", split_axis=1, concat_axis=3, tiled=True)
    convolved = returned[:, 0]
    activated = (queries * (convolved + skip_gain * gated_keys.astype(jnp.float32))).astype(
        jnp.bfloat16
    )
    token_rows = activated.reshape(2 * length, activated.shape[-1])
    channels = token_rows.shape[1]
    owned = lax.psum_scatter(
        lax.dot_general(
            out_weight, token_rows, (((0,), (1,)), ((), ())), preferred_element_type=jnp.float32
        ).astype(jnp.bfloat16),
        "ch",
        scatter_dimension=0,
        tiled=True,
    ).astype(jnp.float32)
    result = owned.T
    return result.astype(jnp.bfloat16).reshape(2, 1, length, channels)


def solution(mesh):
    in_specs = (
        P(None, "ctx", None, None, "ch"),
        P(None, None, "ch"),
        P(None, "ctx", None, "ch"),
        P("ch"),
        P("ch", None),
    )
    out_specs = P(None, "ctx", None, "ch")
    shape = dict(mesh.shape)
    suits = shape == {"ctx": PAIRS, "ch": 8}
    body = fused if suits else local
    return jax.shard_map(body, mesh=mesh, in_specs=in_specs, out_specs=out_specs, check_vma=False)
```

```python
import math

import jax
import jax.numpy as jnp
import ml_dtypes
import numpy as np
from jax import lax
from jax.experimental import pallas as pl
from jax.experimental.pallas import tpu as pltpu
from jax.sharding import PartitionSpec as P

F32 = jnp.float32
BF16 = jnp.bfloat16
MESH = pl.DeviceIdType.MESH
RIM = 16
LANES = 128
PAIRS = 4


def halves(values):
    high = values.astype(ml_dtypes.bfloat16)
    low = (values - high.astype(np.float64)).astype(ml_dtypes.bfloat16)
    return np.stack([high, low])


def odd_tables(length):
    k = np.arange(length)[:, None]
    t = np.arange(length)[None, :]
    angles = ((2 * k + 1) * t % (4 * length)) * (np.pi / (2 * length))
    forward = np.concatenate([np.cos(angles), -np.sin(angles)], axis=0)
    return halves(forward), halves(forward.T / length)


def dot(a, b):
    return jnp.dot(a, b, preferred_element_type=F32)


def kernel(
    x_hbm,
    taps_hbm,
    filter_hbm,
    skip_hbm,
    weight_hbm,
    forward_hbm,
    inverse_hbm,
    out_ref,
    x_ref,
    taps_ref,
    filter_ref,
    skip_ref,
    weight,
    forward,
    inverse,
    halo,
    wide,
    gated,
    queries,
    moved,
    convolved,
    back,
    filter_spec,
    key_spec,
    own,
    act,
    pair_out,
    pair_in,
    first_out,
    first_in,
    second_out,
    second_in,
    local_sem,
    halo_send,
    halo_recv,
    move_send,
    move_recv,
    pair_send,
    pair_recv,
    first_send,
    first_recv,
    second_send,
    second_recv,
):
    rows, channels = gated.shape[1:]
    taps = taps_ref.shape[1]
    middle = forward.shape[2]
    z = lax.axis_index("ctx")
    ch = lax.axis_index("ch")
    core, x, y = ch % 2, ch // 2 % 2, ch // 4

    def ch_of(yy, xx, cc):
        return yy * 4 + xx * 2 + cc

    partner = (z, ch_of(y, x, 1 - core))
    beside_x = (z, ch_of(y, 1 - x, core))
    beside_y = (z, ch_of(1 - y, x, core))

    sources = (x_hbm, filter_hbm, taps_hbm, skip_hbm, forward_hbm, inverse_hbm, weight_hbm)
    places = (x_ref, filter_ref, taps_ref, skip_ref, forward, inverse, weight)
    loads = [
        pltpu.make_async_copy(source, target, local_sem.at[i])
        for i, (source, target) in enumerate(zip(sources, places))
    ]
    for load in loads[:4]:
        load.start()

    barrier = pltpu.get_barrier_semaphore()
    peers = [((z + o) % PAIRS, ch) for o in range(1, PAIRS)] + [partner, beside_x, beside_y]
    for peer in peers:
        pl.semaphore_signal(barrier, inc=1, device_id=peer, device_id_type=MESH)
    pl.semaphore_wait(barrier, len(peers))

    for load in loads[4:]:
        load.start()
    for load in loads[:4]:
        load.wait()
    pending = []

    def remote(src, dst, send, recv, device):
        return pltpu.make_async_remote_copy(
            src_ref=src, dst_ref=dst, send_sem=send, recv_sem=recv, device_id=device, device_id_type=MESH
        )

    last = pl.ds(rows - RIM, RIM)
    up = remote(x_ref.at[0, :, last], halo.at[0], halo_send.at[0], halo_recv.at[0], ((z + 1) % PAIRS, ch))
    down = remote(x_ref.at[1, :, last], halo.at[1], halo_send.at[1], halo_recv.at[1], ((z + 3) % PAIRS, ch))

    @pl.when(z < PAIRS - 1)
    def _():
        up.start()

    @pl.when(z > 0)
    def _():
        down.start()

    def place(h, owner):
        block = owner if h == 0 else PAIRS - 1 - owner
        return (
            pl.ds(pl.multiple_of(block % 2 * rows, rows), rows),
            pl.ds(pl.multiple_of(block // 2 * LANES, LANES), LANES),
        )

    def lane_slice(owner):
        return pl.ds(pl.multiple_of(owner * LANES, LANES), LANES)

    def scatter(kind, source, h):
        mine_rows, mine_lanes = place(h, z)
        copies = []
        for o in (2, 1, 3):
            target = (z + o) % PAIRS
            copy = remote(
                source.at[h, :, lane_slice(target)],
                moved.at[kind, h, mine_rows, mine_lanes],
                move_send.at[kind, h, o - 1],
                move_recv.at[kind, h, o - 1],
                (target, ch),
            )
            copy.start()
            copies.append(copy)
        moved[kind, h, mine_rows, mine_lanes] = source[h, :, lane_slice(z)]
        pending.extend(copies)
        return copies

    def widen(h):
        for s in range(3):
            wide[h, s, RIM:] = x_ref[h, s].astype(F32)

    def taps_of(h, s, cols):
        total = None
        for i in range(taps):
            tap = taps_ref[s].astype(F32)[i : i + 1, cols]
            term = tap * wide[h, s, pl.ds(RIM - i, rows), cols]
            total = term if total is None else total + term
        return total

    columns = [slice(a, a + LANES) for a in range(0, channels, LANES)]

    def make_keys(h):
        for cols in columns:
            gated[h, :, cols] = (taps_of(h, 1, cols) * taps_of(h, 2, cols)).astype(BF16)

    def make_queries(h):
        for cols in columns:
            queries[h, :, cols] = taps_of(h, 0, cols)

    filter_copies, key_copies = [None, None], [None, None]
    filter_copies[0] = scatter(0, filter_ref, 0)
    widen(0)
    widen(1)

    @pl.when(z > 0)
    def _():
        up.wait_recv()

    @pl.when(z == 0)
    def _():
        halo[0] = jnp.zeros(halo.shape[1:], BF16)

    for s in range(3):
        wide[0, s, :RIM] = halo[0, s].astype(F32)
    make_keys(0)
    key_copies[0] = scatter(1, gated, 0)
    filter_copies[1] = scatter(0, filter_ref, 1)

    @pl.when(z < PAIRS - 1)
    def _():
        down.wait_recv()

    @pl.when(z == PAIRS - 1)
    def _():
        halo[1] = x_ref[0, :, rows - RIM :]

    for s in range(3):
        wide[1, s, :RIM] = halo[1, s].astype(F32)
    make_keys(1)
    key_copies[1] = scatter(1, gated, 1)
    loads[4].wait()

    signs = (1 - 2 * (lax.broadcasted_iota(jnp.int32, (middle, LANES), 0) % 2)).astype(F32)

    def spectrum(kind, h):
        data = moved[kind, h]
        return dot(forward[0], data) + dot(forward[1], data)

    def filter_spectra(h):
        for copy in filter_copies[h]:
            copy.wait_recv()
        both = spectrum(0, h)
        for m in range(2):
            filter_spec[0, 2 * h + m] = both[:, m * LANES : (m + 1) * LANES]
        for b in (2 * h, 2 * h + 1):
            if b == 0:
                filter_spec[1, 0] = filter_spec[0, 0]
            else:
                filter_spec[1, b, :middle] = filter_spec[0, b, :middle] - signs * filter_spec[0, b - 1, middle:]
                filter_spec[1, b, middle:] = filter_spec[0, b, middle:] + signs * filter_spec[0, b - 1, :middle]

    def key_spectra(h):
        for copy in key_copies[h]:
            copy.wait_recv()
        both = spectrum(1, h)
        for m in range(2):
            key_spec[2 * h + m] = both[:, m * LANES : (m + 1) * LANES]

    def products(i):
        real, imag = None, None
        for j in range(i + 1):
            ra, ia = filter_spec[1, i - j, :middle], filter_spec[1, i - j, middle:]
            rb, ib = key_spec[j, :middle], key_spec[j, middle:]
            re, im = ra * rb - ia * ib, ra * ib + ia * rb
            real = re if real is None else real + re
            imag = im if imag is None else imag + im
        return jnp.concatenate([real, imag], axis=0)

    back_copies = [None, None]

    def convolve(h):
        both = jnp.concatenate([products(2 * h), products(2 * h + 1)], axis=1)
        high = both.astype(BF16)
        low = (both - high.astype(F32)).astype(BF16)
        result = dot(inverse[0], high) + dot(inverse[0], low) + dot(inverse[1], high)
        convolved[h] = result.astype(BF16)
        copies = []
        for o in (2, 1, 3):
            target = (z + o) % PAIRS
            its_rows, its_lanes = place(h, target)
            copy = remote(
                convolved.at[h, its_rows, its_lanes],
                back.at[h, :, lane_slice(z)],
                move_send.at[2, h, o - 1],
                move_recv.at[2, h, o - 1],
                (target, ch),
            )
            copy.start()
            copies.append(copy)
        mine_rows, mine_lanes = place(h, z)
        back[h, :, lane_slice(z)] = convolved[h, mine_rows, mine_lanes]
        pending.extend(copies)
        back_copies[h] = copies

    filter_spectra(0)
    key_spectra(0)
    loads[5].wait()
    convolve(0)
    make_queries(0)
    filter_spectra(1)
    key_spectra(1)
    convolve(1)
    make_queries(1)
    loads[6].wait()

    steps = [(1, 1), (0, 1), (1, 0), (0, 0)]
    pair_copies = {}
    half = rows // 2
    parts = (slice(0, half), slice(half, rows))

    def weights_for(step, cc):
        yy = 1 - y if step[0] else y
        xx = 1 - x if step[1] else x
        return weight[:, pl.ds(pl.multiple_of(ch_of(yy, xx, cc) * channels, channels), channels)]

    def project(h):
        for copy in back_copies[h]:
            copy.wait_recv()
        for cols in columns:
            summed = back[h, :, cols].astype(F32) + skip_ref[:, cols] * gated[h, :, cols].astype(F32)
            act[h, :, cols] = (queries[h, :, cols] * summed).astype(BF16)
        rows_in = act[h]
        for t, step in enumerate(steps):
            pair_out[h, t] = dot(rows_in, weights_for(step, 1 - core)).astype(BF16)
            copy = remote(pair_out.at[h, t], pair_in.at[h, t], pair_send.at[h, t], pair_recv.at[h, t], partner)
            copy.start()
            pair_copies[h, t] = copy
            pending.append(copy)
        for t, step in enumerate(steps):
            own[h, t] = dot(rows_in, weights_for(step, core))

    first_copies, second_copies = {}, {}

    def pair_sum(h, t, part):
        return own[h, t, part] + pair_in[h, t, part].astype(F32)

    def first(h):
        for t, way, slot in ((0, 0, 0), (0, 1, 0), (1, 0, 1), (2, 1, 1)):
            if way == 0:
                pair_copies[h, t].wait_recv()
            elif t == 2:
                pair_copies[h, t].wait_recv()
            first_out[h, way, slot] = pair_sum(h, t, parts[way]).astype(BF16)
            copy = remote(
                first_out.at[h, way, slot],
                first_in.at[h, way, slot],
                first_send.at[h, way, slot],
                first_recv.at[h, way, slot],
                beside_y if way else beside_x,
            )
            copy.start()
            first_copies[h, way, slot] = copy
            pending.append(copy)

    def second(h):
        for way in range(2):
            first_copies[h, way, 0].wait_recv()
            t = 1 if way else 2
            total = pair_sum(h, t, parts[way]) + first_in[h, way, 0].astype(F32)
            second_out[h, way] = total.astype(BF16)
            copy = remote(
                second_out.at[h, way],
                second_in.at[h, way],
                second_send.at[h, way],
                second_recv.at[h, way],
                beside_x if way else beside_y,
            )
            copy.start()
            second_copies[h, way] = copy
            pending.append(copy)

    def finish(h):
        pair_copies[h, 3].wait_recv()
        for way in range(2):
            first_copies[h, way, 1].wait_recv()
            total = pair_sum(h, 3, parts[way]) + first_in[h, way, 1].astype(F32)
            second_copies[h, way].wait_recv()
            out_ref[h, parts[way]] = (total + second_in[h, way].astype(F32)).astype(BF16)

    project(0)
    first(0)
    project(1)
    second(0)
    first(1)
    finish(0)
    second(1)
    finish(1)

    @pl.when(z < PAIRS - 1)
    def _():
        up.wait_send()

    @pl.when(z > 0)
    def _():
        down.wait_send()

    for copy in pending:
        copy.wait_send()


def fused(features, short_weight, long_filter, skip_gain, out_weight):
    rows, channels = long_filter.shape[2:]
    middle = 2 * rows
    streams = jnp.transpose(features[:, 0], (0, 2, 1, 3))
    taps = jnp.transpose(short_weight, (1, 0, 2))
    forward, inverse = odd_tables(middle)
    in_vmem = pl.BlockSpec(memory_space=pltpu.VMEM)
    in_hbm = pl.BlockSpec(memory_space=pl.ANY)
    vmem = pltpu.VMEM
    dma = pltpu.SemaphoreType.DMA
    out = pl.pallas_call(
        kernel,
        out_shape=jax.ShapeDtypeStruct((2, rows, channels), BF16),
        in_specs=[in_hbm] * 7,
        out_specs=in_vmem,
        scratch_shapes=[
            vmem(streams.shape, BF16),
            vmem(taps.shape, BF16),
            vmem((2, rows, channels), BF16),
            vmem((1, channels), F32),
            vmem(out_weight.shape, BF16),
            vmem(forward.shape, BF16),
            vmem(inverse.shape, BF16),
            vmem((2, 3, RIM, channels), BF16),
            vmem((2, 3, RIM + rows, channels), F32),
            vmem((2, rows, channels), BF16),
            vmem((2, rows, channels), F32),
            vmem((2, 2, middle, 2 * LANES), BF16),
            vmem((2, middle, 2 * LANES), BF16),
            vmem((2, rows, channels), BF16),
            vmem((2, 4, 2 * middle, LANES), F32),
            vmem((4, 2 * middle, LANES), F32),
            vmem((2, 4, rows, channels), F32),
            vmem((2, rows, channels), BF16),
            vmem((2, 4, rows, channels), BF16),
            vmem((2, 4, rows, channels), BF16),
            vmem((2, 2, 2, rows // 2, channels), BF16),
            vmem((2, 2, 2, rows // 2, channels), BF16),
            vmem((2, 2, rows // 2, channels), BF16),
            vmem((2, 2, rows // 2, channels), BF16),
            dma((7,)),
            dma((2,)),
            dma((2,)),
            dma((3, 2, 3)),
            dma((3, 2, 3)),
            dma((2, 4)),
            dma((2, 4)),
            dma((2, 2, 2)),
            dma((2, 2, 2)),
            dma((2, 2)),
            dma((2, 2)),
        ],
        compiler_params=pltpu.CompilerParams(
            collective_id=0, has_side_effects=True, vmem_limit_bytes=62 * 1024 * 1024
        ),
        name="hyena",
    )(
        streams,
        taps,
        long_filter[:, 0],
        skip_gain.reshape(1, channels),
        out_weight,
        jnp.asarray(forward),
        jnp.asarray(inverse),
    )
    return out[:, None]


def from_behind(value, axis, steps):
    count = lax.axis_size(axis)
    initial, last = (max(0, -steps), min(count, count - steps))
    return lax.ppermute(value, axis, [(source, source + steps) for source in range(initial, last)])


def transform_tables(length):
    period = 2 * length
    indices = jnp.arange(period, dtype=jnp.int32)
    phases = indices[:, None] * indices[None, :] % period
    angles = phases.astype(jnp.float32) * (2.0 * math.pi / period)
    cosine = jnp.cos(angles)
    sine_table = jnp.sin(angles)
    forward_full = jnp.concatenate([cosine, -sine_table], axis=0)
    forward_data = forward_full[:, :length]
    inverse = jnp.concatenate([cosine[:length], -sine_table[:length]], axis=1) / period
    return (forward_full, forward_data, inverse)


def complex_product(first, second):
    middle = first.shape[-2] // 2
    real_a = first[..., :middle, :]
    imag_a = first[..., middle:, :]
    real_b = second[..., :middle, :]
    imag_b = second[..., middle:, :]
    return jnp.concatenate(
        [real_a * real_b - imag_a * imag_b, real_a * imag_b + imag_a * real_b], axis=-2
    )


def featurize(tokens, before, kernel):
    extended = jnp.concatenate([before, tokens], axis=0).astype(jnp.float32)
    length = tokens.shape[0]
    margin_rows = kernel.shape[0] - 1
    summed = jnp.zeros(tokens.shape, jnp.float32)
    for offset in range(kernel.shape[0]):
        summed = (
            summed
            + kernel[offset].astype(jnp.float32)
            * extended[margin_rows - offset : margin_rows - offset + length]
        )
    return summed


def ordered(blocks):
    return jnp.concatenate([blocks[0], jnp.flip(blocks[1], axis=0)], axis=0)


def local(features, short_weight, long_filter, skip_gain, out_weight):
    pair_count = lax.axis_size("ctx")
    blocks_all = 2 * pair_count
    position = lax.axis_index("ctx")
    length = features.shape[2]
    margin_rows = short_weight.shape[0] - 1
    trailing = features[:, 0, length - margin_rows :]
    from_before = from_behind(trailing[0], "ctx", 1)
    from_after = from_behind(trailing[1], "ctx", -1)
    second_rim = jnp.where(position == pair_count - 1, trailing[0], from_after)
    first_feat = featurize(features[0, 0], from_before, short_weight)
    second_feat = featurize(features[1, 0], second_rim, short_weight)
    featured = jnp.stack([first_feat, second_feat], axis=0)
    queries = featured[:, :, 0]
    gated_keys = (featured[:, :, 1] * featured[:, :, 2]).astype(jnp.bfloat16)
    forward_full, forward_data, inverse = transform_tables(length)
    precise = lax.Precision.HIGHEST
    moved_gated, moved_filter = (
        lax.all_to_all(gated_keys[:, None], "ctx", split_axis=3, concat_axis=1, tiled=True),
        lax.all_to_all(long_filter, "ctx", split_axis=3, concat_axis=1, tiled=True),
    )
    ordered_gated = ordered(moved_gated).astype(jnp.float32)
    lag_order = ordered(moved_filter)
    padded = jnp.concatenate(
        [jnp.zeros((1,) + lag_order.shape[1:], lag_order.dtype), lag_order], axis=0
    )
    segments = jnp.concatenate([padded[1:], padded[:-1]], axis=1).astype(jnp.float32)
    responses = jnp.einsum("fm,kmc->kfc", forward_full, segments, precision=precise)
    spectra = jnp.einsum("fn,knc->kfc", forward_data, ordered_gated, precision=precise)
    sources = jnp.arange(blocks_all, dtype=jnp.int32)

    def one_target(target):
        distance = target - sources
        picked = jnp.take(responses, jnp.maximum(distance, 0), axis=0)
        products = complex_product(picked, spectra)
        summed = jnp.sum(jnp.where((distance >= 0)[:, None, None], products, 0.0), axis=0)
        return jnp.dot(inverse, summed, precision=precise)

    group_size = math.gcd(blocks_all, 8)
    grouped = sources.reshape(blocks_all // group_size, group_size)
    outputs = lax.map(jax.vmap(one_target), grouped).reshape(
        (blocks_all, length, responses.shape[-1])
    )
    blocks = jnp.stack([outputs[:pair_count], jnp.flip(outputs[pair_count:], axis=0)], axis=0)
    returned = lax.all_to_all(blocks, "ctx", split_axis=1, concat_axis=3, tiled=True)
    convolved = returned[:, 0]
    activated = (queries * (convolved + skip_gain * gated_keys.astype(jnp.float32))).astype(
        jnp.bfloat16
    )
    token_rows = activated.reshape(2 * length, activated.shape[-1])
    channels = token_rows.shape[1]
    owned = lax.psum_scatter(
        lax.dot_general(
            out_weight, token_rows, (((0,), (1,)), ((), ())), preferred_element_type=jnp.float32
        ).astype(jnp.bfloat16),
        "ch",
        scatter_dimension=0,
        tiled=True,
    ).astype(jnp.float32)
    result = owned.T
    return result.astype(jnp.bfloat16).reshape(2, 1, length, channels)


def solution(mesh):
    in_specs = (
        P(None, "ctx", None, None, "ch"),
        P(None, None, "ch"),
        P(None, "ctx", None, "ch"),
        P("ch"),
        P("ch", None),
    )
    out_specs = P(None, "ctx", None, "ch")
    shape = dict(mesh.shape)
    suits = shape == {"ctx": PAIRS, "ch": 8}
    body = fused if suits else local
    return jax.shard_map(body, mesh=mesh, in_specs=in_specs, out_specs=out_specs, check_vma=False)
```

```python
import math

import jax
import jax.numpy as jnp
import ml_dtypes
import numpy as np
from jax import lax
from jax.experimental import pallas as pl
from jax.experimental.pallas import tpu as pltpu
from jax.sharding import PartitionSpec as P

F32 = jnp.float32
BF16 = jnp.bfloat16
MESH = pl.DeviceIdType.MESH
RIM = 8
STRIP = 64
LANES = 128
PAIRS = 4


def halves(values):
    high = values.astype(ml_dtypes.bfloat16)
    low = (values - high.astype(np.float64)).astype(ml_dtypes.bfloat16)
    return np.stack([high, low])


def odd_tables(length):
    k = np.arange(length)[:, None]
    t = np.arange(length)[None, :]
    angles = ((2 * k + 1) * t % (4 * length)) * (np.pi / (2 * length))
    forward = np.concatenate([np.cos(angles), -np.sin(angles)], axis=0)
    return halves(forward), halves(forward.T / length)


def dot(a, b):
    return jnp.dot(a, b, preferred_element_type=F32)


def kernel(
    x_hbm,
    taps_hbm,
    filter_hbm,
    skip_hbm,
    weight_hbm,
    forward_hbm,
    inverse_hbm,
    out_ref,
    x_ref,
    taps_ref,
    filter_ref,
    skip_ref,
    weight,
    forward,
    inverse,
    rim_out,
    halo,
    wide,
    gated,
    queries,
    moved,
    convolved,
    back,
    filter_spec,
    key_spec,
    summed_spec,
    own,
    act,
    pair_out,
    pair_in,
    first_out,
    first_in,
    second_out,
    second_in,
    local_sem,
    halo_send,
    halo_recv,
    move_send,
    move_recv,
    back_send,
    back_recv,
    pair_send,
    pair_recv,
    first_send,
    first_recv,
    second_send,
    second_recv,
):
    rows, channels = gated.shape[1:]
    taps = taps_ref.shape[1]
    middle = forward.shape[2]
    z = lax.axis_index("ctx")
    ch = lax.axis_index("ch")
    core, x, y = ch % 2, ch // 2 % 2, ch // 4

    def ch_of(yy, xx, cc):
        return yy * 4 + xx * 2 + cc

    partner = (z, ch_of(y, x, 1 - core))
    beside_x = (z, ch_of(y, 1 - x, core))
    beside_y = (z, ch_of(1 - y, x, core))

    sources = (x_hbm, filter_hbm, taps_hbm, skip_hbm, forward_hbm, inverse_hbm, weight_hbm)
    places = (x_ref, filter_ref, taps_ref, skip_ref, forward, inverse, weight)
    loads = [
        pltpu.make_async_copy(source, target, local_sem.at[i])
        for i, (source, target) in enumerate(zip(sources, places))
    ]
    for load in loads[:4]:
        load.start()

    barrier = pltpu.get_barrier_semaphore()
    peers = [((z + o) % PAIRS, ch) for o in range(1, PAIRS)] + [partner, beside_x, beside_y]
    for peer in peers:
        pl.semaphore_signal(barrier, inc=1, device_id=peer, device_id_type=MESH)
    pl.semaphore_wait(barrier, len(peers))

    for load in loads[4:]:
        load.start()
    for load in loads[:4]:
        load.wait()
    pending = []

    def remote(src, dst, send, recv, device):
        return pltpu.make_async_remote_copy(
            src_ref=src, dst_ref=dst, send_sem=send, recv_sem=recv, device_id=device, device_id_type=MESH
        )

    def widen(h):
        for s in range(3):
            wide[h, s, RIM:] = x_ref[h, s].astype(F32)

    widen(0)
    widen(1)
    tail = slice(rows, rows + RIM)
    rims = {}
    for kind, streams in ((0, (1, 2)), (1, (0, 0))):
        for h in range(2):
            rim_out[kind, h] = jnp.concatenate([wide[h, s, tail] for s in streams], axis=0).astype(BF16)
            rims[kind, h] = remote(
                rim_out.at[kind, h],
                halo.at[kind, h],
                halo_send.at[kind, h],
                halo_recv.at[kind, h],
                ((z + (1 if h == 0 else 3)) % PAIRS, ch),
            )

    def send_rims(kind):
        @pl.when(z < PAIRS - 1)
        def _():
            rims[kind, 0].start()

        @pl.when(z > 0)
        def _():
            rims[kind, 1].start()

    def take_rim(kind, h):
        has = z > 0 if h == 0 else z < PAIRS - 1

        @pl.when(has)
        def _():
            rims[kind, h].wait_recv()

        @pl.when(jnp.logical_not(has))
        def _():
            halo[kind, h] = jnp.zeros(halo.shape[2:], BF16) if h == 0 else rim_out[kind, 0]

        both = halo[kind, h].astype(F32)
        for m, s in enumerate((1, 2) if kind == 0 else (0,)):
            wide[h, s, :RIM] = both[m * RIM : (m + 1) * RIM]

    send_rims(0)

    def place(h, owner, first_row=0, count=None):
        block = owner if h == 0 else PAIRS - 1 - owner
        count = rows if count is None else count
        return (
            pl.ds(pl.multiple_of(block % 2 * rows + first_row, count), count),
            pl.ds(pl.multiple_of(block // 2 * LANES, LANES), LANES),
        )

    def lane_slice(owner):
        return pl.ds(pl.multiple_of(owner * LANES, LANES), LANES)

    def scatter(kind, source, h):
        mine_rows, mine_lanes = place(h, z)
        copies = []
        for o in (2, 1, 3):
            target = (z + o) % PAIRS
            copy = remote(
                source.at[h, :, lane_slice(target)],
                moved.at[kind, h, mine_rows, mine_lanes],
                move_send.at[kind, h, o - 1],
                move_recv.at[kind, h, o - 1],
                (target, ch),
            )
            copy.start()
            copies.append(copy)
        moved[kind, h, mine_rows, mine_lanes] = source[h, :, lane_slice(z)]
        pending.extend(copies)
        return copies

    tap_rows = [taps_ref[s].astype(F32) for s in range(3)]

    def taps_of(h, s, cols):
        total = None
        for i in range(taps):
            tap = tap_rows[s][i : i + 1, cols]
            term = tap * wide[h, s, pl.ds(RIM - i, rows), cols]
            total = term if total is None else total + term
        return total

    columns = [slice(a, a + LANES) for a in range(0, channels, LANES)]

    def make_keys(h):
        for cols in columns:
            gated[h, :, cols] = (taps_of(h, 1, cols) * taps_of(h, 2, cols)).astype(BF16)

    def make_queries(h):
        for cols in columns:
            queries[h, :, cols] = taps_of(h, 0, cols)

    filter_copies, key_copies = [None, None], [None, None]
    filter_copies[0] = scatter(0, filter_ref, 0)
    take_rim(0, 0)
    make_keys(0)
    key_copies[0] = scatter(1, gated, 0)
    send_rims(1)
    filter_copies[1] = scatter(0, filter_ref, 1)
    take_rim(0, 1)
    make_keys(1)
    loads[4].wait()

    signs = (1 - 2 * (lax.broadcasted_iota(jnp.int32, (middle, LANES), 0) % 2)).astype(F32)

    def spectrum(kind, h):
        data = moved[kind, h]
        return dot(forward[0], data) + dot(forward[1], data)

    def filter_spectra(h):
        for copy in filter_copies[h]:
            copy.wait_recv()
        both = spectrum(0, h)
        for m in range(2):
            filter_spec[0, 2 * h + m] = both[:, m * LANES : (m + 1) * LANES]
        for b in (2 * h, 2 * h + 1):
            if b == 0:
                filter_spec[1, 0] = filter_spec[0, 0]
            else:
                filter_spec[1, b, :middle] = filter_spec[0, b, :middle] - signs * filter_spec[0, b - 1, middle:]
                filter_spec[1, b, middle:] = filter_spec[0, b, middle:] + signs * filter_spec[0, b - 1, :middle]

    def key_spectra(h):
        for copy in key_copies[h]:
            copy.wait_recv()
        both = spectrum(1, h)
        for m in range(2):
            key_spec[2 * h + m] = both[:, m * LANES : (m + 1) * LANES]

    def products(h):
        for m in range(2):
            i = 2 * h + m
            cols = slice(m * LANES, (m + 1) * LANES)
            for start in range(0, middle, STRIP):
                re_rows = slice(start, start + STRIP)
                im_rows = slice(middle + start, middle + start + STRIP)
                real, imag = None, None
                for j in range(i + 1):
                    ra, ia = filter_spec[1, i - j, re_rows], filter_spec[1, i - j, im_rows]
                    rb, ib = key_spec[j, re_rows], key_spec[j, im_rows]
                    re, im = ra * rb - ia * ib, ra * ib + ia * rb
                    real = re if real is None else real + re
                    imag = im if imag is None else imag + im
                for where, value in ((re_rows, real), (im_rows, imag)):
                    high = value.astype(BF16)
                    summed_spec[0, where, cols] = high
                    summed_spec[1, where, cols] = (value - high.astype(F32)).astype(BF16)

    chunks = [(0, 0, rows), (1, 0, rows // 2), (1, rows // 2, rows // 2)]
    back_copies = {}

    def send_back(q):
        h, first_row, count = chunks[q]
        copies = []
        for o in (2, 1, 3):
            target = (z + o) % PAIRS
            its_rows, its_lanes = place(h, target, first_row, count)
            copy = remote(
                convolved.at[h, its_rows, its_lanes],
                back.at[h, pl.ds(first_row, count), lane_slice(z)],
                back_send.at[q, o - 1],
                back_recv.at[q, o - 1],
                (target, ch),
            )
            copy.start()
            copies.append(copy)
        mine_rows, mine_lanes = place(h, z, first_row, count)
        back[h, pl.ds(first_row, count), lane_slice(z)] = convolved[h, mine_rows, mine_lanes]
        pending.extend(copies)
        back_copies[q] = copies

    def convolve(h):
        products(h)
        high, low = summed_spec[0], summed_spec[1]
        result = dot(inverse[0], high) + dot(inverse[0], low) + dot(inverse[1], high)
        convolved[h] = result.astype(BF16)

    filter_spectra(0)
    key_spectra(0)
    key_copies[1] = scatter(1, gated, 1)
    loads[5].wait()
    convolve(0)
    send_back(0)
    take_rim(1, 0)
    make_queries(0)
    take_rim(1, 1)
    make_queries(1)
    filter_spectra(1)
    key_spectra(1)
    convolve(1)
    send_back(1)
    send_back(2)
    loads[6].wait()

    steps = [(1, 1), (0, 1), (1, 0), (0, 0)]
    pair_copies = {}

    def parts(q):
        h, first_row, count = chunks[q]
        half = count // 2
        return slice(first_row, first_row + half), slice(first_row + half, first_row + count)

    def slot_rows(q):
        return pl.ds(chunks[q][1] // 2, chunks[q][2] // 2)

    def weights_for(step, cc):
        yy = 1 - y if step[0] else y
        xx = 1 - x if step[1] else x
        return weight[:, pl.ds(pl.multiple_of(ch_of(yy, xx, cc) * channels, channels), channels)]

    def project(q):
        h, first_row, count = chunks[q]
        span = slice(first_row, first_row + count)
        for copy in back_copies[q]:
            copy.wait_recv()
        for cols in columns:
            summed = back[h, span, cols].astype(F32) + skip_ref[:, cols] * gated[h, span, cols].astype(F32)
            act[h, span, cols] = (queries[h, span, cols] * summed).astype(BF16)
        rows_in = act[h, span]
        for t, step in enumerate(steps):
            pair_out[h, t, span] = dot(rows_in, weights_for(step, 1 - core)).astype(BF16)
            copy = remote(
                pair_out.at[h, t, pl.ds(first_row, count)],
                pair_in.at[h, t, pl.ds(first_row, count)],
                pair_send.at[q, t],
                pair_recv.at[q, t],
                partner,
            )
            copy.start()
            pair_copies[q, t] = copy
            pending.append(copy)
        for t, step in enumerate(steps):
            own[h, t, span] = dot(rows_in, weights_for(step, core))

    first_copies, second_copies = {}, {}

    def pair_sum(q, t, way):
        h, part = chunks[q][0], parts(q)[way]
        return own[h, t, part] + pair_in[h, t, part].astype(F32)

    def first(q):
        h, where = chunks[q][0], slot_rows(q)
        for t, way, slot in ((0, 0, 0), (0, 1, 0), (1, 0, 1), (2, 1, 1)):
            if (t, way) != (0, 1):
                pair_copies[q, t].wait_recv()
            first_out[h, way, slot, where] = pair_sum(q, t, way).astype(BF16)
            copy = remote(
                first_out.at[h, way, slot, where],
                first_in.at[h, way, slot, where],
                first_send.at[q, way, slot],
                first_recv.at[q, way, slot],
                beside_y if way else beside_x,
            )
            copy.start()
            first_copies[q, way, slot] = copy
            pending.append(copy)

    def second(q):
        h, where = chunks[q][0], slot_rows(q)
        for way in range(2):
            first_copies[q, way, 0].wait_recv()
            t = 1 if way else 2
            total = pair_sum(q, t, way) + first_in[h, way, 0, where].astype(F32)
            second_out[h, way, where] = total.astype(BF16)
            copy = remote(
                second_out.at[h, way, where],
                second_in.at[h, way, where],
                second_send.at[q, way],
                second_recv.at[q, way],
                beside_x if way else beside_y,
            )
            copy.start()
            second_copies[q, way] = copy
            pending.append(copy)

    def finish(q):
        h, where = chunks[q][0], slot_rows(q)
        pair_copies[q, 3].wait_recv()
        for way in range(2):
            first_copies[q, way, 1].wait_recv()
            total = pair_sum(q, 3, way) + first_in[h, way, 1, where].astype(F32)
            second_copies[q, way].wait_recv()
            out_ref[h, parts(q)[way]] = (total + second_in[h, way, where].astype(F32)).astype(BF16)

    project(0)
    first(0)
    project(1)
    first(1)
    project(2)
    second(0)
    first(2)
    second(1)
    finish(0)
    second(2)
    finish(1)
    finish(2)

    @pl.when(z < PAIRS - 1)
    def _():
        rims[0, 0].wait_send()
        rims[1, 0].wait_send()

    @pl.when(z > 0)
    def _():
        rims[0, 1].wait_send()
        rims[1, 1].wait_send()

    for copy in pending:
        copy.wait_send()


def fused(features, short_weight, long_filter, skip_gain, out_weight):
    rows, channels = long_filter.shape[2:]
    middle = 2 * rows
    streams = jnp.transpose(features[:, 0], (0, 2, 1, 3))
    taps = jnp.transpose(short_weight, (1, 0, 2))
    forward, inverse = odd_tables(middle)
    in_vmem = pl.BlockSpec(memory_space=pltpu.VMEM)
    in_hbm = pl.BlockSpec(memory_space=pl.ANY)
    vmem = pltpu.VMEM
    dma = pltpu.SemaphoreType.DMA
    out = pl.pallas_call(
        kernel,
        out_shape=pltpu.VMEM((2, rows, channels), BF16),
        in_specs=[in_hbm] * 7,
        out_specs=in_vmem,
        scratch_shapes=[
            vmem(streams.shape, BF16),
            vmem(taps.shape, BF16),
            vmem((2, rows, channels), BF16),
            vmem((1, channels), F32),
            vmem(out_weight.shape, BF16),
            vmem(forward.shape, BF16),
            vmem(inverse.shape, BF16),
            vmem((2, 2, 2 * RIM, channels), BF16),
            vmem((2, 2, 2 * RIM, channels), BF16),
            vmem((2, 3, RIM + rows, channels), F32),
            vmem((2, rows, channels), BF16),
            vmem((2, rows, channels), F32),
            vmem((2, 2, middle, 2 * LANES), BF16),
            vmem((2, middle, 2 * LANES), BF16),
            vmem((2, rows, channels), BF16),
            vmem((2, 4, 2 * middle, LANES), F32),
            vmem((4, 2 * middle, LANES), F32),
            vmem((2, 2 * middle, 2 * LANES), BF16),
            vmem((2, 4, rows, channels), F32),
            vmem((2, rows, channels), BF16),
            vmem((2, 4, rows, channels), BF16),
            vmem((2, 4, rows, channels), BF16),
            vmem((2, 2, 2, rows // 2, channels), BF16),
            vmem((2, 2, 2, rows // 2, channels), BF16),
            vmem((2, 2, rows // 2, channels), BF16),
            vmem((2, 2, rows // 2, channels), BF16),
            dma((7,)),
            dma((2, 2)),
            dma((2, 2)),
            dma((2, 2, 3)),
            dma((2, 2, 3)),
            dma((3, 3)),
            dma((3, 3)),
            dma((3, 4)),
            dma((3, 4)),
            dma((3, 2, 2)),
            dma((3, 2, 2)),
            dma((3, 2)),
            dma((3, 2)),
        ],
        compiler_params=pltpu.CompilerParams(
            collective_id=0, has_side_effects=True, vmem_limit_bytes=62 * 1024 * 1024
        ),
        name="hyena",
    )(
        streams,
        taps,
        long_filter[:, 0],
        skip_gain.reshape(1, channels),
        out_weight,
        jnp.asarray(forward),
        jnp.asarray(inverse),
    )
    return out[:, None]


def from_behind(value, axis, steps):
    count = lax.axis_size(axis)
    initial, last = (max(0, -steps), min(count, count - steps))
    return lax.ppermute(value, axis, [(source, source + steps) for source in range(initial, last)])


def transform_tables(length):
    period = 2 * length
    indices = jnp.arange(period, dtype=jnp.int32)
    phases = indices[:, None] * indices[None, :] % period
    angles = phases.astype(jnp.float32) * (2.0 * math.pi / period)
    cosine = jnp.cos(angles)
    sine_table = jnp.sin(angles)
    forward_full = jnp.concatenate([cosine, -sine_table], axis=0)
    forward_data = forward_full[:, :length]
    inverse = jnp.concatenate([cosine[:length], -sine_table[:length]], axis=1) / period
    return (forward_full, forward_data, inverse)


def complex_product(first, second):
    middle = first.shape[-2] // 2
    real_a = first[..., :middle, :]
    imag_a = first[..., middle:, :]
    real_b = second[..., :middle, :]
    imag_b = second[..., middle:, :]
    return jnp.concatenate(
        [real_a * real_b - imag_a * imag_b, real_a * imag_b + imag_a * real_b], axis=-2
    )


def featurize(tokens, before, kernel):
    extended = jnp.concatenate([before, tokens], axis=0).astype(jnp.float32)
    length = tokens.shape[0]
    margin_rows = kernel.shape[0] - 1
    summed = jnp.zeros(tokens.shape, jnp.float32)
    for offset in range(kernel.shape[0]):
        summed = (
            summed
            + kernel[offset].astype(jnp.float32)
            * extended[margin_rows - offset : margin_rows - offset + length]
        )
    return summed


def ordered(blocks):
    return jnp.concatenate([blocks[0], jnp.flip(blocks[1], axis=0)], axis=0)


def local(features, short_weight, long_filter, skip_gain, out_weight):
    pair_count = lax.axis_size("ctx")
    blocks_all = 2 * pair_count
    position = lax.axis_index("ctx")
    length = features.shape[2]
    margin_rows = short_weight.shape[0] - 1
    trailing = features[:, 0, length - margin_rows :]
    from_before = from_behind(trailing[0], "ctx", 1)
    from_after = from_behind(trailing[1], "ctx", -1)
    second_rim = jnp.where(position == pair_count - 1, trailing[0], from_after)
    first_feat = featurize(features[0, 0], from_before, short_weight)
    second_feat = featurize(features[1, 0], second_rim, short_weight)
    featured = jnp.stack([first_feat, second_feat], axis=0)
    queries = featured[:, :, 0]
    gated_keys = (featured[:, :, 1] * featured[:, :, 2]).astype(jnp.bfloat16)
    forward_full, forward_data, inverse = transform_tables(length)
    precise = lax.Precision.HIGHEST
    moved_gated, moved_filter = (
        lax.all_to_all(gated_keys[:, None], "ctx", split_axis=3, concat_axis=1, tiled=True),
        lax.all_to_all(long_filter, "ctx", split_axis=3, concat_axis=1, tiled=True),
    )
    ordered_gated = ordered(moved_gated).astype(jnp.float32)
    lag_order = ordered(moved_filter)
    padded = jnp.concatenate(
        [jnp.zeros((1,) + lag_order.shape[1:], lag_order.dtype), lag_order], axis=0
    )
    segments = jnp.concatenate([padded[1:], padded[:-1]], axis=1).astype(jnp.float32)
    responses = jnp.einsum("fm,kmc->kfc", forward_full, segments, precision=precise)
    spectra = jnp.einsum("fn,knc->kfc", forward_data, ordered_gated, precision=precise)
    sources = jnp.arange(blocks_all, dtype=jnp.int32)

    def one_target(target):
        distance = target - sources
        picked = jnp.take(responses, jnp.maximum(distance, 0), axis=0)
        products = complex_product(picked, spectra)
        summed = jnp.sum(jnp.where((distance >= 0)[:, None, None], products, 0.0), axis=0)
        return jnp.dot(inverse, summed, precision=precise)

    group_size = math.gcd(blocks_all, 8)
    grouped = sources.reshape(blocks_all // group_size, group_size)
    outputs = lax.map(jax.vmap(one_target), grouped).reshape(
        (blocks_all, length, responses.shape[-1])
    )
    blocks = jnp.stack([outputs[:pair_count], jnp.flip(outputs[pair_count:], axis=0)], axis=0)
    returned = lax.all_to_all(blocks, "ctx", split_axis=1, concat_axis=3, tiled=True)
    convolved = returned[:, 0]
    activated = (queries * (convolved + skip_gain * gated_keys.astype(jnp.float32))).astype(
        jnp.bfloat16
    )
    token_rows = activated.reshape(2 * length, activated.shape[-1])
    channels = token_rows.shape[1]
    owned = lax.psum_scatter(
        lax.dot_general(
            out_weight, token_rows, (((0,), (1,)), ((), ())), preferred_element_type=jnp.float32
        ).astype(jnp.bfloat16),
        "ch",
        scatter_dimension=0,
        tiled=True,
    ).astype(jnp.float32)
    result = owned.T
    return result.astype(jnp.bfloat16).reshape(2, 1, length, channels)


def solution(mesh):
    in_specs = (
        P(None, "ctx", None, None, "ch"),
        P(None, None, "ch"),
        P(None, "ctx", None, "ch"),
        P("ch"),
        P("ch", None),
    )
    out_specs = P(None, "ctx", None, "ch")
    shape = dict(mesh.shape)
    suits = shape == {"ctx": PAIRS, "ch": 8}
    body = fused if suits else local
    return jax.shard_map(body, mesh=mesh, in_specs=in_specs, out_specs=out_specs, check_vma=False)
```

```python
import math

import jax
import jax.numpy as jnp
import ml_dtypes
import numpy as np
from jax import lax
from jax.experimental import pallas as pl
from jax.experimental.pallas import tpu as pltpu
from jax.sharding import PartitionSpec as P

F32 = jnp.float32
BF16 = jnp.bfloat16
MESH = pl.DeviceIdType.MESH
RIM = 8
STRIP = 64
LANES = 128
PAIRS = 4


def halves(values):
    high = values.astype(ml_dtypes.bfloat16)
    low = (values - high.astype(np.float64)).astype(ml_dtypes.bfloat16)
    return np.stack([high, low])


def odd_tables(length):
    k = np.arange(length)[:, None]
    t = np.arange(length)[None, :]
    angles = ((2 * k + 1) * t % (4 * length)) * (np.pi / (2 * length))
    forward = np.concatenate([np.cos(angles), -np.sin(angles)], axis=0)
    return halves(forward), halves(forward.T / length)


def dot(a, b):
    return jnp.dot(a, b, preferred_element_type=F32)


def kernel(
    x_hbm,
    taps_hbm,
    filter_hbm,
    skip_hbm,
    weight_hbm,
    forward_hbm,
    inverse_hbm,
    out_ref,
    x_ref,
    taps_ref,
    filter_ref,
    skip_ref,
    weight,
    forward,
    inverse,
    rim_out,
    halo,
    wide,
    gated,
    queries,
    moved,
    convolved,
    back,
    filter_spec,
    key_spec,
    summed_spec,
    early,
    own,
    act,
    pair_out,
    pair_in,
    first_out,
    first_in,
    second_out,
    second_in,
    local_sem,
    halo_send,
    halo_recv,
    move_send,
    move_recv,
    back_send,
    back_recv,
    pair_send,
    pair_recv,
    first_send,
    first_recv,
    second_send,
    second_recv,
):
    rows, channels = gated.shape[1:]
    taps = taps_ref.shape[1]
    middle = forward.shape[2]
    z = lax.axis_index("ctx")
    ch = lax.axis_index("ch")
    core, x, y = ch % 2, ch // 2 % 2, ch // 4

    def ch_of(yy, xx, cc):
        return yy * 4 + xx * 2 + cc

    partner = (z, ch_of(y, x, 1 - core))
    beside_x = (z, ch_of(y, 1 - x, core))
    beside_y = (z, ch_of(1 - y, x, core))

    sources = (x_hbm, filter_hbm, taps_hbm, skip_hbm, forward_hbm, inverse_hbm, weight_hbm)
    places = (x_ref, filter_ref, taps_ref, skip_ref, forward, inverse, weight)
    loads = [
        pltpu.make_async_copy(source, target, local_sem.at[i])
        for i, (source, target) in enumerate(zip(sources, places))
    ]
    for load in loads[:4]:
        load.start()

    barrier = pltpu.get_barrier_semaphore()
    peers = [((z + o) % PAIRS, ch) for o in range(1, PAIRS)] + [partner, beside_x, beside_y]
    for peer in peers:
        pl.semaphore_signal(barrier, inc=1, device_id=peer, device_id_type=MESH)
    pl.semaphore_wait(barrier, len(peers))

    for load in loads[4:]:
        load.start()
    pending = []

    def remote(src, dst, send, recv, device):
        return pltpu.make_async_remote_copy(
            src_ref=src, dst_ref=dst, send_sem=send, recv_sem=recv, device_id=device, device_id_type=MESH
        )

    def keep(kind, source, h):
        mine_rows, mine_lanes = place(h, z)
        moved[kind, h, mine_rows, mine_lanes] = source[h, :, lane_slice(z)]

    def place(h, owner, first_row=0, count=None):
        block = owner if h == 0 else PAIRS - 1 - owner
        count = rows if count is None else count
        return (
            pl.ds(pl.multiple_of(block % 2 * rows + first_row, count), count),
            pl.ds(pl.multiple_of(block // 2 * LANES, LANES), LANES),
        )

    def lane_slice(owner):
        return pl.ds(pl.multiple_of(owner * LANES, LANES), LANES)

    def scatter(kind, source, h):
        mine_rows, mine_lanes = place(h, z)
        copies = []
        for o in (3, 2, 1):
            target = (z + o) % PAIRS
            copy = remote(
                source.at[h, :, lane_slice(target)],
                moved.at[kind, h, mine_rows, mine_lanes],
                move_send.at[kind, h, o - 1],
                move_recv.at[kind, h, o - 1],
                (target, ch),
            )
            copy.start()
            copies.append(copy)
        pending.extend(copies)
        return copies

    filter_copies, key_copies = [None, None], [None, None]
    filter_copies[0] = scatter(0, filter_hbm, 0)
    loads[0].wait()

    def widen(h):
        for s in range(3):
            wide[h, s, RIM:] = x_ref[h, s].astype(F32)

    tails = [[x_ref[h, s, rows - 2 * RIM :].astype(F32)[RIM:] for s in range(3)] for h in range(2)]
    rims = {}
    for kind, streams in ((0, (1, 2)), (1, (0, 0))):
        for h in range(2):
            rim_out[kind, h] = jnp.concatenate([tails[h][s] for s in streams], axis=0).astype(BF16)
            rims[kind, h] = remote(
                rim_out.at[kind, h],
                halo.at[kind, h],
                halo_send.at[kind, h],
                halo_recv.at[kind, h],
                ((z + (1 if h == 0 else 3)) % PAIRS, ch),
            )

    def send_rims(kind):
        @pl.when(z < PAIRS - 1)
        def _():
            rims[kind, 0].start()

        @pl.when(z > 0)
        def _():
            rims[kind, 1].start()

    def take_rim(kind, h):
        has = z > 0 if h == 0 else z < PAIRS - 1

        @pl.when(has)
        def _():
            rims[kind, h].wait_recv()

        @pl.when(jnp.logical_not(has))
        def _():
            halo[kind, h] = jnp.zeros(halo.shape[2:], BF16) if h == 0 else rim_out[kind, 0]

        both = halo[kind, h].astype(F32)
        for m, s in enumerate((1, 2) if kind == 0 else (0,)):
            wide[h, s, :RIM] = both[m * RIM : (m + 1) * RIM]

    send_rims(0)
    widen(0)
    widen(1)

    loads[2].wait()
    tap_rows = [taps_ref[s].astype(F32) for s in range(3)]

    def taps_of(h, s, cols):
        total = None
        for i in range(taps):
            tap = tap_rows[s][i : i + 1, cols]
            term = tap * wide[h, s, pl.ds(RIM - i, rows), cols]
            total = term if total is None else total + term
        return total

    columns = [slice(a, a + LANES) for a in range(0, channels, LANES)]

    def make_keys(h):
        for cols in columns:
            gated[h, :, cols] = (taps_of(h, 1, cols) * taps_of(h, 2, cols)).astype(BF16)

    def make_queries(h):
        for cols in columns:
            queries[h, :, cols] = taps_of(h, 0, cols)

    take_rim(0, 0)
    make_keys(0)
    key_copies[0] = scatter(1, gated, 0)
    keep(1, gated, 0)
    send_rims(1)
    filter_copies[1] = scatter(0, filter_hbm, 1)
    loads[1].wait()
    keep(0, filter_ref, 0)
    keep(0, filter_ref, 1)
    take_rim(0, 1)
    make_keys(1)
    loads[4].wait()

    signs = (1 - 2 * (lax.broadcasted_iota(jnp.int32, (middle, LANES), 0) % 2)).astype(F32)

    def spectrum(kind, h):
        data = moved[kind, h]
        return dot(forward[0], data) + dot(forward[1], data)

    def filter_spectra(h):
        for copy in filter_copies[h]:
            copy.wait_recv()
        both = spectrum(0, h)
        for m in range(2):
            filter_spec[0, 2 * h + m] = both[:, m * LANES : (m + 1) * LANES]
        for b in (2 * h, 2 * h + 1):
            if b == 0:
                filter_spec[1, 0] = filter_spec[0, 0]
            else:
                filter_spec[1, b, :middle] = filter_spec[0, b, :middle] - signs * filter_spec[0, b - 1, middle:]
                filter_spec[1, b, middle:] = filter_spec[0, b, middle:] + signs * filter_spec[0, b - 1, :middle]

    def key_spectra(h):
        for copy in key_copies[h]:
            copy.wait_recv()
        both = spectrum(1, h)
        for m in range(2):
            key_spec[2 * h + m] = both[:, m * LANES : (m + 1) * LANES]

    def pair_products(i, sources, re_rows, im_rows):
        real, imag = None, None
        for j in sources:
            ra, ia = filter_spec[1, i - j, re_rows], filter_spec[1, i - j, im_rows]
            rb, ib = key_spec[j, re_rows], key_spec[j, im_rows]
            re, im = ra * rb - ia * ib, ra * ib + ia * rb
            real = re if real is None else real + re
            imag = im if imag is None else imag + im
        return real, imag

    strips = [
        (slice(start, start + STRIP), slice(middle + start, middle + start + STRIP))
        for start in range(0, middle, STRIP)
    ]

    def early_products():
        for m in range(2):
            for re_rows, im_rows in strips:
                early[m, re_rows], early[m, im_rows] = pair_products(2 + m, (0, 1), re_rows, im_rows)

    def products(h):
        for m in range(2):
            i = 2 * h + m
            cols = slice(m * LANES, (m + 1) * LANES)
            for re_rows, im_rows in strips:
                sums = pair_products(i, range(2 * h, i + 1), re_rows, im_rows)
                for where, value in zip((re_rows, im_rows), sums):
                    if h == 1:
                        value = value + early[m, where]
                    high = value.astype(BF16)
                    summed_spec[0, where, cols] = high
                    summed_spec[1, where, cols] = (value - high.astype(F32)).astype(BF16)

    chunks = [(0, 0, rows), (1, 0, rows // 2), (1, rows // 2, rows // 2)]
    back_copies = {}

    def send_back(q):
        h, first_row, count = chunks[q]
        copies = []
        for o in (2, 1, 3):
            target = (z + o) % PAIRS
            its_rows, its_lanes = place(h, target, first_row, count)
            copy = remote(
                convolved.at[h, its_rows, its_lanes],
                back.at[h, pl.ds(first_row, count), lane_slice(z)],
                back_send.at[q, o - 1],
                back_recv.at[q, o - 1],
                (target, ch),
            )
            copy.start()
            copies.append(copy)
        mine_rows, mine_lanes = place(h, z, first_row, count)
        back[h, pl.ds(first_row, count), lane_slice(z)] = convolved[h, mine_rows, mine_lanes]
        pending.extend(copies)
        back_copies[q] = copies

    def convolve(h):
        products(h)
        high, low = summed_spec[0], summed_spec[1]
        result = dot(inverse[0], high) + dot(inverse[0], low) + dot(inverse[1], high)
        convolved[h] = result.astype(BF16)

    filter_spectra(0)
    key_spectra(0)
    key_copies[1] = scatter(1, gated, 1)
    keep(1, gated, 1)
    loads[5].wait()
    convolve(0)
    send_back(0)
    take_rim(1, 0)
    make_queries(0)
    take_rim(1, 1)
    make_queries(1)
    filter_spectra(1)
    early_products()
    key_spectra(1)
    convolve(1)
    send_back(1)
    send_back(2)
    loads[6].wait()
    loads[3].wait()

    steps = [(1, 1), (0, 1), (1, 0), (0, 0)]
    pair_copies = {}

    def parts(q):
        h, first_row, count = chunks[q]
        half = count // 2
        return slice(first_row, first_row + half), slice(first_row + half, first_row + count)

    def slot_rows(q):
        return pl.ds(chunks[q][1] // 2, chunks[q][2] // 2)

    def weights_for(step, cc):
        yy = 1 - y if step[0] else y
        xx = 1 - x if step[1] else x
        return weight[:, pl.ds(pl.multiple_of(ch_of(yy, xx, cc) * channels, channels), channels)]

    def project(q):
        h, first_row, count = chunks[q]
        span = slice(first_row, first_row + count)
        for copy in back_copies[q]:
            copy.wait_recv()
        for cols in columns:
            summed = back[h, span, cols].astype(F32) + skip_ref[:, cols] * gated[h, span, cols].astype(F32)
            act[h, span, cols] = (queries[h, span, cols] * summed).astype(BF16)
        rows_in = act[h, span]
        for t, step in enumerate(steps):
            pair_out[h, t, span] = dot(rows_in, weights_for(step, 1 - core)).astype(BF16)
            copy = remote(
                pair_out.at[h, t, pl.ds(first_row, count)],
                pair_in.at[h, t, pl.ds(first_row, count)],
                pair_send.at[q, t],
                pair_recv.at[q, t],
                partner,
            )
            copy.start()
            pair_copies[q, t] = copy
            pending.append(copy)

    def project_own(q, t):
        h, first_row, count = chunks[q]
        span = slice(first_row, first_row + count)
        own[h, t, span] = dot(act[h, span], weights_for(steps[t], core))

    first_copies, second_copies = {}, {}

    def pair_sum(q, t, way):
        h, part = chunks[q][0], parts(q)[way]
        return own[h, t, part] + pair_in[h, t, part].astype(F32)

    def first(q):
        h, where = chunks[q][0], slot_rows(q)
        for t, way, slot in ((0, 0, 0), (0, 1, 0), (1, 0, 1), (2, 1, 1)):
            if (t, way) != (0, 1):
                project_own(q, t)
                pair_copies[q, t].wait_recv()
            first_out[h, way, slot, where] = pair_sum(q, t, way).astype(BF16)
            copy = remote(
                first_out.at[h, way, slot, where],
                first_in.at[h, way, slot, where],
                first_send.at[q, way, slot],
                first_recv.at[q, way, slot],
                beside_y if way else beside_x,
            )
            copy.start()
            first_copies[q, way, slot] = copy
            pending.append(copy)
        project_own(q, 3)

    def second(q):
        h, where = chunks[q][0], slot_rows(q)
        for way in range(2):
            first_copies[q, way, 0].wait_recv()
            t = 1 if way else 2
            total = pair_sum(q, t, way) + first_in[h, way, 0, where].astype(F32)
            second_out[h, way, where] = total.astype(BF16)
            copy = remote(
                second_out.at[h, way, where],
                second_in.at[h, way, where],
                second_send.at[q, way],
                second_recv.at[q, way],
                beside_x if way else beside_y,
            )
            copy.start()
            second_copies[q, way] = copy
            pending.append(copy)

    def finish(q):
        h, where = chunks[q][0], slot_rows(q)
        pair_copies[q, 3].wait_recv()
        for way in range(2):
            first_copies[q, way, 1].wait_recv()
            total = pair_sum(q, 3, way) + first_in[h, way, 1, where].astype(F32)
            second_copies[q, way].wait_recv()
            out_ref[h, parts(q)[way]] = (total + second_in[h, way, where].astype(F32)).astype(BF16)

    project(0)
    first(0)
    project(1)
    first(1)
    project(2)
    second(0)
    first(2)
    second(1)
    finish(0)
    second(2)
    finish(1)
    finish(2)

    @pl.when(z < PAIRS - 1)
    def _():
        rims[0, 0].wait_send()
        rims[1, 0].wait_send()

    @pl.when(z > 0)
    def _():
        rims[0, 1].wait_send()
        rims[1, 1].wait_send()

    for copy in pending:
        copy.wait_send()


def fused(features, short_weight, long_filter, skip_gain, out_weight):
    rows, channels = long_filter.shape[2:]
    middle = 2 * rows
    streams = jnp.transpose(features[:, 0], (0, 2, 1, 3))
    taps = jnp.transpose(short_weight, (1, 0, 2))
    forward, inverse = odd_tables(middle)
    in_vmem = pl.BlockSpec(memory_space=pltpu.VMEM)
    in_hbm = pl.BlockSpec(memory_space=pl.ANY)
    vmem = pltpu.VMEM
    dma = pltpu.SemaphoreType.DMA
    out = pl.pallas_call(
        kernel,
        out_shape=pltpu.VMEM((2, rows, channels), BF16),
        in_specs=[in_hbm] * 7,
        out_specs=in_vmem,
        scratch_shapes=[
            vmem(streams.shape, BF16),
            vmem(taps.shape, BF16),
            vmem((2, rows, channels), BF16),
            vmem((1, channels), F32),
            vmem(out_weight.shape, BF16),
            vmem(forward.shape, BF16),
            vmem(inverse.shape, BF16),
            vmem((2, 2, 2 * RIM, channels), BF16),
            vmem((2, 2, 2 * RIM, channels), BF16),
            vmem((2, 3, RIM + rows, channels), F32),
            vmem((2, rows, channels), BF16),
            vmem((2, rows, channels), F32),
            vmem((2, 2, middle, 2 * LANES), BF16),
            vmem((2, middle, 2 * LANES), BF16),
            vmem((2, rows, channels), BF16),
            vmem((2, 4, 2 * middle, LANES), F32),
            vmem((4, 2 * middle, LANES), F32),
            vmem((2, 2 * middle, 2 * LANES), BF16),
            vmem((2, 2 * middle, LANES), F32),
            vmem((2, 4, rows, channels), F32),
            vmem((2, rows, channels), BF16),
            vmem((2, 4, rows, channels), BF16),
            vmem((2, 4, rows, channels), BF16),
            vmem((2, 2, 2, rows // 2, channels), BF16),
            vmem((2, 2, 2, rows // 2, channels), BF16),
            vmem((2, 2, rows // 2, channels), BF16),
            vmem((2, 2, rows // 2, channels), BF16),
            dma((7,)),
            dma((2, 2)),
            dma((2, 2)),
            dma((2, 2, 3)),
            dma((2, 2, 3)),
            dma((3, 3)),
            dma((3, 3)),
            dma((3, 4)),
            dma((3, 4)),
            dma((3, 2, 2)),
            dma((3, 2, 2)),
            dma((3, 2)),
            dma((3, 2)),
        ],
        compiler_params=pltpu.CompilerParams(
            collective_id=0, has_side_effects=True, vmem_limit_bytes=62 * 1024 * 1024
        ),
        name="hyena",
    )(
        streams,
        taps,
        long_filter[:, 0],
        skip_gain.reshape(1, channels),
        out_weight,
        jnp.asarray(forward),
        jnp.asarray(inverse),
    )
    return out[:, None]


def from_behind(value, axis, steps):
    count = lax.axis_size(axis)
    initial, last = (max(0, -steps), min(count, count - steps))
    return lax.ppermute(value, axis, [(source, source + steps) for source in range(initial, last)])


def transform_tables(length):
    period = 2 * length
    indices = jnp.arange(period, dtype=jnp.int32)
    phases = indices[:, None] * indices[None, :] % period
    angles = phases.astype(jnp.float32) * (2.0 * math.pi / period)
    cosine = jnp.cos(angles)
    sine_table = jnp.sin(angles)
    forward_full = jnp.concatenate([cosine, -sine_table], axis=0)
    forward_data = forward_full[:, :length]
    inverse = jnp.concatenate([cosine[:length], -sine_table[:length]], axis=1) / period
    return (forward_full, forward_data, inverse)


def complex_product(first, second):
    middle = first.shape[-2] // 2
    real_a = first[..., :middle, :]
    imag_a = first[..., middle:, :]
    real_b = second[..., :middle, :]
    imag_b = second[..., middle:, :]
    return jnp.concatenate(
        [real_a * real_b - imag_a * imag_b, real_a * imag_b + imag_a * real_b], axis=-2
    )


def featurize(tokens, before, kernel):
    extended = jnp.concatenate([before, tokens], axis=0).astype(jnp.float32)
    length = tokens.shape[0]
    margin_rows = kernel.shape[0] - 1
    summed = jnp.zeros(tokens.shape, jnp.float32)
    for offset in range(kernel.shape[0]):
        summed = (
            summed
            + kernel[offset].astype(jnp.float32)
            * extended[margin_rows - offset : margin_rows - offset + length]
        )
    return summed


def ordered(blocks):
    return jnp.concatenate([blocks[0], jnp.flip(blocks[1], axis=0)], axis=0)


def local(features, short_weight, long_filter, skip_gain, out_weight):
    pair_count = lax.axis_size("ctx")
    blocks_all = 2 * pair_count
    position = lax.axis_index("ctx")
    length = features.shape[2]
    margin_rows = short_weight.shape[0] - 1
    trailing = features[:, 0, length - margin_rows :]
    from_before = from_behind(trailing[0], "ctx", 1)
    from_after = from_behind(trailing[1], "ctx", -1)
    second_rim = jnp.where(position == pair_count - 1, trailing[0], from_after)
    first_feat = featurize(features[0, 0], from_before, short_weight)
    second_feat = featurize(features[1, 0], second_rim, short_weight)
    featured = jnp.stack([first_feat, second_feat], axis=0)
    queries = featured[:, :, 0]
    gated_keys = (featured[:, :, 1] * featured[:, :, 2]).astype(jnp.bfloat16)
    forward_full, forward_data, inverse = transform_tables(length)
    precise = lax.Precision.HIGHEST
    moved_gated, moved_filter = (
        lax.all_to_all(gated_keys[:, None], "ctx", split_axis=3, concat_axis=1, tiled=True),
        lax.all_to_all(long_filter, "ctx", split_axis=3, concat_axis=1, tiled=True),
    )
    ordered_gated = ordered(moved_gated).astype(jnp.float32)
    lag_order = ordered(moved_filter)
    padded = jnp.concatenate(
        [jnp.zeros((1,) + lag_order.shape[1:], lag_order.dtype), lag_order], axis=0
    )
    segments = jnp.concatenate([padded[1:], padded[:-1]], axis=1).astype(jnp.float32)
    responses = jnp.einsum("fm,kmc->kfc", forward_full, segments, precision=precise)
    spectra = jnp.einsum("fn,knc->kfc", forward_data, ordered_gated, precision=precise)
    sources = jnp.arange(blocks_all, dtype=jnp.int32)

    def one_target(target):
        distance = target - sources
        picked = jnp.take(responses, jnp.maximum(distance, 0), axis=0)
        products = complex_product(picked, spectra)
        summed = jnp.sum(jnp.where((distance >= 0)[:, None, None], products, 0.0), axis=0)
        return jnp.dot(inverse, summed, precision=precise)

    group_size = math.gcd(blocks_all, 8)
    grouped = sources.reshape(blocks_all // group_size, group_size)
    outputs = lax.map(jax.vmap(one_target), grouped).reshape(
        (blocks_all, length, responses.shape[-1])
    )
    blocks = jnp.stack([outputs[:pair_count], jnp.flip(outputs[pair_count:], axis=0)], axis=0)
    returned = lax.all_to_all(blocks, "ctx", split_axis=1, concat_axis=3, tiled=True)
    convolved = returned[:, 0]
    activated = (queries * (convolved + skip_gain * gated_keys.astype(jnp.float32))).astype(
        jnp.bfloat16
    )
    token_rows = activated.reshape(2 * length, activated.shape[-1])
    channels = token_rows.shape[1]
    owned = lax.psum_scatter(
        lax.dot_general(
            out_weight, token_rows, (((0,), (1,)), ((), ())), preferred_element_type=jnp.float32
        ).astype(jnp.bfloat16),
        "ch",
        scatter_dimension=0,
        tiled=True,
    ).astype(jnp.float32)
    result = owned.T
    return result.astype(jnp.bfloat16).reshape(2, 1, length, channels)


def solution(mesh):
    in_specs = (
        P(None, "ctx", None, None, "ch"),
        P(None, None, "ch"),
        P(None, "ctx", None, "ch"),
        P("ch"),
        P("ch", None),
    )
    out_specs = P(None, "ctx", None, "ch")
    shape = dict(mesh.shape)
    suits = shape == {"ctx": PAIRS, "ch": 8}
    body = fused if suits else local
    return jax.shard_map(body, mesh=mesh, in_specs=in_specs, out_specs=out_specs, check_vma=False)
```

```python
import math

import jax
import jax.numpy as jnp
import ml_dtypes
import numpy as np
from jax import lax
from jax.experimental import pallas as pl
from jax.experimental.pallas import tpu as pltpu
from jax.sharding import PartitionSpec as P

F32 = jnp.float32
BF16 = jnp.bfloat16
MESH = pl.DeviceIdType.MESH
RIM = 8
STRIP = 64
LANES = 128
PAIRS = 4


def halves(values):
    high = values.astype(ml_dtypes.bfloat16)
    low = (values - high.astype(np.float64)).astype(ml_dtypes.bfloat16)
    return np.stack([high, low])


def odd_tables(length):
    k = np.arange(length)[:, None]
    t = np.arange(length)[None, :]
    angles = ((2 * k + 1) * t % (4 * length)) * (np.pi / (2 * length))
    forward = np.concatenate([np.cos(angles), -np.sin(angles)], axis=0)
    return halves(forward), halves(forward.T / length)


def dot(a, b):
    return jnp.dot(a, b, preferred_element_type=F32)


def kernel(
    x_hbm,
    taps_hbm,
    filter_hbm,
    skip_hbm,
    weight_hbm,
    forward_hbm,
    inverse_hbm,
    out_ref,
    x_ref,
    taps_ref,
    filter_ref,
    skip_ref,
    weight,
    forward,
    inverse,
    rim_out,
    halo,
    wide,
    gated,
    queries,
    moved,
    convolved,
    back,
    filter_spec,
    key_spec,
    summed_spec,
    early,
    own,
    act,
    pair_out,
    pair_in,
    first_out,
    first_in,
    second_out,
    second_in,
    local_sem,
    halo_send,
    halo_recv,
    move_send,
    move_recv,
    back_send,
    back_recv,
    pair_send,
    pair_recv,
    first_send,
    first_recv,
    second_send,
    second_recv,
):
    rows, channels = gated.shape[1:]
    taps = taps_ref.shape[1]
    middle = forward.shape[2]
    z = lax.axis_index("ctx")
    ch = lax.axis_index("ch")
    core, x, y = ch % 2, ch // 2 % 2, ch // 4

    def ch_of(yy, xx, cc):
        return yy * 4 + xx * 2 + cc

    partner = (z, ch_of(y, x, 1 - core))
    beside_x = (z, ch_of(y, 1 - x, core))
    beside_y = (z, ch_of(1 - y, x, core))

    sources = (x_hbm, filter_hbm, taps_hbm, skip_hbm, forward_hbm, inverse_hbm, weight_hbm)
    places = (x_ref, filter_ref, taps_ref, skip_ref, forward, inverse, weight)
    loads = [
        pltpu.make_async_copy(source, target, local_sem.at[i])
        for i, (source, target) in enumerate(zip(sources, places))
    ]
    for load in loads[:4]:
        load.start()

    barrier = pltpu.get_barrier_semaphore()
    peers = [((z + o) % PAIRS, ch) for o in range(1, PAIRS)] + [partner, beside_x, beside_y]
    for peer in peers:
        pl.semaphore_signal(barrier, inc=1, device_id=peer, device_id_type=MESH)
    pl.semaphore_wait(barrier, len(peers))

    for load in loads[4:]:
        load.start()
    pending = []

    def remote(src, dst, send, recv, device):
        return pltpu.make_async_remote_copy(
            src_ref=src, dst_ref=dst, send_sem=send, recv_sem=recv, device_id=device, device_id_type=MESH
        )

    def keep(kind, source, h):
        mine_rows, mine_lanes = place(h, z)
        moved[kind, h, mine_rows, mine_lanes] = source[h, :, lane_slice(z)]

    def place(h, owner, first_row=0, count=None):
        block = owner if h == 0 else PAIRS - 1 - owner
        count = rows if count is None else count
        return (
            pl.ds(pl.multiple_of(block % 2 * rows + first_row, count), count),
            pl.ds(pl.multiple_of(block // 2 * LANES, LANES), LANES),
        )

    def lane_slice(owner):
        return pl.ds(pl.multiple_of(owner * LANES, LANES), LANES)

    def scatter(kind, source, h):
        mine_rows, mine_lanes = place(h, z)
        copies = []
        for o in (2, 1, 3):
            target = (z + o) % PAIRS
            copy = remote(
                source.at[h, :, lane_slice(target)],
                moved.at[kind, h, mine_rows, mine_lanes],
                move_send.at[kind, h, o - 1],
                move_recv.at[kind, h, o - 1],
                (target, ch),
            )
            copy.start()
            copies.append(copy)
        pending.extend(copies)
        return copies

    filter_copies, key_copies = [None, None], [None, None]
    loads[0].wait()

    def widen(h):
        for s in range(3):
            wide[h, s, RIM:] = x_ref[h, s].astype(F32)

    tails = [[x_ref[h, s, rows - 2 * RIM :].astype(F32)[RIM:] for s in range(3)] for h in range(2)]
    rims = {}
    for kind, streams in ((0, (1, 2)), (1, (0, 0))):
        for h in range(2):
            rim_out[kind, h] = jnp.concatenate([tails[h][s] for s in streams], axis=0).astype(BF16)
            rims[kind, h] = remote(
                rim_out.at[kind, h],
                halo.at[kind, h],
                halo_send.at[kind, h],
                halo_recv.at[kind, h],
                ((z + (1 if h == 0 else 3)) % PAIRS, ch),
            )

    def send_rims(kind):
        @pl.when(z < PAIRS - 1)
        def _():
            rims[kind, 0].start()

        @pl.when(z > 0)
        def _():
            rims[kind, 1].start()

    def take_rim(kind, h):
        has = z > 0 if h == 0 else z < PAIRS - 1

        @pl.when(has)
        def _():
            rims[kind, h].wait_recv()

        @pl.when(jnp.logical_not(has))
        def _():
            halo[kind, h] = jnp.zeros(halo.shape[2:], BF16) if h == 0 else rim_out[kind, 0]

        both = halo[kind, h].astype(F32)
        for m, s in enumerate((1, 2) if kind == 0 else (0,)):
            wide[h, s, :RIM] = both[m * RIM : (m + 1) * RIM]

    send_rims(0)
    loads[1].wait()
    filter_copies[0] = scatter(0, filter_ref, 0)
    widen(0)
    widen(1)

    loads[2].wait()
    tap_rows = [taps_ref[s].astype(F32) for s in range(3)]

    def taps_of(h, s, cols):
        total = None
        for i in range(taps):
            tap = tap_rows[s][i : i + 1, cols]
            term = tap * wide[h, s, pl.ds(RIM - i, rows), cols]
            total = term if total is None else total + term
        return total

    columns = [slice(a, a + LANES) for a in range(0, channels, LANES)]

    def make_keys(h):
        for cols in columns:
            gated[h, :, cols] = (taps_of(h, 1, cols) * taps_of(h, 2, cols)).astype(BF16)

    def make_queries(h):
        for cols in columns:
            queries[h, :, cols] = taps_of(h, 0, cols)

    take_rim(0, 0)
    make_keys(0)
    key_copies[0] = scatter(1, gated, 0)
    keep(1, gated, 0)
    send_rims(1)
    filter_copies[1] = scatter(0, filter_ref, 1)
    keep(0, filter_ref, 0)
    keep(0, filter_ref, 1)
    take_rim(0, 1)
    make_keys(1)
    loads[4].wait()

    signs = (1 - 2 * (lax.broadcasted_iota(jnp.int32, (middle, LANES), 0) % 2)).astype(F32)

    def spectrum(kind, h):
        data = moved[kind, h]
        return dot(forward[0], data) + dot(forward[1], data)

    def filter_spectra(h):
        for copy in filter_copies[h]:
            copy.wait_recv()
        both = spectrum(0, h)
        for m in range(2):
            filter_spec[0, 2 * h + m] = both[:, m * LANES : (m + 1) * LANES]
        for b in (2 * h, 2 * h + 1):
            if b == 0:
                filter_spec[1, 0] = filter_spec[0, 0]
            else:
                filter_spec[1, b, :middle] = filter_spec[0, b, :middle] - signs * filter_spec[0, b - 1, middle:]
                filter_spec[1, b, middle:] = filter_spec[0, b, middle:] + signs * filter_spec[0, b - 1, :middle]

    def key_spectra(h):
        for copy in key_copies[h]:
            copy.wait_recv()
        both = spectrum(1, h)
        for m in range(2):
            key_spec[2 * h + m] = both[:, m * LANES : (m + 1) * LANES]

    def pair_products(i, sources, re_rows, im_rows):
        real, imag = None, None
        for j in sources:
            ra, ia = filter_spec[1, i - j, re_rows], filter_spec[1, i - j, im_rows]
            rb, ib = key_spec[j, re_rows], key_spec[j, im_rows]
            re, im = ra * rb - ia * ib, ra * ib + ia * rb
            real = re if real is None else real + re
            imag = im if imag is None else imag + im
        return real, imag

    strips = [
        (slice(start, start + STRIP), slice(middle + start, middle + start + STRIP))
        for start in range(0, middle, STRIP)
    ]

    def early_products():
        for m in range(2):
            for re_rows, im_rows in strips:
                early[m, re_rows], early[m, im_rows] = pair_products(2 + m, (0, 1), re_rows, im_rows)

    def products(h):
        for m in range(2):
            i = 2 * h + m
            cols = slice(m * LANES, (m + 1) * LANES)
            for re_rows, im_rows in strips:
                sums = pair_products(i, range(2 * h, i + 1), re_rows, im_rows)
                for where, value in zip((re_rows, im_rows), sums):
                    if h == 1:
                        value = value + early[m, where]
                    high = value.astype(BF16)
                    summed_spec[0, where, cols] = high
                    summed_spec[1, where, cols] = (value - high.astype(F32)).astype(BF16)

    chunks = [(0, 0, rows), (1, 0, rows // 2), (1, rows // 2, rows // 2)]
    back_copies = {}

    def send_back(q):
        h, first_row, count = chunks[q]
        copies = []
        for o in (2, 1, 3):
            target = (z + o) % PAIRS
            its_rows, its_lanes = place(h, target, first_row, count)
            copy = remote(
                convolved.at[h, its_rows, its_lanes],
                back.at[h, pl.ds(first_row, count), lane_slice(z)],
                back_send.at[q, o - 1],
                back_recv.at[q, o - 1],
                (target, ch),
            )
            copy.start()
            copies.append(copy)
        mine_rows, mine_lanes = place(h, z, first_row, count)
        back[h, pl.ds(first_row, count), lane_slice(z)] = convolved[h, mine_rows, mine_lanes]
        pending.extend(copies)
        back_copies[q] = copies

    def convolve(h):
        products(h)
        high, low = summed_spec[0], summed_spec[1]
        result = dot(inverse[0], high) + dot(inverse[0], low) + dot(inverse[1], high)
        convolved[h] = result.astype(BF16)

    filter_spectra(0)
    key_spectra(0)
    key_copies[1] = scatter(1, gated, 1)
    keep(1, gated, 1)
    loads[5].wait()
    convolve(0)
    send_back(0)
    take_rim(1, 0)
    make_queries(0)
    take_rim(1, 1)
    make_queries(1)
    filter_spectra(1)
    early_products()
    key_spectra(1)
    convolve(1)
    send_back(1)
    send_back(2)
    loads[6].wait()
    loads[3].wait()

    steps = [(1, 1), (0, 1), (1, 0), (0, 0)]
    pair_copies = {}

    def parts(q):
        h, first_row, count = chunks[q]
        half = count // 2
        return slice(first_row, first_row + half), slice(first_row + half, first_row + count)

    def slot_rows(q):
        return pl.ds(chunks[q][1] // 2, chunks[q][2] // 2)

    def weights_for(step, cc):
        yy = 1 - y if step[0] else y
        xx = 1 - x if step[1] else x
        return weight[:, pl.ds(pl.multiple_of(ch_of(yy, xx, cc) * channels, channels), channels)]

    def project(q):
        h, first_row, count = chunks[q]
        span = slice(first_row, first_row + count)
        for copy in back_copies[q]:
            copy.wait_recv()
        for cols in columns:
            summed = back[h, span, cols].astype(F32) + skip_ref[:, cols] * gated[h, span, cols].astype(F32)
            act[h, span, cols] = (queries[h, span, cols] * summed).astype(BF16)
        rows_in = act[h, span]
        for t, step in enumerate(steps):
            pair_out[h, t, span] = dot(rows_in, weights_for(step, 1 - core)).astype(BF16)
            copy = remote(
                pair_out.at[h, t, pl.ds(first_row, count)],
                pair_in.at[h, t, pl.ds(first_row, count)],
                pair_send.at[q, t],
                pair_recv.at[q, t],
                partner,
            )
            copy.start()
            pair_copies[q, t] = copy
            pending.append(copy)

    def project_own(q, t):
        h, first_row, count = chunks[q]
        span = slice(first_row, first_row + count)
        own[h, t, span] = dot(act[h, span], weights_for(steps[t], core))

    first_copies, second_copies = {}, {}

    def pair_sum(q, t, way):
        h, part = chunks[q][0], parts(q)[way]
        return own[h, t, part] + pair_in[h, t, part].astype(F32)

    def first(q):
        h, where = chunks[q][0], slot_rows(q)
        for t, way, slot in ((0, 0, 0), (0, 1, 0), (1, 0, 1), (2, 1, 1)):
            if (t, way) != (0, 1):
                project_own(q, t)
                pair_copies[q, t].wait_recv()
            first_out[h, way, slot, where] = pair_sum(q, t, way).astype(BF16)
            copy = remote(
                first_out.at[h, way, slot, where],
                first_in.at[h, way, slot, where],
                first_send.at[q, way, slot],
                first_recv.at[q, way, slot],
                beside_y if way else beside_x,
            )
            copy.start()
            first_copies[q, way, slot] = copy
            pending.append(copy)
        project_own(q, 3)

    def second(q):
        h, where = chunks[q][0], slot_rows(q)
        for way in range(2):
            first_copies[q, way, 0].wait_recv()
            t = 1 if way else 2
            total = pair_sum(q, t, way) + first_in[h, way, 0, where].astype(F32)
            second_out[h, way, where] = total.astype(BF16)
            copy = remote(
                second_out.at[h, way, where],
                second_in.at[h, way, where],
                second_send.at[q, way],
                second_recv.at[q, way],
                beside_x if way else beside_y,
            )
            copy.start()
            second_copies[q, way] = copy
            pending.append(copy)

    def finish(q):
        h, where = chunks[q][0], slot_rows(q)
        pair_copies[q, 3].wait_recv()
        for way in range(2):
            first_copies[q, way, 1].wait_recv()
            total = pair_sum(q, 3, way) + first_in[h, way, 1, where].astype(F32)
            second_copies[q, way].wait_recv()
            out_ref[h, parts(q)[way]] = (total + second_in[h, way, where].astype(F32)).astype(BF16)

    project(0)
    first(0)
    project(1)
    first(1)
    project(2)
    second(0)
    first(2)
    second(1)
    finish(0)
    second(2)
    finish(1)
    finish(2)

    @pl.when(z < PAIRS - 1)
    def _():
        rims[0, 0].wait_send()
        rims[1, 0].wait_send()

    @pl.when(z > 0)
    def _():
        rims[0, 1].wait_send()
        rims[1, 1].wait_send()

    for copy in pending:
        copy.wait_send()


def fused(features, short_weight, long_filter, skip_gain, out_weight):
    rows, channels = long_filter.shape[2:]
    middle = 2 * rows
    streams = jnp.transpose(features[:, 0], (0, 2, 1, 3))
    taps = jnp.transpose(short_weight, (1, 0, 2))
    forward, inverse = odd_tables(middle)
    in_vmem = pl.BlockSpec(memory_space=pltpu.VMEM)
    in_hbm = pl.BlockSpec(memory_space=pl.ANY)
    vmem = pltpu.VMEM
    dma = pltpu.SemaphoreType.DMA
    out = pl.pallas_call(
        kernel,
        out_shape=pltpu.VMEM((2, rows, channels), BF16),
        in_specs=[in_hbm] * 7,
        out_specs=in_vmem,
        scratch_shapes=[
            vmem(streams.shape, BF16),
            vmem(taps.shape, BF16),
            vmem((2, rows, channels), BF16),
            vmem((1, channels), F32),
            vmem(out_weight.shape, BF16),
            vmem(forward.shape, BF16),
            vmem(inverse.shape, BF16),
            vmem((2, 2, 2 * RIM, channels), BF16),
            vmem((2, 2, 2 * RIM, channels), BF16),
            vmem((2, 3, RIM + rows, channels), F32),
            vmem((2, rows, channels), BF16),
            vmem((2, rows, channels), F32),
            vmem((2, 2, middle, 2 * LANES), BF16),
            vmem((2, middle, 2 * LANES), BF16),
            vmem((2, rows, channels), BF16),
            vmem((2, 4, 2 * middle, LANES), F32),
            vmem((4, 2 * middle, LANES), F32),
            vmem((2, 2 * middle, 2 * LANES), BF16),
            vmem((2, 2 * middle, LANES), F32),
            vmem((2, 4, rows, channels), F32),
            vmem((2, rows, channels), BF16),
            vmem((2, 4, rows, channels), BF16),
            vmem((2, 4, rows, channels), BF16),
            vmem((2, 2, 2, rows // 2, channels), BF16),
            vmem((2, 2, 2, rows // 2, channels), BF16),
            vmem((2, 2, rows // 2, channels), BF16),
            vmem((2, 2, rows // 2, channels), BF16),
            dma((7,)),
            dma((2, 2)),
            dma((2, 2)),
            dma((2, 2, 3)),
            dma((2, 2, 3)),
            dma((3, 3)),
            dma((3, 3)),
            dma((3, 4)),
            dma((3, 4)),
            dma((3, 2, 2)),
            dma((3, 2, 2)),
            dma((3, 2)),
            dma((3, 2)),
        ],
        compiler_params=pltpu.CompilerParams(
            collective_id=0, has_side_effects=True, vmem_limit_bytes=62 * 1024 * 1024
        ),
        name="hyena",
    )(
        streams,
        taps,
        long_filter[:, 0],
        skip_gain.reshape(1, channels),
        out_weight,
        jnp.asarray(forward),
        jnp.asarray(inverse),
    )
    return out[:, None]


def from_behind(value, axis, steps):
    count = lax.axis_size(axis)
    initial, last = (max(0, -steps), min(count, count - steps))
    return lax.ppermute(value, axis, [(source, source + steps) for source in range(initial, last)])


def transform_tables(length):
    period = 2 * length
    indices = jnp.arange(period, dtype=jnp.int32)
    phases = indices[:, None] * indices[None, :] % period
    angles = phases.astype(jnp.float32) * (2.0 * math.pi / period)
    cosine = jnp.cos(angles)
    sine_table = jnp.sin(angles)
    forward_full = jnp.concatenate([cosine, -sine_table], axis=0)
    forward_data = forward_full[:, :length]
    inverse = jnp.concatenate([cosine[:length], -sine_table[:length]], axis=1) / period
    return (forward_full, forward_data, inverse)


def complex_product(first, second):
    middle = first.shape[-2] // 2
    real_a = first[..., :middle, :]
    imag_a = first[..., middle:, :]
    real_b = second[..., :middle, :]
    imag_b = second[..., middle:, :]
    return jnp.concatenate(
        [real_a * real_b - imag_a * imag_b, real_a * imag_b + imag_a * real_b], axis=-2
    )


def featurize(tokens, before, kernel):
    extended = jnp.concatenate([before, tokens], axis=0).astype(jnp.float32)
    length = tokens.shape[0]
    margin_rows = kernel.shape[0] - 1
    summed = jnp.zeros(tokens.shape, jnp.float32)
    for offset in range(kernel.shape[0]):
        summed = (
            summed
            + kernel[offset].astype(jnp.float32)
            * extended[margin_rows - offset : margin_rows - offset + length]
        )
    return summed


def ordered(blocks):
    return jnp.concatenate([blocks[0], jnp.flip(blocks[1], axis=0)], axis=0)


def local(features, short_weight, long_filter, skip_gain, out_weight):
    pair_count = lax.axis_size("ctx")
    blocks_all = 2 * pair_count
    position = lax.axis_index("ctx")
    length = features.shape[2]
    margin_rows = short_weight.shape[0] - 1
    trailing = features[:, 0, length - margin_rows :]
    from_before = from_behind(trailing[0], "ctx", 1)
    from_after = from_behind(trailing[1], "ctx", -1)
    second_rim = jnp.where(position == pair_count - 1, trailing[0], from_after)
    first_feat = featurize(features[0, 0], from_before, short_weight)
    second_feat = featurize(features[1, 0], second_rim, short_weight)
    featured = jnp.stack([first_feat, second_feat], axis=0)
    queries = featured[:, :, 0]
    gated_keys = (featured[:, :, 1] * featured[:, :, 2]).astype(jnp.bfloat16)
    forward_full, forward_data, inverse = transform_tables(length)
    precise = lax.Precision.HIGHEST
    moved_gated, moved_filter = (
        lax.all_to_all(gated_keys[:, None], "ctx", split_axis=3, concat_axis=1, tiled=True),
        lax.all_to_all(long_filter, "ctx", split_axis=3, concat_axis=1, tiled=True),
    )
    ordered_gated = ordered(moved_gated).astype(jnp.float32)
    lag_order = ordered(moved_filter)
    padded = jnp.concatenate(
        [jnp.zeros((1,) + lag_order.shape[1:], lag_order.dtype), lag_order], axis=0
    )
    segments = jnp.concatenate([padded[1:], padded[:-1]], axis=1).astype(jnp.float32)
    responses = jnp.einsum("fm,kmc->kfc", forward_full, segments, precision=precise)
    spectra = jnp.einsum("fn,knc->kfc", forward_data, ordered_gated, precision=precise)
    sources = jnp.arange(blocks_all, dtype=jnp.int32)

    def one_target(target):
        distance = target - sources
        picked = jnp.take(responses, jnp.maximum(distance, 0), axis=0)
        products = complex_product(picked, spectra)
        summed = jnp.sum(jnp.where((distance >= 0)[:, None, None], products, 0.0), axis=0)
        return jnp.dot(inverse, summed, precision=precise)

    group_size = math.gcd(blocks_all, 8)
    grouped = sources.reshape(blocks_all // group_size, group_size)
    outputs = lax.map(jax.vmap(one_target), grouped).reshape(
        (blocks_all, length, responses.shape[-1])
    )
    blocks = jnp.stack([outputs[:pair_count], jnp.flip(outputs[pair_count:], axis=0)], axis=0)
    returned = lax.all_to_all(blocks, "ctx", split_axis=1, concat_axis=3, tiled=True)
    convolved = returned[:, 0]
    activated = (queries * (convolved + skip_gain * gated_keys.astype(jnp.float32))).astype(
        jnp.bfloat16
    )
    token_rows = activated.reshape(2 * length, activated.shape[-1])
    channels = token_rows.shape[1]
    owned = lax.psum_scatter(
        lax.dot_general(
            out_weight, token_rows, (((0,), (1,)), ((), ())), preferred_element_type=jnp.float32
        ).astype(jnp.bfloat16),
        "ch",
        scatter_dimension=0,
        tiled=True,
    ).astype(jnp.float32)
    result = owned.T
    return result.astype(jnp.bfloat16).reshape(2, 1, length, channels)


def solution(mesh):
    in_specs = (
        P(None, "ctx", None, None, "ch"),
        P(None, None, "ch"),
        P(None, "ctx", None, "ch"),
        P("ch"),
        P("ch", None),
    )
    out_specs = P(None, "ctx", None, "ch")
    shape = dict(mesh.shape)
    suits = shape == {"ctx": PAIRS, "ch": 8}
    body = fused if suits else local
    return jax.shard_map(body, mesh=mesh, in_specs=in_specs, out_specs=out_specs, check_vma=False)
```

```python
import math

import jax
import jax.numpy as jnp
import ml_dtypes
import numpy as np
from jax import lax
from jax.experimental import pallas as pl
from jax.experimental.pallas import tpu as pltpu
from jax.sharding import PartitionSpec as P

F32 = jnp.float32
BF16 = jnp.bfloat16
MESH = pl.DeviceIdType.MESH
RIM = 8
STRIP = 64
LANES = 128
PAIRS = 4


def halves(values):
    high = values.astype(ml_dtypes.bfloat16)
    low = (values - high.astype(np.float64)).astype(ml_dtypes.bfloat16)
    return np.stack([high, low])


def odd_tables(length):
    k = np.arange(length)[:, None]
    t = np.arange(length)[None, :]
    angles = ((2 * k + 1) * t % (4 * length)) * (np.pi / (2 * length))
    forward = np.concatenate([np.cos(angles), -np.sin(angles)], axis=0)
    return halves(forward), halves(forward.T / length)


def dot(a, b):
    return jnp.dot(a, b, preferred_element_type=F32)


def kernel(
    x_hbm,
    taps_hbm,
    filter_hbm,
    skip_hbm,
    weight_hbm,
    forward_hbm,
    inverse_hbm,
    out_ref,
    x_ref,
    taps_ref,
    filter_ref,
    skip_ref,
    weight,
    forward,
    inverse,
    rim_out,
    halo,
    wide,
    gated,
    queries,
    moved,
    convolved,
    back,
    filter_spec,
    key_spec,
    summed_spec,
    early,
    own,
    act,
    pair_out,
    pair_in,
    first_out,
    first_in,
    second_out,
    second_in,
    local_sem,
    filter_sem,
    halo_send,
    halo_recv,
    move_send,
    move_recv,
    back_send,
    back_recv,
    pair_send,
    pair_recv,
    first_send,
    first_recv,
    second_send,
    second_recv,
):
    rows = gated.shape[2]
    channels = weight.shape[0]
    taps = taps_ref.shape[1]
    middle = forward.shape[2]
    z = lax.axis_index("ctx")
    ch = lax.axis_index("ch")
    core, x, y = ch % 2, ch // 2 % 2, ch // 4

    def ch_of(yy, xx, cc):
        return yy * 4 + xx * 2 + cc

    partner = (z, ch_of(y, x, 1 - core))
    beside_x = (z, ch_of(y, 1 - x, core))
    beside_y = (z, ch_of(1 - y, x, core))

    sources = (x_hbm, taps_hbm, skip_hbm, forward_hbm, inverse_hbm, weight_hbm)
    places = (x_ref, taps_ref, skip_ref, forward, inverse, weight)
    loads = [
        pltpu.make_async_copy(source, target, local_sem.at[i])
        for i, (source, target) in enumerate(zip(sources, places))
    ]
    filter_loads = [
        pltpu.make_async_copy(
            filter_hbm.at[h, :, pl.ds(c * LANES, LANES)], filter_ref.at[h, c], filter_sem.at[h, c]
        )
        for h in range(2)
        for c in range(channels // LANES)
    ]
    for load in (loads[0], *filter_loads, loads[1], loads[2]):
        load.start()

    barrier = pltpu.get_barrier_semaphore()
    peers = [((z + o) % PAIRS, ch) for o in range(1, PAIRS)] + [partner, beside_x, beside_y]
    for peer in peers:
        pl.semaphore_signal(barrier, inc=1, device_id=peer, device_id_type=MESH)
    pl.semaphore_wait(barrier, len(peers))

    for load in loads[3:]:
        load.start()
    pending = []

    def remote(src, dst, send, recv, device):
        return pltpu.make_async_remote_copy(
            src_ref=src, dst_ref=dst, send_sem=send, recv_sem=recv, device_id=device, device_id_type=MESH
        )

    def keep(kind, source, h):
        moved[kind, h, block_of(h, z)] = source[h, z]

    def block_of(h, owner):
        return owner if h == 0 else PAIRS - 1 - owner

    def scatter(kind, source, h):
        copies = []
        for o in (2, 1, 3):
            target = (z + o) % PAIRS
            copy = remote(
                source.at[h, target],
                moved.at[kind, h, block_of(h, z)],
                move_send.at[kind, h, o - 1],
                move_recv.at[kind, h, o - 1],
                (target, ch),
            )
            copy.start()
            copies.append(copy)
        pending.extend(copies)
        return copies

    filter_copies, key_copies = [None, None], [None, None]
    loads[0].wait()

    def widen(h):
        for s in range(3):
            wide[h, s, RIM:] = x_ref[h, s].astype(F32)

    tails = [[x_ref[h, s, rows - 2 * RIM :].astype(F32)[RIM:] for s in range(3)] for h in range(2)]
    rims = {}
    for kind, streams in ((0, (1, 2)), (1, (0, 0))):
        for h in range(2):
            rim_out[kind, h] = jnp.concatenate([tails[h][s] for s in streams], axis=0).astype(BF16)
            rims[kind, h] = remote(
                rim_out.at[kind, h],
                halo.at[kind, h],
                halo_send.at[kind, h],
                halo_recv.at[kind, h],
                ((z + (1 if h == 0 else 3)) % PAIRS, ch),
            )

    def send_rims(kind):
        @pl.when(z < PAIRS - 1)
        def _():
            rims[kind, 0].start()

        @pl.when(z > 0)
        def _():
            rims[kind, 1].start()

    def take_rim(kind, h):
        has = z > 0 if h == 0 else z < PAIRS - 1

        @pl.when(has)
        def _():
            rims[kind, h].wait_recv()

        @pl.when(jnp.logical_not(has))
        def _():
            halo[kind, h] = jnp.zeros(halo.shape[2:], BF16) if h == 0 else rim_out[kind, 0]

        both = halo[kind, h].astype(F32)
        for m, s in enumerate((1, 2) if kind == 0 else (0,)):
            wide[h, s, :RIM] = both[m * RIM : (m + 1) * RIM]

    send_rims(0)
    for load in filter_loads:
        load.wait()
    filter_copies[0] = scatter(0, filter_ref, 0)
    widen(0)
    widen(1)

    loads[1].wait()
    tap_rows = [taps_ref[s].astype(F32) for s in range(3)]

    def taps_of(h, s, cols):
        total = None
        for i in range(taps):
            tap = tap_rows[s][i : i + 1, cols]
            term = tap * wide[h, s, pl.ds(RIM - i, rows), cols]
            total = term if total is None else total + term
        return total

    columns = [slice(a, a + LANES) for a in range(0, channels, LANES)]

    def make_keys(h):
        for c, cols in enumerate(columns):
            gated[h, c] = (taps_of(h, 1, cols) * taps_of(h, 2, cols)).astype(BF16)

    def make_queries(h):
        for cols in columns:
            queries[h, :, cols] = taps_of(h, 0, cols)

    take_rim(0, 0)
    make_keys(0)
    key_copies[0] = scatter(1, gated, 0)
    keep(1, gated, 0)
    send_rims(1)
    filter_copies[1] = scatter(0, filter_ref, 1)
    keep(0, filter_ref, 0)
    keep(0, filter_ref, 1)
    take_rim(0, 1)
    make_keys(1)
    loads[3].wait()

    signs = (1 - 2 * (lax.broadcasted_iota(jnp.int32, (middle, LANES), 0) % 2)).astype(F32)

    def spectrum(kind, h):
        data = jnp.concatenate(
            [jnp.concatenate([moved[kind, h, 2 * m], moved[kind, h, 2 * m + 1]], axis=0) for m in range(2)], axis=1
        )
        return dot(forward[0], data) + dot(forward[1], data)

    def filter_spectra(h):
        for copy in filter_copies[h]:
            copy.wait_recv()
        both = spectrum(0, h)
        for m in range(2):
            filter_spec[0, 2 * h + m] = both[:, m * LANES : (m + 1) * LANES]
        for b in (2 * h, 2 * h + 1):
            if b == 0:
                filter_spec[1, 0] = filter_spec[0, 0]
            else:
                filter_spec[1, b, :middle] = filter_spec[0, b, :middle] - signs * filter_spec[0, b - 1, middle:]
                filter_spec[1, b, middle:] = filter_spec[0, b, middle:] + signs * filter_spec[0, b - 1, :middle]

    def key_spectra(h):
        for copy in key_copies[h]:
            copy.wait_recv()
        both = spectrum(1, h)
        for m in range(2):
            key_spec[2 * h + m] = both[:, m * LANES : (m + 1) * LANES]

    def pair_products(i, sources, re_rows, im_rows):
        real, imag = None, None
        for j in sources:
            ra, ia = filter_spec[1, i - j, re_rows], filter_spec[1, i - j, im_rows]
            rb, ib = key_spec[j, re_rows], key_spec[j, im_rows]
            re, im = ra * rb - ia * ib, ra * ib + ia * rb
            real = re if real is None else real + re
            imag = im if imag is None else imag + im
        return real, imag

    strips = [
        (slice(start, start + STRIP), slice(middle + start, middle + start + STRIP))
        for start in range(0, middle, STRIP)
    ]

    def early_products():
        for m in range(2):
            for re_rows, im_rows in strips:
                early[m, re_rows], early[m, im_rows] = pair_products(2 + m, (0, 1), re_rows, im_rows)

    def products(h):
        for m in range(2):
            i = 2 * h + m
            cols = slice(m * LANES, (m + 1) * LANES)
            for re_rows, im_rows in strips:
                sums = pair_products(i, range(2 * h, i + 1), re_rows, im_rows)
                for where, value in zip((re_rows, im_rows), sums):
                    if h == 1:
                        value = value + early[m, where]
                    high = value.astype(BF16)
                    summed_spec[0, where, cols] = high
                    summed_spec[1, where, cols] = (value - high.astype(F32)).astype(BF16)

    chunks = [(0, 0, rows), (1, 0, rows // 2), (1, rows // 2, rows // 2)]
    back_copies = {}

    def send_back(q):
        h, first_row, count = chunks[q]
        copies = []
        for o in (2, 1, 3):
            target = (z + o) % PAIRS
            copy = remote(
                convolved.at[h, block_of(h, target), pl.ds(first_row, count)],
                back.at[h, z, pl.ds(first_row, count)],
                back_send.at[q, o - 1],
                back_recv.at[q, o - 1],
                (target, ch),
            )
            copy.start()
            copies.append(copy)
        back[h, z, pl.ds(first_row, count)] = convolved[h, block_of(h, z), pl.ds(first_row, count)]
        pending.extend(copies)
        back_copies[q] = copies

    def convolve(h):
        products(h)
        high, low = summed_spec[0], summed_spec[1]
        result = dot(inverse[0], high) + dot(inverse[0], low) + dot(inverse[1], high)
        result = result.astype(BF16)
        for block in range(PAIRS):
            m, part = divmod(block, 2)
            convolved[h, block] = result[part * rows : (part + 1) * rows, m * LANES : (m + 1) * LANES]

    filter_spectra(0)
    key_spectra(0)
    loads[4].wait()
    convolve(0)
    send_back(0)
    key_copies[1] = scatter(1, gated, 1)
    keep(1, gated, 1)
    take_rim(1, 0)
    make_queries(0)
    take_rim(1, 1)
    make_queries(1)
    filter_spectra(1)
    early_products()
    key_spectra(1)
    convolve(1)
    send_back(1)
    send_back(2)
    loads[5].wait()
    loads[2].wait()

    steps = [(1, 1), (0, 1), (1, 0), (0, 0)]
    pair_copies = {}

    def parts(q):
        h, first_row, count = chunks[q]
        half = count // 2
        return slice(first_row, first_row + half), slice(first_row + half, first_row + count)

    def slot_rows(q):
        return pl.ds(chunks[q][1] // 2, chunks[q][2] // 2)

    def weights_for(step, cc):
        yy = 1 - y if step[0] else y
        xx = 1 - x if step[1] else x
        return weight[:, pl.ds(pl.multiple_of(ch_of(yy, xx, cc) * channels, channels), channels)]

    def project(q):
        h, first_row, count = chunks[q]
        span = slice(first_row, first_row + count)
        for copy in back_copies[q]:
            copy.wait_recv()
        for c, cols in enumerate(columns):
            summed = back[h, c, span].astype(F32) + skip_ref[:, cols] * gated[h, c, span].astype(F32)
            act[h, span, cols] = (queries[h, span, cols] * summed).astype(BF16)
        rows_in = act[h, span]
        for t, step in enumerate(steps):
            pair_out[h, t, span] = dot(rows_in, weights_for(step, 1 - core)).astype(BF16)
            copy = remote(
                pair_out.at[h, t, pl.ds(first_row, count)],
                pair_in.at[h, t, pl.ds(first_row, count)],
                pair_send.at[q, t],
                pair_recv.at[q, t],
                partner,
            )
            copy.start()
            pair_copies[q, t] = copy
            pending.append(copy)

    def project_own(q, t):
        h, first_row, count = chunks[q]
        span = slice(first_row, first_row + count)
        own[h, t, span] = dot(act[h, span], weights_for(steps[t], core))

    first_copies, second_copies = {}, {}

    def pair_sum(q, t, way):
        h, part = chunks[q][0], parts(q)[way]
        return own[h, t, part] + pair_in[h, t, part].astype(F32)

    def first(q):
        h, where = chunks[q][0], slot_rows(q)
        for t, way, slot in ((0, 0, 0), (0, 1, 0), (1, 0, 1), (2, 1, 1)):
            if (t, way) != (0, 1):
                project_own(q, t)
                pair_copies[q, t].wait_recv()
            first_out[h, way, slot, where] = pair_sum(q, t, way).astype(BF16)
            copy = remote(
                first_out.at[h, way, slot, where],
                first_in.at[h, way, slot, where],
                first_send.at[q, way, slot],
                first_recv.at[q, way, slot],
                beside_y if way else beside_x,
            )
            copy.start()
            first_copies[q, way, slot] = copy
            pending.append(copy)
        project_own(q, 3)

    def second(q):
        h, where = chunks[q][0], slot_rows(q)
        for way in range(2):
            first_copies[q, way, 0].wait_recv()
            t = 1 if way else 2
            total = pair_sum(q, t, way) + first_in[h, way, 0, where].astype(F32)
            second_out[h, way, where] = total.astype(BF16)
            copy = remote(
                second_out.at[h, way, where],
                second_in.at[h, way, where],
                second_send.at[q, way],
                second_recv.at[q, way],
                beside_x if way else beside_y,
            )
            copy.start()
            second_copies[q, way] = copy
            pending.append(copy)

    def finish(q):
        h, where = chunks[q][0], slot_rows(q)
        pair_copies[q, 3].wait_recv()
        for way in range(2):
            first_copies[q, way, 1].wait_recv()
            total = pair_sum(q, 3, way) + first_in[h, way, 1, where].astype(F32)
            second_copies[q, way].wait_recv()
            out_ref[h, parts(q)[way]] = (total + second_in[h, way, where].astype(F32)).astype(BF16)

    project(0)
    first(0)
    project(1)
    first(1)
    project(2)
    second(0)
    first(2)
    second(1)
    finish(0)
    second(2)
    finish(1)
    finish(2)

    @pl.when(z < PAIRS - 1)
    def _():
        rims[0, 0].wait_send()
        rims[1, 0].wait_send()

    @pl.when(z > 0)
    def _():
        rims[0, 1].wait_send()
        rims[1, 1].wait_send()

    for copy in pending:
        copy.wait_send()


def fused(features, short_weight, long_filter, skip_gain, out_weight):
    rows, channels = long_filter.shape[2:]
    middle = 2 * rows
    streams = jnp.transpose(features[:, 0], (0, 2, 1, 3))
    taps = jnp.transpose(short_weight, (1, 0, 2))
    forward, inverse = odd_tables(middle)
    blocked = (2, channels // LANES, rows, LANES)
    in_vmem = pl.BlockSpec(memory_space=pltpu.VMEM)
    in_hbm = pl.BlockSpec(memory_space=pl.ANY)
    vmem = pltpu.VMEM
    dma = pltpu.SemaphoreType.DMA
    out = pl.pallas_call(
        kernel,
        out_shape=pltpu.VMEM((2, rows, channels), BF16),
        in_specs=[in_hbm] * 7,
        out_specs=in_vmem,
        scratch_shapes=[
            vmem(streams.shape, BF16),
            vmem(taps.shape, BF16),
            vmem(blocked, BF16),
            vmem((1, channels), F32),
            vmem(out_weight.shape, BF16),
            vmem(forward.shape, BF16),
            vmem(inverse.shape, BF16),
            vmem((2, 2, 2 * RIM, channels), BF16),
            vmem((2, 2, 2 * RIM, channels), BF16),
            vmem((2, 3, RIM + rows, channels), F32),
            vmem(blocked, BF16),
            vmem((2, rows, channels), F32),
            vmem((2, *blocked), BF16),
            vmem(blocked, BF16),
            vmem(blocked, BF16),
            vmem((2, 4, 2 * middle, LANES), F32),
            vmem((4, 2 * middle, LANES), F32),
            vmem((2, 2 * middle, 2 * LANES), BF16),
            vmem((2, 2 * middle, LANES), F32),
            vmem((2, 4, rows, channels), F32),
            vmem((2, rows, channels), BF16),
            vmem((2, 4, rows, channels), BF16),
            vmem((2, 4, rows, channels), BF16),
            vmem((2, 2, 2, rows // 2, channels), BF16),
            vmem((2, 2, 2, rows // 2, channels), BF16),
            vmem((2, 2, rows // 2, channels), BF16),
            vmem((2, 2, rows // 2, channels), BF16),
            dma((6,)),
            dma((2, channels // LANES)),
            dma((2, 2)),
            dma((2, 2)),
            dma((2, 2, 3)),
            dma((2, 2, 3)),
            dma((3, 3)),
            dma((3, 3)),
            dma((3, 4)),
            dma((3, 4)),
            dma((3, 2, 2)),
            dma((3, 2, 2)),
            dma((3, 2)),
            dma((3, 2)),
        ],
        compiler_params=pltpu.CompilerParams(
            collective_id=0, has_side_effects=True, vmem_limit_bytes=62 * 1024 * 1024
        ),
        name="hyena",
    )(
        streams,
        taps,
        long_filter[:, 0],
        skip_gain.reshape(1, channels),
        out_weight,
        jnp.asarray(forward),
        jnp.asarray(inverse),
    )
    return out[:, None]


def from_behind(value, axis, steps):
    count = lax.axis_size(axis)
    initial, last = (max(0, -steps), min(count, count - steps))
    return lax.ppermute(value, axis, [(source, source + steps) for source in range(initial, last)])


def transform_tables(length):
    period = 2 * length
    indices = jnp.arange(period, dtype=jnp.int32)
    phases = indices[:, None] * indices[None, :] % period
    angles = phases.astype(jnp.float32) * (2.0 * math.pi / period)
    cosine = jnp.cos(angles)
    sine_table = jnp.sin(angles)
    forward_full = jnp.concatenate([cosine, -sine_table], axis=0)
    forward_data = forward_full[:, :length]
    inverse = jnp.concatenate([cosine[:length], -sine_table[:length]], axis=1) / period
    return (forward_full, forward_data, inverse)


def complex_product(first, second):
    middle = first.shape[-2] // 2
    real_a = first[..., :middle, :]
    imag_a = first[..., middle:, :]
    real_b = second[..., :middle, :]
    imag_b = second[..., middle:, :]
    return jnp.concatenate(
        [real_a * real_b - imag_a * imag_b, real_a * imag_b + imag_a * real_b], axis=-2
    )


def featurize(tokens, before, kernel):
    extended = jnp.concatenate([before, tokens], axis=0).astype(jnp.float32)
    length = tokens.shape[0]
    margin_rows = kernel.shape[0] - 1
    summed = jnp.zeros(tokens.shape, jnp.float32)
    for offset in range(kernel.shape[0]):
        summed = (
            summed
            + kernel[offset].astype(jnp.float32)
            * extended[margin_rows - offset : margin_rows - offset + length]
        )
    return summed


def ordered(blocks):
    return jnp.concatenate([blocks[0], jnp.flip(blocks[1], axis=0)], axis=0)


def local(features, short_weight, long_filter, skip_gain, out_weight):
    pair_count = lax.axis_size("ctx")
    blocks_all = 2 * pair_count
    position = lax.axis_index("ctx")
    length = features.shape[2]
    margin_rows = short_weight.shape[0] - 1
    trailing = features[:, 0, length - margin_rows :]
    from_before = from_behind(trailing[0], "ctx", 1)
    from_after = from_behind(trailing[1], "ctx", -1)
    second_rim = jnp.where(position == pair_count - 1, trailing[0], from_after)
    first_feat = featurize(features[0, 0], from_before, short_weight)
    second_feat = featurize(features[1, 0], second_rim, short_weight)
    featured = jnp.stack([first_feat, second_feat], axis=0)
    queries = featured[:, :, 0]
    gated_keys = (featured[:, :, 1] * featured[:, :, 2]).astype(jnp.bfloat16)
    forward_full, forward_data, inverse = transform_tables(length)
    precise = lax.Precision.HIGHEST
    moved_gated, moved_filter = (
        lax.all_to_all(gated_keys[:, None], "ctx", split_axis=3, concat_axis=1, tiled=True),
        lax.all_to_all(long_filter, "ctx", split_axis=3, concat_axis=1, tiled=True),
    )
    ordered_gated = ordered(moved_gated).astype(jnp.float32)
    lag_order = ordered(moved_filter)
    padded = jnp.concatenate(
        [jnp.zeros((1,) + lag_order.shape[1:], lag_order.dtype), lag_order], axis=0
    )
    segments = jnp.concatenate([padded[1:], padded[:-1]], axis=1).astype(jnp.float32)
    responses = jnp.einsum("fm,kmc->kfc", forward_full, segments, precision=precise)
    spectra = jnp.einsum("fn,knc->kfc", forward_data, ordered_gated, precision=precise)
    sources = jnp.arange(blocks_all, dtype=jnp.int32)

    def one_target(target):
        distance = target - sources
        picked = jnp.take(responses, jnp.maximum(distance, 0), axis=0)
        products = complex_product(picked, spectra)
        summed = jnp.sum(jnp.where((distance >= 0)[:, None, None], products, 0.0), axis=0)
        return jnp.dot(inverse, summed, precision=precise)

    group_size = math.gcd(blocks_all, 8)
    grouped = sources.reshape(blocks_all // group_size, group_size)
    outputs = lax.map(jax.vmap(one_target), grouped).reshape(
        (blocks_all, length, responses.shape[-1])
    )
    blocks = jnp.stack([outputs[:pair_count], jnp.flip(outputs[pair_count:], axis=0)], axis=0)
    returned = lax.all_to_all(blocks, "ctx", split_axis=1, concat_axis=3, tiled=True)
    convolved = returned[:, 0]
    activated = (queries * (convolved + skip_gain * gated_keys.astype(jnp.float32))).astype(
        jnp.bfloat16
    )
    token_rows = activated.reshape(2 * length, activated.shape[-1])
    channels = token_rows.shape[1]
    owned = lax.psum_scatter(
        lax.dot_general(
            out_weight, token_rows, (((0,), (1,)), ((), ())), preferred_element_type=jnp.float32
        ).astype(jnp.bfloat16),
        "ch",
        scatter_dimension=0,
        tiled=True,
    ).astype(jnp.float32)
    result = owned.T
    return result.astype(jnp.bfloat16).reshape(2, 1, length, channels)


def solution(mesh):
    in_specs = (
        P(None, "ctx", None, None, "ch"),
        P(None, None, "ch"),
        P(None, "ctx", None, "ch"),
        P("ch"),
        P("ch", None),
    )
    out_specs = P(None, "ctx", None, "ch")
    shape = dict(mesh.shape)
    suits = shape == {"ctx": PAIRS, "ch": 8}
    body = fused if suits else local
    return jax.shard_map(body, mesh=mesh, in_specs=in_specs, out_specs=out_specs, check_vma=False)
```

```python
import math

import jax
import jax.numpy as jnp
import ml_dtypes
import numpy as np
from jax import lax
from jax.experimental import pallas as pl
from jax.experimental.pallas import tpu as pltpu
from jax.sharding import PartitionSpec as P

F32 = jnp.float32
BF16 = jnp.bfloat16
MESH = pl.DeviceIdType.MESH
RIM = 8
STRIP = 64
LANES = 128
PAIRS = 4


def halves(values):
    high = values.astype(ml_dtypes.bfloat16)
    low = (values - high.astype(np.float64)).astype(ml_dtypes.bfloat16)
    return np.stack([high, low])


def odd_tables(length):
    k = np.arange(length)[:, None]
    t = np.arange(length)[None, :]
    angles = ((2 * k + 1) * t % (4 * length)) * (np.pi / (2 * length))
    forward = np.concatenate([np.cos(angles), -np.sin(angles)], axis=0)
    return halves(forward), halves(forward.T / length)


def dot(a, b):
    return jnp.dot(a, b, preferred_element_type=F32)


def kernel(
    x_hbm,
    taps_hbm,
    filter_hbm,
    skip_hbm,
    weight_hbm,
    forward_hbm,
    inverse_hbm,
    out_ref,
    x_ref,
    taps_ref,
    filter_ref,
    skip_ref,
    weight,
    forward,
    inverse,
    rim_out,
    halo,
    wide,
    gated,
    queries,
    moved,
    convolved,
    back,
    filter_spec,
    key_spec,
    summed_spec,
    early,
    own,
    act,
    pair_out,
    pair_in,
    first_out,
    first_in,
    second_out,
    second_in,
    local_sem,
    filter_sem,
    halo_send,
    halo_recv,
    move_send,
    move_recv,
    back_send,
    back_recv,
    pair_send,
    pair_recv,
    first_send,
    first_recv,
    second_send,
    second_recv,
):
    rows = gated.shape[2]
    channels = weight.shape[0]
    taps = taps_ref.shape[1]
    middle = forward.shape[2]
    z = lax.axis_index("ctx")
    ch = lax.axis_index("ch")
    core, x, y = ch % 2, ch // 2 % 2, ch // 4

    def ch_of(yy, xx, cc):
        return yy * 4 + xx * 2 + cc

    partner = (z, ch_of(y, x, 1 - core))
    beside_x = (z, ch_of(y, 1 - x, core))
    beside_y = (z, ch_of(1 - y, x, core))

    sources = (x_hbm, taps_hbm, skip_hbm, forward_hbm, inverse_hbm, weight_hbm)
    places = (x_ref, taps_ref, skip_ref, forward, inverse, weight)
    loads = [
        pltpu.make_async_copy(source, target, local_sem.at[i])
        for i, (source, target) in enumerate(zip(sources, places))
    ]
    filter_loads = [
        pltpu.make_async_copy(
            filter_hbm.at[h, :, pl.ds(c * LANES, LANES)], filter_ref.at[h, c], filter_sem.at[h, c]
        )
        for h in range(2)
        for c in range(channels // LANES)
    ]
    for load in (loads[0], *filter_loads, loads[1], loads[2]):
        load.start()

    barrier = pltpu.get_barrier_semaphore()
    peers = [((z + o) % PAIRS, ch) for o in range(1, PAIRS)] + [partner, beside_x, beside_y]
    for peer in peers:
        pl.semaphore_signal(barrier, inc=1, device_id=peer, device_id_type=MESH)
    pl.semaphore_wait(barrier, len(peers))

    for load in loads[3:]:
        load.start()
    pending = []

    def remote(src, dst, send, recv, device):
        return pltpu.make_async_remote_copy(
            src_ref=src, dst_ref=dst, send_sem=send, recv_sem=recv, device_id=device, device_id_type=MESH
        )

    def keep(kind, source, h):
        moved[kind, h, block_of(h, z)] = source[h, z]

    def block_of(h, owner):
        return owner if h == 0 else PAIRS - 1 - owner

    def scatter(kind, source, h):
        copies = []
        for o in (2, 1, 3):
            target = (z + o) % PAIRS
            copy = remote(
                source.at[h, target],
                moved.at[kind, h, block_of(h, z)],
                move_send.at[kind, h, o - 1],
                move_recv.at[kind, h, o - 1],
                (target, ch),
            )
            copy.start()
            copies.append(copy)
        pending.extend(copies)
        return copies

    filter_copies, key_copies = [None, None], [None, None]
    loads[0].wait()

    def widen(h):
        for s in range(3):
            wide[h, s, RIM:] = x_ref[h, s].astype(F32)

    tails = [[x_ref[h, s, rows - 2 * RIM :].astype(F32)[RIM:] for s in range(3)] for h in range(2)]
    rims = {}
    for kind, streams in ((0, (1, 2)), (1, (0, 0))):
        for h in range(2):
            rim_out[kind, h] = jnp.concatenate([tails[h][s] for s in streams], axis=0).astype(BF16)
            rims[kind, h] = remote(
                rim_out.at[kind, h],
                halo.at[kind, h],
                halo_send.at[kind, h],
                halo_recv.at[kind, h],
                ((z + (1 if h == 0 else 3)) % PAIRS, ch),
            )

    def send_rims(kind):
        @pl.when(z < PAIRS - 1)
        def _():
            rims[kind, 0].start()

        @pl.when(z > 0)
        def _():
            rims[kind, 1].start()

    def take_rim(kind, h):
        has = z > 0 if h == 0 else z < PAIRS - 1

        @pl.when(has)
        def _():
            rims[kind, h].wait_recv()

        @pl.when(jnp.logical_not(has))
        def _():
            halo[kind, h] = jnp.zeros(halo.shape[2:], BF16) if h == 0 else rim_out[kind, 0]

        both = halo[kind, h].astype(F32)
        for m, s in enumerate((1, 2) if kind == 0 else (0,)):
            wide[h, s, :RIM] = both[m * RIM : (m + 1) * RIM]

    send_rims(0)
    for load in filter_loads:
        load.wait()
    filter_copies[0] = scatter(0, filter_ref, 0)
    widen(0)
    widen(1)

    loads[1].wait()
    tap_rows = [taps_ref[s].astype(F32) for s in range(3)]

    def taps_of(h, s, cols):
        total = None
        for i in range(taps):
            tap = tap_rows[s][i : i + 1, cols]
            term = tap * wide[h, s, pl.ds(RIM - i, rows), cols]
            total = term if total is None else total + term
        return total

    columns = [slice(a, a + LANES) for a in range(0, channels, LANES)]

    def make_keys(h):
        for c, cols in enumerate(columns):
            gated[h, c] = (taps_of(h, 1, cols) * taps_of(h, 2, cols)).astype(BF16)

    def make_queries(h):
        for cols in columns:
            queries[h, :, cols] = taps_of(h, 0, cols)

    take_rim(0, 0)
    make_keys(0)
    key_copies[0] = scatter(1, gated, 0)
    keep(1, gated, 0)
    send_rims(1)
    filter_copies[1] = scatter(0, filter_ref, 1)
    keep(0, filter_ref, 0)
    keep(0, filter_ref, 1)
    take_rim(0, 1)
    make_keys(1)
    key_copies[1] = scatter(1, gated, 1)
    keep(1, gated, 1)
    loads[3].wait()

    signs = (1 - 2 * (lax.broadcasted_iota(jnp.int32, (middle, LANES), 0) % 2)).astype(F32)

    def spectrum(kind, h):
        data = jnp.concatenate(
            [jnp.concatenate([moved[kind, h, 2 * m], moved[kind, h, 2 * m + 1]], axis=0) for m in range(2)], axis=1
        )
        return dot(forward[0], data) + dot(forward[1], data)

    def filter_spectra(h):
        for copy in filter_copies[h]:
            copy.wait_recv()
        both = spectrum(0, h)
        for m in range(2):
            filter_spec[0, 2 * h + m] = both[:, m * LANES : (m + 1) * LANES]
        for b in (2 * h, 2 * h + 1):
            if b == 0:
                filter_spec[1, 0] = filter_spec[0, 0]
            else:
                filter_spec[1, b, :middle] = filter_spec[0, b, :middle] - signs * filter_spec[0, b - 1, middle:]
                filter_spec[1, b, middle:] = filter_spec[0, b, middle:] + signs * filter_spec[0, b - 1, :middle]

    def key_spectra(h):
        for copy in key_copies[h]:
            copy.wait_recv()
        both = spectrum(1, h)
        for m in range(2):
            key_spec[2 * h + m] = both[:, m * LANES : (m + 1) * LANES]

    def pair_products(i, sources, re_rows, im_rows):
        real, imag = None, None
        for j in sources:
            ra, ia = filter_spec[1, i - j, re_rows], filter_spec[1, i - j, im_rows]
            rb, ib = key_spec[j, re_rows], key_spec[j, im_rows]
            re, im = ra * rb - ia * ib, ra * ib + ia * rb
            real = re if real is None else real + re
            imag = im if imag is None else imag + im
        return real, imag

    strips = [
        (slice(start, start + STRIP), slice(middle + start, middle + start + STRIP))
        for start in range(0, middle, STRIP)
    ]

    def early_products():
        for m in range(2):
            for re_rows, im_rows in strips:
                early[m, re_rows], early[m, im_rows] = pair_products(2 + m, (0, 1), re_rows, im_rows)

    def products(h):
        for m in range(2):
            i = 2 * h + m
            cols = slice(m * LANES, (m + 1) * LANES)
            for re_rows, im_rows in strips:
                sums = pair_products(i, range(2 * h, i + 1), re_rows, im_rows)
                for where, value in zip((re_rows, im_rows), sums):
                    if h == 1:
                        value = value + early[m, where]
                    high = value.astype(BF16)
                    summed_spec[0, where, cols] = high
                    summed_spec[1, where, cols] = (value - high.astype(F32)).astype(BF16)

    chunks = [(0, 0, rows), (1, 0, rows // 2), (1, rows // 2, rows // 2)]
    back_copies = {}

    def send_back(q):
        h, first_row, count = chunks[q]
        copies = []
        for o in (2, 1, 3):
            target = (z + o) % PAIRS
            copy = remote(
                convolved.at[h, block_of(h, target), pl.ds(first_row, count)],
                back.at[h, z, pl.ds(first_row, count)],
                back_send.at[q, o - 1],
                back_recv.at[q, o - 1],
                (target, ch),
            )
            copy.start()
            copies.append(copy)
        back[h, z, pl.ds(first_row, count)] = convolved[h, block_of(h, z), pl.ds(first_row, count)]
        pending.extend(copies)
        back_copies[q] = copies

    def convolve(h):
        products(h)
        high, low = summed_spec[0], summed_spec[1]
        result = dot(inverse[0], high) + dot(inverse[0], low) + dot(inverse[1], high)
        result = result.astype(BF16)
        for block in range(PAIRS):
            m, part = divmod(block, 2)
            convolved[h, block] = result[part * rows : (part + 1) * rows, m * LANES : (m + 1) * LANES]

    filter_spectra(0)
    key_spectra(0)
    loads[4].wait()
    convolve(0)
    send_back(0)
    take_rim(1, 0)
    make_queries(0)
    take_rim(1, 1)
    make_queries(1)
    filter_spectra(1)
    early_products()
    key_spectra(1)
    convolve(1)
    send_back(1)
    send_back(2)
    loads[5].wait()
    loads[2].wait()

    steps = [(1, 1), (0, 1), (1, 0), (0, 0)]
    pair_copies = {}

    def parts(q):
        h, first_row, count = chunks[q]
        half = count // 2
        return slice(first_row, first_row + half), slice(first_row + half, first_row + count)

    def slot_rows(q):
        return pl.ds(chunks[q][1] // 2, chunks[q][2] // 2)

    def weights_for(step, cc):
        yy = 1 - y if step[0] else y
        xx = 1 - x if step[1] else x
        return weight[:, pl.ds(pl.multiple_of(ch_of(yy, xx, cc) * channels, channels), channels)]

    def project(q):
        h, first_row, count = chunks[q]
        span = slice(first_row, first_row + count)
        for copy in back_copies[q]:
            copy.wait_recv()
        for c, cols in enumerate(columns):
            summed = back[h, c, span].astype(F32) + skip_ref[:, cols] * gated[h, c, span].astype(F32)
            act[h, span, cols] = (queries[h, span, cols] * summed).astype(BF16)
        rows_in = act[h, span]
        for t, step in enumerate(steps):
            pair_out[h, t, span] = dot(rows_in, weights_for(step, 1 - core)).astype(BF16)
            copy = remote(
                pair_out.at[h, t, pl.ds(first_row, count)],
                pair_in.at[h, t, pl.ds(first_row, count)],
                pair_send.at[q, t],
                pair_recv.at[q, t],
                partner,
            )
            copy.start()
            pair_copies[q, t] = copy
            pending.append(copy)

    def project_own(q, t):
        h, first_row, count = chunks[q]
        span = slice(first_row, first_row + count)
        own[h, t, span] = dot(act[h, span], weights_for(steps[t], core))

    first_copies, second_copies = {}, {}

    def pair_sum(q, t, way):
        h, part = chunks[q][0], parts(q)[way]
        return own[h, t, part] + pair_in[h, t, part].astype(F32)

    def first(q):
        h, where = chunks[q][0], slot_rows(q)
        for t, way, slot in ((0, 0, 0), (0, 1, 0), (1, 0, 1), (2, 1, 1)):
            if (t, way) != (0, 1):
                project_own(q, t)
                pair_copies[q, t].wait_recv()
            first_out[h, way, slot, where] = pair_sum(q, t, way).astype(BF16)
            copy = remote(
                first_out.at[h, way, slot, where],
                first_in.at[h, way, slot, where],
                first_send.at[q, way, slot],
                first_recv.at[q, way, slot],
                beside_y if way else beside_x,
            )
            copy.start()
            first_copies[q, way, slot] = copy
            pending.append(copy)
        project_own(q, 3)

    def second(q):
        h, where = chunks[q][0], slot_rows(q)
        for way in range(2):
            first_copies[q, way, 0].wait_recv()
            t = 1 if way else 2
            total = pair_sum(q, t, way) + first_in[h, way, 0, where].astype(F32)
            second_out[h, way, where] = total.astype(BF16)
            copy = remote(
                second_out.at[h, way, where],
                second_in.at[h, way, where],
                second_send.at[q, way],
                second_recv.at[q, way],
                beside_x if way else beside_y,
            )
            copy.start()
            second_copies[q, way] = copy
            pending.append(copy)

    def finish(q):
        h, where = chunks[q][0], slot_rows(q)
        pair_copies[q, 3].wait_recv()
        for way in range(2):
            first_copies[q, way, 1].wait_recv()
            total = pair_sum(q, 3, way) + first_in[h, way, 1, where].astype(F32)
            second_copies[q, way].wait_recv()
            out_ref[h, parts(q)[way]] = (total + second_in[h, way, where].astype(F32)).astype(BF16)

    project(0)
    first(0)
    project(1)
    first(1)
    project(2)
    second(0)
    first(2)
    second(1)
    finish(0)
    second(2)
    finish(1)
    finish(2)

    @pl.when(z < PAIRS - 1)
    def _():
        rims[0, 0].wait_send()
        rims[1, 0].wait_send()

    @pl.when(z > 0)
    def _():
        rims[0, 1].wait_send()
        rims[1, 1].wait_send()

    for copy in pending:
        copy.wait_send()


def fused(features, short_weight, long_filter, skip_gain, out_weight):
    rows, channels = long_filter.shape[2:]
    middle = 2 * rows
    streams = jnp.transpose(features[:, 0], (0, 2, 1, 3))
    taps = jnp.transpose(short_weight, (1, 0, 2))
    forward, inverse = odd_tables(middle)
    blocked = (2, channels // LANES, rows, LANES)
    in_vmem = pl.BlockSpec(memory_space=pltpu.VMEM)
    in_hbm = pl.BlockSpec(memory_space=pl.ANY)
    vmem = pltpu.VMEM
    dma = pltpu.SemaphoreType.DMA
    out = pl.pallas_call(
        kernel,
        out_shape=pltpu.VMEM((2, rows, channels), BF16),
        in_specs=[in_hbm] * 7,
        out_specs=in_vmem,
        scratch_shapes=[
            vmem(streams.shape, BF16),
            vmem(taps.shape, BF16),
            vmem(blocked, BF16),
            vmem((1, channels), F32),
            vmem(out_weight.shape, BF16),
            vmem(forward.shape, BF16),
            vmem(inverse.shape, BF16),
            vmem((2, 2, 2 * RIM, channels), BF16),
            vmem((2, 2, 2 * RIM, channels), BF16),
            vmem((2, 3, RIM + rows, channels), F32),
            vmem(blocked, BF16),
            vmem((2, rows, channels), F32),
            vmem((2, *blocked), BF16),
            vmem(blocked, BF16),
            vmem(blocked, BF16),
            vmem((2, 4, 2 * middle, LANES), F32),
            vmem((4, 2 * middle, LANES), F32),
            vmem((2, 2 * middle, 2 * LANES), BF16),
            vmem((2, 2 * middle, LANES), F32),
            vmem((2, 4, rows, channels), F32),
            vmem((2, rows, channels), BF16),
            vmem((2, 4, rows, channels), BF16),
            vmem((2, 4, rows, channels), BF16),
            vmem((2, 2, 2, rows // 2, channels), BF16),
            vmem((2, 2, 2, rows // 2, channels), BF16),
            vmem((2, 2, rows // 2, channels), BF16),
            vmem((2, 2, rows // 2, channels), BF16),
            dma((6,)),
            dma((2, channels // LANES)),
            dma((2, 2)),
            dma((2, 2)),
            dma((2, 2, 3)),
            dma((2, 2, 3)),
            dma((3, 3)),
            dma((3, 3)),
            dma((3, 4)),
            dma((3, 4)),
            dma((3, 2, 2)),
            dma((3, 2, 2)),
            dma((3, 2)),
            dma((3, 2)),
        ],
        compiler_params=pltpu.CompilerParams(
            collective_id=0, has_side_effects=True, vmem_limit_bytes=62 * 1024 * 1024
        ),
        name="hyena",
    )(
        streams,
        taps,
        long_filter[:, 0],
        skip_gain.reshape(1, channels),
        out_weight,
        jnp.asarray(forward),
        jnp.asarray(inverse),
    )
    return out[:, None]


def from_behind(value, axis, steps):
    count = lax.axis_size(axis)
    initial, last = (max(0, -steps), min(count, count - steps))
    return lax.ppermute(value, axis, [(source, source + steps) for source in range(initial, last)])


def transform_tables(length):
    period = 2 * length
    indices = jnp.arange(period, dtype=jnp.int32)
    phases = indices[:, None] * indices[None, :] % period
    angles = phases.astype(jnp.float32) * (2.0 * math.pi / period)
    cosine = jnp.cos(angles)
    sine_table = jnp.sin(angles)
    forward_full = jnp.concatenate([cosine, -sine_table], axis=0)
    forward_data = forward_full[:, :length]
    inverse = jnp.concatenate([cosine[:length], -sine_table[:length]], axis=1) / period
    return (forward_full, forward_data, inverse)


def complex_product(first, second):
    middle = first.shape[-2] // 2
    real_a = first[..., :middle, :]
    imag_a = first[..., middle:, :]
    real_b = second[..., :middle, :]
    imag_b = second[..., middle:, :]
    return jnp.concatenate(
        [real_a * real_b - imag_a * imag_b, real_a * imag_b + imag_a * real_b], axis=-2
    )


def featurize(tokens, before, kernel):
    extended = jnp.concatenate([before, tokens], axis=0).astype(jnp.float32)
    length = tokens.shape[0]
    margin_rows = kernel.shape[0] - 1
    summed = jnp.zeros(tokens.shape, jnp.float32)
    for offset in range(kernel.shape[0]):
        summed = (
            summed
            + kernel[offset].astype(jnp.float32)
            * extended[margin_rows - offset : margin_rows - offset + length]
        )
    return summed


def ordered(blocks):
    return jnp.concatenate([blocks[0], jnp.flip(blocks[1], axis=0)], axis=0)


def local(features, short_weight, long_filter, skip_gain, out_weight):
    pair_count = lax.axis_size("ctx")
    blocks_all = 2 * pair_count
    position = lax.axis_index("ctx")
    length = features.shape[2]
    margin_rows = short_weight.shape[0] - 1
    trailing = features[:, 0, length - margin_rows :]
    from_before = from_behind(trailing[0], "ctx", 1)
    from_after = from_behind(trailing[1], "ctx", -1)
    second_rim = jnp.where(position == pair_count - 1, trailing[0], from_after)
    first_feat = featurize(features[0, 0], from_before, short_weight)
    second_feat = featurize(features[1, 0], second_rim, short_weight)
    featured = jnp.stack([first_feat, second_feat], axis=0)
    queries = featured[:, :, 0]
    gated_keys = (featured[:, :, 1] * featured[:, :, 2]).astype(jnp.bfloat16)
    forward_full, forward_data, inverse = transform_tables(length)
    precise = lax.Precision.HIGHEST
    moved_gated, moved_filter = (
        lax.all_to_all(gated_keys[:, None], "ctx", split_axis=3, concat_axis=1, tiled=True),
        lax.all_to_all(long_filter, "ctx", split_axis=3, concat_axis=1, tiled=True),
    )
    ordered_gated = ordered(moved_gated).astype(jnp.float32)
    lag_order = ordered(moved_filter)
    padded = jnp.concatenate(
        [jnp.zeros((1,) + lag_order.shape[1:], lag_order.dtype), lag_order], axis=0
    )
    segments = jnp.concatenate([padded[1:], padded[:-1]], axis=1).astype(jnp.float32)
    responses = jnp.einsum("fm,kmc->kfc", forward_full, segments, precision=precise)
    spectra = jnp.einsum("fn,knc->kfc", forward_data, ordered_gated, precision=precise)
    sources = jnp.arange(blocks_all, dtype=jnp.int32)

    def one_target(target):
        distance = target - sources
        picked = jnp.take(responses, jnp.maximum(distance, 0), axis=0)
        products = complex_product(picked, spectra)
        summed = jnp.sum(jnp.where((distance >= 0)[:, None, None], products, 0.0), axis=0)
        return jnp.dot(inverse, summed, precision=precise)

    group_size = math.gcd(blocks_all, 8)
    grouped = sources.reshape(blocks_all // group_size, group_size)
    outputs = lax.map(jax.vmap(one_target), grouped).reshape(
        (blocks_all, length, responses.shape[-1])
    )
    blocks = jnp.stack([outputs[:pair_count], jnp.flip(outputs[pair_count:], axis=0)], axis=0)
    returned = lax.all_to_all(blocks, "ctx", split_axis=1, concat_axis=3, tiled=True)
    convolved = returned[:, 0]
    activated = (queries * (convolved + skip_gain * gated_keys.astype(jnp.float32))).astype(
        jnp.bfloat16
    )
    token_rows = activated.reshape(2 * length, activated.shape[-1])
    channels = token_rows.shape[1]
    owned = lax.psum_scatter(
        lax.dot_general(
            out_weight, token_rows, (((0,), (1,)), ((), ())), preferred_element_type=jnp.float32
        ).astype(jnp.bfloat16),
        "ch",
        scatter_dimension=0,
        tiled=True,
    ).astype(jnp.float32)
    result = owned.T
    return result.astype(jnp.bfloat16).reshape(2, 1, length, channels)


def solution(mesh):
    in_specs = (
        P(None, "ctx", None, None, "ch"),
        P(None, None, "ch"),
        P(None, "ctx", None, "ch"),
        P("ch"),
        P("ch", None),
    )
    out_specs = P(None, "ctx", None, "ch")
    shape = dict(mesh.shape)
    suits = shape == {"ctx": PAIRS, "ch": 8}
    body = fused if suits else local
    return jax.shard_map(body, mesh=mesh, in_specs=in_specs, out_specs=out_specs, check_vma=False)
```

```python
import math

import jax
import jax.numpy as jnp
import ml_dtypes
import numpy as np
from jax import lax
from jax.experimental import pallas as pl
from jax.experimental.pallas import tpu as pltpu
from jax.sharding import PartitionSpec as P

F32 = jnp.float32
BF16 = jnp.bfloat16
MESH = pl.DeviceIdType.MESH
RIM = 8
STRIP = 64
LANES = 128
PAIRS = 4


def halves(values):
    high = values.astype(ml_dtypes.bfloat16)
    low = (values - high.astype(np.float64)).astype(ml_dtypes.bfloat16)
    return np.stack([high, low])


def odd_tables(length):
    k = np.arange(length)[:, None]
    t = np.arange(length)[None, :]
    angles = ((2 * k + 1) * t % (4 * length)) * (np.pi / (2 * length))
    forward = np.concatenate([np.cos(angles), -np.sin(angles)], axis=0)
    return halves(forward), halves(forward.T / length)


def dot(a, b):
    return jnp.dot(a, b, preferred_element_type=F32)


def kernel(
    x_hbm,
    taps_hbm,
    filter_hbm,
    skip_hbm,
    weight_hbm,
    forward_hbm,
    inverse_hbm,
    out_ref,
    x_ref,
    taps_ref,
    filter_ref,
    skip_ref,
    weight,
    forward,
    inverse,
    rim_out,
    halo,
    wide,
    gated,
    queries,
    moved,
    convolved,
    back,
    filter_spec,
    key_spec,
    summed_spec,
    early,
    own,
    act,
    pair_out,
    pair_in,
    first_out,
    first_in,
    second_out,
    second_in,
    local_sem,
    filter_sem,
    halo_send,
    halo_recv,
    move_send,
    move_recv,
    back_send,
    back_recv,
    pair_send,
    pair_recv,
    first_send,
    first_recv,
    second_send,
    second_recv,
):
    rows = gated.shape[2]
    channels = weight.shape[0]
    taps = taps_ref.shape[1]
    middle = forward.shape[2]
    z = lax.axis_index("ctx")
    ch = lax.axis_index("ch")
    core, x, y = ch % 2, ch // 2 % 2, ch // 4

    def ch_of(yy, xx, cc):
        return yy * 4 + xx * 2 + cc

    partner = (z, ch_of(y, x, 1 - core))
    beside_x = (z, ch_of(y, 1 - x, core))
    beside_y = (z, ch_of(1 - y, x, core))

    sources = (x_hbm, taps_hbm, skip_hbm, forward_hbm, inverse_hbm, weight_hbm)
    places = (x_ref, taps_ref, skip_ref, forward, inverse, weight)
    loads = [
        pltpu.make_async_copy(source, target, local_sem.at[i])
        for i, (source, target) in enumerate(zip(sources, places))
    ]
    filter_loads = [
        pltpu.make_async_copy(
            filter_hbm.at[h, :, pl.ds(c * LANES, LANES)], filter_ref.at[h, c], filter_sem.at[h, c]
        )
        for h in range(2)
        for c in range(channels // LANES)
    ]
    for load in (loads[0], *filter_loads, loads[1], loads[2]):
        load.start()

    barrier = pltpu.get_barrier_semaphore()
    peers = [((z + o) % PAIRS, ch) for o in range(1, PAIRS)] + [partner, beside_x, beside_y]
    for peer in peers:
        pl.semaphore_signal(barrier, inc=1, device_id=peer, device_id_type=MESH)
    pl.semaphore_wait(barrier, len(peers))

    for load in loads[3:]:
        load.start()
    pending = []

    def remote(src, dst, send, recv, device):
        return pltpu.make_async_remote_copy(
            src_ref=src, dst_ref=dst, send_sem=send, recv_sem=recv, device_id=device, device_id_type=MESH
        )

    def keep(kind, source, h):
        moved[kind, h, block_of(h, z)] = source[h, z]

    def block_of(h, owner):
        return owner if h == 0 else PAIRS - 1 - owner

    def scatter(kind, source, h):
        copies = []
        for o in (2, 1, 3):
            target = (z + o) % PAIRS
            copy = remote(
                source.at[h, target],
                moved.at[kind, h, block_of(h, z)],
                move_send.at[kind, h, o - 1],
                move_recv.at[kind, h, o - 1],
                (target, ch),
            )
            copy.start()
            copies.append(copy)
        pending.extend(copies)
        return copies

    filter_copies, key_copies = [None, None], [None, None]
    loads[0].wait()

    def widen(h):
        for s in range(3):
            wide[h, s, RIM:] = x_ref[h, s].astype(F32)

    tails = [[x_ref[h, s, rows - 2 * RIM :].astype(F32)[RIM:] for s in range(3)] for h in range(2)]
    rims = {}
    for kind, streams in ((0, (1, 2)), (1, (0, 0))):
        for h in range(2):
            rim_out[kind, h] = jnp.concatenate([tails[h][s] for s in streams], axis=0).astype(BF16)
            rims[kind, h] = remote(
                rim_out.at[kind, h],
                halo.at[kind, h],
                halo_send.at[kind, h],
                halo_recv.at[kind, h],
                ((z + (1 if h == 0 else 3)) % PAIRS, ch),
            )

    def send_rims(kind):
        @pl.when(z < PAIRS - 1)
        def _():
            rims[kind, 0].start()

        @pl.when(z > 0)
        def _():
            rims[kind, 1].start()

    def take_rim(kind, h):
        has = z > 0 if h == 0 else z < PAIRS - 1

        @pl.when(has)
        def _():
            rims[kind, h].wait_recv()

        @pl.when(jnp.logical_not(has))
        def _():
            halo[kind, h] = jnp.zeros(halo.shape[2:], BF16) if h == 0 else rim_out[kind, 0]

        both = halo[kind, h].astype(F32)
        for m, s in enumerate((1, 2) if kind == 0 else (0,)):
            wide[h, s, :RIM] = both[m * RIM : (m + 1) * RIM]

    send_rims(0)
    for load in filter_loads:
        load.wait()
    filter_copies[0] = scatter(0, filter_ref, 0)
    widen(0)
    widen(1)

    loads[1].wait()
    tap_rows = [taps_ref[s].astype(F32) for s in range(3)]

    def taps_of(h, s, cols):
        total = None
        for i in range(taps):
            tap = tap_rows[s][i : i + 1, cols]
            term = tap * wide[h, s, pl.ds(RIM - i, rows), cols]
            total = term if total is None else total + term
        return total

    columns = [slice(a, a + LANES) for a in range(0, channels, LANES)]

    def make_keys(h):
        for c, cols in enumerate(columns):
            gated[h, c] = (taps_of(h, 1, cols) * taps_of(h, 2, cols)).astype(BF16)

    def make_queries(h):
        for cols in columns:
            queries[h, :, cols] = taps_of(h, 0, cols)

    take_rim(0, 0)
    make_keys(0)
    key_copies[0] = scatter(1, gated, 0)
    keep(1, gated, 0)
    send_rims(1)
    filter_copies[1] = scatter(0, filter_ref, 1)
    keep(0, filter_ref, 0)
    keep(0, filter_ref, 1)
    take_rim(0, 1)
    make_keys(1)
    key_copies[1] = scatter(1, gated, 1)
    keep(1, gated, 1)
    loads[3].wait()

    signs = (1 - 2 * (lax.broadcasted_iota(jnp.int32, (middle, LANES), 0) % 2)).astype(F32)

    def spectrum(kind, h):
        data = jnp.concatenate(
            [jnp.concatenate([moved[kind, h, 2 * m], moved[kind, h, 2 * m + 1]], axis=0) for m in range(2)], axis=1
        )
        return dot(forward[0], data) + dot(forward[1], data)

    def filter_spectra(h):
        for copy in filter_copies[h]:
            copy.wait_recv()
        both = spectrum(0, h)
        for m in range(2):
            filter_spec[0, 2 * h + m] = both[:, m * LANES : (m + 1) * LANES]
        for b in (2 * h, 2 * h + 1):
            if b == 0:
                filter_spec[1, 0] = filter_spec[0, 0]
            else:
                filter_spec[1, b, :middle] = filter_spec[0, b, :middle] - signs * filter_spec[0, b - 1, middle:]
                filter_spec[1, b, middle:] = filter_spec[0, b, middle:] + signs * filter_spec[0, b - 1, :middle]

    def key_spectra(h):
        for copy in key_copies[h]:
            copy.wait_recv()
        both = spectrum(1, h)
        for m in range(2):
            key_spec[2 * h + m] = both[:, m * LANES : (m + 1) * LANES]

    def pair_products(i, sources, re_rows, im_rows):
        real, imag = None, None
        for j in sources:
            ra, ia = filter_spec[1, i - j, re_rows], filter_spec[1, i - j, im_rows]
            rb, ib = key_spec[j, re_rows], key_spec[j, im_rows]
            re, im = ra * rb - ia * ib, ra * ib + ia * rb
            real = re if real is None else real + re
            imag = im if imag is None else imag + im
        return real, imag

    strips = [
        (slice(start, start + STRIP), slice(middle + start, middle + start + STRIP))
        for start in range(0, middle, STRIP)
    ]

    def early_products():
        for m in range(2):
            for re_rows, im_rows in strips:
                early[m, re_rows], early[m, im_rows] = pair_products(2 + m, (0, 1), re_rows, im_rows)

    def products(h):
        for m in range(2):
            i = 2 * h + m
            cols = slice(m * LANES, (m + 1) * LANES)
            for re_rows, im_rows in strips:
                sums = pair_products(i, range(2 * h, i + 1), re_rows, im_rows)
                for where, value in zip((re_rows, im_rows), sums):
                    if h == 1:
                        value = value + early[m, where]
                    high = value.astype(BF16)
                    summed_spec[0, where, cols] = high
                    summed_spec[1, where, cols] = (value - high.astype(F32)).astype(BF16)

    chunks = [(h, first_row, rows // 2) for h in range(2) for first_row in (0, rows // 2)]
    back_copies = {}

    def send_back(q):
        h, first_row, count = chunks[q]
        copies = []
        for o in (2, 1, 3):
            target = (z + o) % PAIRS
            copy = remote(
                convolved.at[h, block_of(h, target), pl.ds(first_row, count)],
                back.at[h, z, pl.ds(first_row, count)],
                back_send.at[q, o - 1],
                back_recv.at[q, o - 1],
                (target, ch),
            )
            copy.start()
            copies.append(copy)
        back[h, z, pl.ds(first_row, count)] = convolved[h, block_of(h, z), pl.ds(first_row, count)]
        pending.extend(copies)
        back_copies[q] = copies

    def convolve(h):
        products(h)
        high, low = summed_spec[0], summed_spec[1]
        result = dot(inverse[0], high) + dot(inverse[0], low) + dot(inverse[1], high)
        result = result.astype(BF16)
        for block in range(PAIRS):
            m, part = divmod(block, 2)
            convolved[h, block] = result[part * rows : (part + 1) * rows, m * LANES : (m + 1) * LANES]

    filter_spectra(0)
    key_spectra(0)
    loads[4].wait()
    convolve(0)
    send_back(0)
    send_back(1)
    take_rim(1, 0)
    make_queries(0)
    take_rim(1, 1)
    make_queries(1)
    filter_spectra(1)
    early_products()
    key_spectra(1)
    convolve(1)
    send_back(2)
    send_back(3)
    loads[5].wait()
    loads[2].wait()

    steps = [(1, 1), (0, 1), (1, 0), (0, 0)]
    pair_copies = {}

    def parts(q):
        h, first_row, count = chunks[q]
        half = count // 2
        return slice(first_row, first_row + half), slice(first_row + half, first_row + count)

    def slot_rows(q):
        return pl.ds(chunks[q][1] // 2, chunks[q][2] // 2)

    def weights_for(step, cc):
        yy = 1 - y if step[0] else y
        xx = 1 - x if step[1] else x
        return weight[:, pl.ds(pl.multiple_of(ch_of(yy, xx, cc) * channels, channels), channels)]

    def project(q):
        h, first_row, count = chunks[q]
        span = slice(first_row, first_row + count)
        for copy in back_copies[q]:
            copy.wait_recv()
        for c, cols in enumerate(columns):
            summed = back[h, c, span].astype(F32) + skip_ref[:, cols] * gated[h, c, span].astype(F32)
            act[h, span, cols] = (queries[h, span, cols] * summed).astype(BF16)
        rows_in = act[h, span]
        for t, step in enumerate(steps):
            pair_out[h, t, span] = dot(rows_in, weights_for(step, 1 - core)).astype(BF16)
            copy = remote(
                pair_out.at[h, t, pl.ds(first_row, count)],
                pair_in.at[h, t, pl.ds(first_row, count)],
                pair_send.at[q, t],
                pair_recv.at[q, t],
                partner,
            )
            copy.start()
            pair_copies[q, t] = copy
            pending.append(copy)

    def project_own(q, t):
        h, first_row, count = chunks[q]
        span = slice(first_row, first_row + count)
        own[h, t, span] = dot(act[h, span], weights_for(steps[t], core))

    first_copies, second_copies = {}, {}

    def pair_sum(q, t, way):
        h, part = chunks[q][0], parts(q)[way]
        return own[h, t, part] + pair_in[h, t, part].astype(F32)

    def first(q):
        h, where = chunks[q][0], slot_rows(q)
        for t, way, slot in ((0, 0, 0), (0, 1, 0), (1, 0, 1), (2, 1, 1)):
            if (t, way) != (0, 1):
                project_own(q, t)
                pair_copies[q, t].wait_recv()
            first_out[h, way, slot, where] = pair_sum(q, t, way).astype(BF16)
            copy = remote(
                first_out.at[h, way, slot, where],
                first_in.at[h, way, slot, where],
                first_send.at[q, way, slot],
                first_recv.at[q, way, slot],
                beside_y if way else beside_x,
            )
            copy.start()
            first_copies[q, way, slot] = copy
            pending.append(copy)
        project_own(q, 3)

    def second(q):
        h, where = chunks[q][0], slot_rows(q)
        for way in range(2):
            first_copies[q, way, 0].wait_recv()
            t = 1 if way else 2
            total = pair_sum(q, t, way) + first_in[h, way, 0, where].astype(F32)
            second_out[h, way, where] = total.astype(BF16)
            copy = remote(
                second_out.at[h, way, where],
                second_in.at[h, way, where],
                second_send.at[q, way],
                second_recv.at[q, way],
                beside_x if way else beside_y,
            )
            copy.start()
            second_copies[q, way] = copy
            pending.append(copy)

    def finish(q):
        h, where = chunks[q][0], slot_rows(q)
        pair_copies[q, 3].wait_recv()
        for way in range(2):
            first_copies[q, way, 1].wait_recv()
            total = pair_sum(q, 3, way) + first_in[h, way, 1, where].astype(F32)
            second_copies[q, way].wait_recv()
            out_ref[h, parts(q)[way]] = (total + second_in[h, way, where].astype(F32)).astype(BF16)

    project(0)
    first(0)
    project(1)
    first(1)
    project(2)
    second(0)
    first(2)
    project(3)
    second(1)
    first(3)
    finish(0)
    second(2)
    finish(1)
    second(3)
    finish(2)
    finish(3)

    @pl.when(z < PAIRS - 1)
    def _():
        rims[0, 0].wait_send()
        rims[1, 0].wait_send()

    @pl.when(z > 0)
    def _():
        rims[0, 1].wait_send()
        rims[1, 1].wait_send()

    for copy in pending:
        copy.wait_send()


def fused(features, short_weight, long_filter, skip_gain, out_weight):
    rows, channels = long_filter.shape[2:]
    middle = 2 * rows
    streams = jnp.transpose(features[:, 0], (0, 2, 1, 3))
    taps = jnp.transpose(short_weight, (1, 0, 2))
    forward, inverse = odd_tables(middle)
    blocked = (2, channels // LANES, rows, LANES)
    in_vmem = pl.BlockSpec(memory_space=pltpu.VMEM)
    in_hbm = pl.BlockSpec(memory_space=pl.ANY)
    vmem = pltpu.VMEM
    dma = pltpu.SemaphoreType.DMA
    out = pl.pallas_call(
        kernel,
        out_shape=pltpu.VMEM((2, rows, channels), BF16),
        in_specs=[in_hbm] * 7,
        out_specs=in_vmem,
        scratch_shapes=[
            vmem(streams.shape, BF16),
            vmem(taps.shape, BF16),
            vmem(blocked, BF16),
            vmem((1, channels), F32),
            vmem(out_weight.shape, BF16),
            vmem(forward.shape, BF16),
            vmem(inverse.shape, BF16),
            vmem((2, 2, 2 * RIM, channels), BF16),
            vmem((2, 2, 2 * RIM, channels), BF16),
            vmem((2, 3, RIM + rows, channels), F32),
            vmem(blocked, BF16),
            vmem((2, rows, channels), F32),
            vmem((2, *blocked), BF16),
            vmem(blocked, BF16),
            vmem(blocked, BF16),
            vmem((2, 4, 2 * middle, LANES), F32),
            vmem((4, 2 * middle, LANES), F32),
            vmem((2, 2 * middle, 2 * LANES), BF16),
            vmem((2, 2 * middle, LANES), F32),
            vmem((2, 4, rows, channels), F32),
            vmem((2, rows, channels), BF16),
            vmem((2, 4, rows, channels), BF16),
            vmem((2, 4, rows, channels), BF16),
            vmem((2, 2, 2, rows // 2, channels), BF16),
            vmem((2, 2, 2, rows // 2, channels), BF16),
            vmem((2, 2, rows // 2, channels), BF16),
            vmem((2, 2, rows // 2, channels), BF16),
            dma((6,)),
            dma((2, channels // LANES)),
            dma((2, 2)),
            dma((2, 2)),
            dma((2, 2, 3)),
            dma((2, 2, 3)),
            dma((4, 3)),
            dma((4, 3)),
            dma((4, 4)),
            dma((4, 4)),
            dma((4, 2, 2)),
            dma((4, 2, 2)),
            dma((4, 2)),
            dma((4, 2)),
        ],
        compiler_params=pltpu.CompilerParams(
            collective_id=0, has_side_effects=True, vmem_limit_bytes=62 * 1024 * 1024
        ),
        name="hyena",
    )(
        streams,
        taps,
        long_filter[:, 0],
        skip_gain.reshape(1, channels),
        out_weight,
        jnp.asarray(forward),
        jnp.asarray(inverse),
    )
    return out[:, None]


def from_behind(value, axis, steps):
    count = lax.axis_size(axis)
    initial, last = (max(0, -steps), min(count, count - steps))
    return lax.ppermute(value, axis, [(source, source + steps) for source in range(initial, last)])


def transform_tables(length):
    period = 2 * length
    indices = jnp.arange(period, dtype=jnp.int32)
    phases = indices[:, None] * indices[None, :] % period
    angles = phases.astype(jnp.float32) * (2.0 * math.pi / period)
    cosine = jnp.cos(angles)
    sine_table = jnp.sin(angles)
    forward_full = jnp.concatenate([cosine, -sine_table], axis=0)
    forward_data = forward_full[:, :length]
    inverse = jnp.concatenate([cosine[:length], -sine_table[:length]], axis=1) / period
    return (forward_full, forward_data, inverse)


def complex_product(first, second):
    middle = first.shape[-2] // 2
    real_a = first[..., :middle, :]
    imag_a = first[..., middle:, :]
    real_b = second[..., :middle, :]
    imag_b = second[..., middle:, :]
    return jnp.concatenate(
        [real_a * real_b - imag_a * imag_b, real_a * imag_b + imag_a * real_b], axis=-2
    )


def featurize(tokens, before, kernel):
    extended = jnp.concatenate([before, tokens], axis=0).astype(jnp.float32)
    length = tokens.shape[0]
    margin_rows = kernel.shape[0] - 1
    summed = jnp.zeros(tokens.shape, jnp.float32)
    for offset in range(kernel.shape[0]):
        summed = (
            summed
            + kernel[offset].astype(jnp.float32)
            * extended[margin_rows - offset : margin_rows - offset + length]
        )
    return summed


def ordered(blocks):
    return jnp.concatenate([blocks[0], jnp.flip(blocks[1], axis=0)], axis=0)


def local(features, short_weight, long_filter, skip_gain, out_weight):
    pair_count = lax.axis_size("ctx")
    blocks_all = 2 * pair_count
    position = lax.axis_index("ctx")
    length = features.shape[2]
    margin_rows = short_weight.shape[0] - 1
    trailing = features[:, 0, length - margin_rows :]
    from_before = from_behind(trailing[0], "ctx", 1)
    from_after = from_behind(trailing[1], "ctx", -1)
    second_rim = jnp.where(position == pair_count - 1, trailing[0], from_after)
    first_feat = featurize(features[0, 0], from_before, short_weight)
    second_feat = featurize(features[1, 0], second_rim, short_weight)
    featured = jnp.stack([first_feat, second_feat], axis=0)
    queries = featured[:, :, 0]
    gated_keys = (featured[:, :, 1] * featured[:, :, 2]).astype(jnp.bfloat16)
    forward_full, forward_data, inverse = transform_tables(length)
    precise = lax.Precision.HIGHEST
    moved_gated, moved_filter = (
        lax.all_to_all(gated_keys[:, None], "ctx", split_axis=3, concat_axis=1, tiled=True),
        lax.all_to_all(long_filter, "ctx", split_axis=3, concat_axis=1, tiled=True),
    )
    ordered_gated = ordered(moved_gated).astype(jnp.float32)
    lag_order = ordered(moved_filter)
    padded = jnp.concatenate(
        [jnp.zeros((1,) + lag_order.shape[1:], lag_order.dtype), lag_order], axis=0
    )
    segments = jnp.concatenate([padded[1:], padded[:-1]], axis=1).astype(jnp.float32)
    responses = jnp.einsum("fm,kmc->kfc", forward_full, segments, precision=precise)
    spectra = jnp.einsum("fn,knc->kfc", forward_data, ordered_gated, precision=precise)
    sources = jnp.arange(blocks_all, dtype=jnp.int32)

    def one_target(target):
        distance = target - sources
        picked = jnp.take(responses, jnp.maximum(distance, 0), axis=0)
        products = complex_product(picked, spectra)
        summed = jnp.sum(jnp.where((distance >= 0)[:, None, None], products, 0.0), axis=0)
        return jnp.dot(inverse, summed, precision=precise)

    group_size = math.gcd(blocks_all, 8)
    grouped = sources.reshape(blocks_all // group_size, group_size)
    outputs = lax.map(jax.vmap(one_target), grouped).reshape(
        (blocks_all, length, responses.shape[-1])
    )
    blocks = jnp.stack([outputs[:pair_count], jnp.flip(outputs[pair_count:], axis=0)], axis=0)
    returned = lax.all_to_all(blocks, "ctx", split_axis=1, concat_axis=3, tiled=True)
    convolved = returned[:, 0]
    activated = (queries * (convolved + skip_gain * gated_keys.astype(jnp.float32))).astype(
        jnp.bfloat16
    )
    token_rows = activated.reshape(2 * length, activated.shape[-1])
    channels = token_rows.shape[1]
    owned = lax.psum_scatter(
        lax.dot_general(
            out_weight, token_rows, (((0,), (1,)), ((), ())), preferred_element_type=jnp.float32
        ).astype(jnp.bfloat16),
        "ch",
        scatter_dimension=0,
        tiled=True,
    ).astype(jnp.float32)
    result = owned.T
    return result.astype(jnp.bfloat16).reshape(2, 1, length, channels)


def solution(mesh):
    in_specs = (
        P(None, "ctx", None, None, "ch"),
        P(None, None, "ch"),
        P(None, "ctx", None, "ch"),
        P("ch"),
        P("ch", None),
    )
    out_specs = P(None, "ctx", None, "ch")
    shape = dict(mesh.shape)
    suits = shape == {"ctx": PAIRS, "ch": 8}
    body = fused if suits else local
    return jax.shard_map(body, mesh=mesh, in_specs=in_specs, out_specs=out_specs, check_vma=False)
```

```python
import math

import jax
import jax.numpy as jnp
import ml_dtypes
import numpy as np
from jax import lax
from jax.experimental import pallas as pl
from jax.experimental.pallas import tpu as pltpu
from jax.sharding import PartitionSpec as P

F32 = jnp.float32
BF16 = jnp.bfloat16
MESH = pl.DeviceIdType.MESH
RIM = 8
STRIP = 64
LANES = 128
PAIRS = 4


def halves(values):
    high = values.astype(ml_dtypes.bfloat16)
    low = (values - high.astype(np.float64)).astype(ml_dtypes.bfloat16)
    return np.stack([high, low])


def odd_tables(length):
    k = np.arange(length)[:, None]
    t = np.arange(length)[None, :]
    angles = ((2 * k + 1) * t % (4 * length)) * (np.pi / (2 * length))
    forward = np.concatenate([np.cos(angles), -np.sin(angles)], axis=0)
    return halves(forward), halves(forward.T / length)


def dot(a, b):
    return jnp.dot(a, b, preferred_element_type=F32)


def kernel(
    x_hbm,
    taps_hbm,
    filter_hbm,
    skip_hbm,
    weight_hbm,
    forward_hbm,
    inverse_hbm,
    out_ref,
    x_ref,
    taps_ref,
    filter_ref,
    skip_ref,
    weight,
    forward,
    inverse,
    rim_out,
    halo,
    wide,
    gated,
    queries,
    moved,
    convolved,
    back,
    filter_spec,
    key_spec,
    summed_spec,
    early,
    own,
    act,
    pair_out,
    pair_in,
    first_out,
    first_in,
    second_out,
    second_in,
    local_sem,
    filter_sem,
    halo_send,
    halo_recv,
    move_send,
    move_recv,
    back_send,
    back_recv,
    pair_send,
    pair_recv,
    first_send,
    first_recv,
    second_send,
    second_recv,
):
    rows = gated.shape[2]
    channels = weight.shape[0]
    taps = taps_ref.shape[1]
    middle = forward.shape[2]
    z = lax.axis_index("ctx")
    ch = lax.axis_index("ch")
    core, x, y = ch % 2, ch // 2 % 2, ch // 4

    def ch_of(yy, xx, cc):
        return yy * 4 + xx * 2 + cc

    partner = (z, ch_of(y, x, 1 - core))
    beside_x = (z, ch_of(y, 1 - x, core))
    beside_y = (z, ch_of(1 - y, x, core))

    sources = (x_hbm, taps_hbm, skip_hbm, forward_hbm, inverse_hbm, weight_hbm)
    places = (x_ref, taps_ref, skip_ref, forward, inverse, weight)
    loads = [
        pltpu.make_async_copy(source, target, local_sem.at[i])
        for i, (source, target) in enumerate(zip(sources, places))
    ]
    filter_loads = [
        pltpu.make_async_copy(
            filter_hbm.at[h, :, pl.ds(c * LANES, LANES)], filter_ref.at[h, c], filter_sem.at[h, c]
        )
        for h in range(2)
        for c in range(channels // LANES)
    ]
    for load in (loads[0], *filter_loads, loads[1], loads[2]):
        load.start()

    barrier = pltpu.get_barrier_semaphore()
    peers = [((z + o) % PAIRS, ch) for o in range(1, PAIRS)] + [partner, beside_x, beside_y]
    for peer in peers:
        pl.semaphore_signal(barrier, inc=1, device_id=peer, device_id_type=MESH)
    pl.semaphore_wait(barrier, len(peers))

    for load in loads[3:]:
        load.start()
    pending = []

    def remote(src, dst, send, recv, device):
        return pltpu.make_async_remote_copy(
            src_ref=src, dst_ref=dst, send_sem=send, recv_sem=recv, device_id=device, device_id_type=MESH
        )

    def keep(kind, source, h):
        moved[kind, h, block_of(h, z)] = source[h, z]

    def block_of(h, owner):
        return owner if h == 0 else PAIRS - 1 - owner

    def scatter(kind, source, h, offsets=(2, 1, 3)):
        copies = []
        for o in offsets:
            target = (z + o) % PAIRS
            copy = remote(
                source.at[h, target],
                moved.at[kind, h, block_of(h, z)],
                move_send.at[kind, h, o - 1],
                move_recv.at[kind, h, o - 1],
                (target, ch),
            )
            copy.start()
            copies.append(copy)
        pending.extend(copies)
        return copies

    filter_copies, key_copies = [None, None], [None, None]
    loads[0].wait()

    def widen(h):
        for s in range(3):
            wide[h, s, RIM:] = x_ref[h, s].astype(F32)

    tails = [[x_ref[h, s, rows - 2 * RIM :].astype(F32)[RIM:] for s in range(3)] for h in range(2)]
    rims = {}
    for kind, streams in ((0, (1, 2)), (1, (0, 0))):
        for h in range(2):
            rim_out[kind, h] = jnp.concatenate([tails[h][s] for s in streams], axis=0).astype(BF16)
            rims[kind, h] = remote(
                rim_out.at[kind, h],
                halo.at[kind, h],
                halo_send.at[kind, h],
                halo_recv.at[kind, h],
                ((z + (1 if h == 0 else 3)) % PAIRS, ch),
            )

    def send_rims(kind):
        @pl.when(z < PAIRS - 1)
        def _():
            rims[kind, 0].start()

        @pl.when(z > 0)
        def _():
            rims[kind, 1].start()

    def take_rim(kind, h):
        has = z > 0 if h == 0 else z < PAIRS - 1

        @pl.when(has)
        def _():
            rims[kind, h].wait_recv()

        @pl.when(jnp.logical_not(has))
        def _():
            halo[kind, h] = jnp.zeros(halo.shape[2:], BF16) if h == 0 else rim_out[kind, 0]

        both = halo[kind, h].astype(F32)
        for m, s in enumerate((1, 2) if kind == 0 else (0,)):
            wide[h, s, :RIM] = both[m * RIM : (m + 1) * RIM]

    send_rims(0)
    for load in filter_loads:
        load.wait()
    filter_copies[0] = scatter(0, filter_ref, 0)
    widen(0)
    widen(1)

    loads[1].wait()
    tap_rows = [taps_ref[s].astype(F32) for s in range(3)]

    def taps_of(h, s, cols):
        total = None
        for i in range(taps):
            tap = tap_rows[s][i : i + 1, cols]
            term = tap * wide[h, s, pl.ds(RIM - i, rows), cols]
            total = term if total is None else total + term
        return total

    columns = [slice(a, a + LANES) for a in range(0, channels, LANES)]

    def make_keys(h):
        for c, cols in enumerate(columns):
            gated[h, c] = (taps_of(h, 1, cols) * taps_of(h, 2, cols)).astype(BF16)

    def make_queries(h):
        for cols in columns:
            queries[h, :, cols] = taps_of(h, 0, cols)

    take_rim(0, 0)
    make_keys(0)
    key_copies[0] = scatter(1, gated, 0)
    keep(1, gated, 0)
    send_rims(1)
    filter_copies[1] = scatter(0, filter_ref, 1)
    keep(0, filter_ref, 0)
    keep(0, filter_ref, 1)
    take_rim(0, 1)
    make_keys(1)
    key_copies[1] = scatter(1, gated, 1, (2,))
    keep(1, gated, 1)
    loads[3].wait()

    signs = (1 - 2 * (lax.broadcasted_iota(jnp.int32, (middle, LANES), 0) % 2)).astype(F32)

    def spectrum(kind, h):
        data = jnp.concatenate(
            [jnp.concatenate([moved[kind, h, 2 * m], moved[kind, h, 2 * m + 1]], axis=0) for m in range(2)], axis=1
        )
        return dot(forward[0], data) + dot(forward[1], data)

    def filter_spectra(h):
        for copy in filter_copies[h]:
            copy.wait_recv()
        both = spectrum(0, h)
        for m in range(2):
            filter_spec[0, 2 * h + m] = both[:, m * LANES : (m + 1) * LANES]
        for b in (2 * h, 2 * h + 1):
            if b == 0:
                filter_spec[1, 0] = filter_spec[0, 0]
            else:
                filter_spec[1, b, :middle] = filter_spec[0, b, :middle] - signs * filter_spec[0, b - 1, middle:]
                filter_spec[1, b, middle:] = filter_spec[0, b, middle:] + signs * filter_spec[0, b - 1, :middle]

    def key_spectra(h):
        for copy in key_copies[h]:
            copy.wait_recv()
        both = spectrum(1, h)
        for m in range(2):
            key_spec[2 * h + m] = both[:, m * LANES : (m + 1) * LANES]

    def pair_products(i, sources, re_rows, im_rows):
        real, imag = None, None
        for j in sources:
            ra, ia = filter_spec[1, i - j, re_rows], filter_spec[1, i - j, im_rows]
            rb, ib = key_spec[j, re_rows], key_spec[j, im_rows]
            re, im = ra * rb - ia * ib, ra * ib + ia * rb
            real = re if real is None else real + re
            imag = im if imag is None else imag + im
        return real, imag

    strips = [
        (slice(start, start + STRIP), slice(middle + start, middle + start + STRIP))
        for start in range(0, middle, STRIP)
    ]

    def early_products():
        for m in range(2):
            for re_rows, im_rows in strips:
                early[m, re_rows], early[m, im_rows] = pair_products(2 + m, (0, 1), re_rows, im_rows)

    def products(h):
        for m in range(2):
            i = 2 * h + m
            cols = slice(m * LANES, (m + 1) * LANES)
            for re_rows, im_rows in strips:
                sums = pair_products(i, range(2 * h, i + 1), re_rows, im_rows)
                for where, value in zip((re_rows, im_rows), sums):
                    if h == 1:
                        value = value + early[m, where]
                    high = value.astype(BF16)
                    summed_spec[0, where, cols] = high
                    summed_spec[1, where, cols] = (value - high.astype(F32)).astype(BF16)

    chunks = [(h, first_row, rows // 2) for h in range(2) for first_row in (0, rows // 2)]
    back_copies = {}

    def send_back(q):
        h, first_row, count = chunks[q]
        copies = []
        for o in (2, 1, 3):
            target = (z + o) % PAIRS
            copy = remote(
                convolved.at[h, block_of(h, target), pl.ds(first_row, count)],
                back.at[h, z, pl.ds(first_row, count)],
                back_send.at[q, o - 1],
                back_recv.at[q, o - 1],
                (target, ch),
            )
            copy.start()
            copies.append(copy)
        back[h, z, pl.ds(first_row, count)] = convolved[h, block_of(h, z), pl.ds(first_row, count)]
        pending.extend(copies)
        back_copies[q] = copies

    def convolve(h):
        products(h)
        high, low = summed_spec[0], summed_spec[1]
        result = dot(inverse[0], high) + dot(inverse[0], low) + dot(inverse[1], high)
        result = result.astype(BF16)
        for block in range(PAIRS):
            m, part = divmod(block, 2)
            convolved[h, block] = result[part * rows : (part + 1) * rows, m * LANES : (m + 1) * LANES]

    filter_spectra(0)
    key_spectra(0)
    loads[4].wait()
    convolve(0)
    send_back(0)
    send_back(1)
    key_copies[1] += scatter(1, gated, 1, (1, 3))
    take_rim(1, 0)
    make_queries(0)
    take_rim(1, 1)
    make_queries(1)
    filter_spectra(1)
    early_products()
    key_spectra(1)
    convolve(1)
    send_back(2)
    send_back(3)
    loads[5].wait()
    loads[2].wait()

    steps = [(1, 1), (0, 1), (1, 0), (0, 0)]
    pair_copies = {}

    def parts(q):
        h, first_row, count = chunks[q]
        half = count // 2
        return slice(first_row, first_row + half), slice(first_row + half, first_row + count)

    def slot_rows(q):
        return pl.ds(chunks[q][1] // 2, chunks[q][2] // 2)

    def weights_for(step, cc):
        yy = 1 - y if step[0] else y
        xx = 1 - x if step[1] else x
        return weight[:, pl.ds(pl.multiple_of(ch_of(yy, xx, cc) * channels, channels), channels)]

    def project(q):
        h, first_row, count = chunks[q]
        span = slice(first_row, first_row + count)
        for copy in back_copies[q]:
            copy.wait_recv()
        for c, cols in enumerate(columns):
            summed = back[h, c, span].astype(F32) + skip_ref[:, cols] * gated[h, c, span].astype(F32)
            act[h, span, cols] = (queries[h, span, cols] * summed).astype(BF16)
        rows_in = act[h, span]
        for t, step in enumerate(steps):
            pair_out[h, t, span] = dot(rows_in, weights_for(step, 1 - core)).astype(BF16)
            copy = remote(
                pair_out.at[h, t, pl.ds(first_row, count)],
                pair_in.at[h, t, pl.ds(first_row, count)],
                pair_send.at[q, t],
                pair_recv.at[q, t],
                partner,
            )
            copy.start()
            pair_copies[q, t] = copy
            pending.append(copy)

    def project_own(q, t):
        h, first_row, count = chunks[q]
        span = slice(first_row, first_row + count)
        own[h, t, span] = dot(act[h, span], weights_for(steps[t], core))

    first_copies, second_copies = {}, {}

    def pair_sum(q, t, way):
        h, part = chunks[q][0], parts(q)[way]
        return own[h, t, part] + pair_in[h, t, part].astype(F32)

    def first(q):
        h, where = chunks[q][0], slot_rows(q)
        for t, way, slot in ((0, 0, 0), (0, 1, 0), (1, 0, 1), (2, 1, 1)):
            if (t, way) != (0, 1):
                project_own(q, t)
                pair_copies[q, t].wait_recv()
            first_out[h, way, slot, where] = pair_sum(q, t, way).astype(BF16)
            copy = remote(
                first_out.at[h, way, slot, where],
                first_in.at[h, way, slot, where],
                first_send.at[q, way, slot],
                first_recv.at[q, way, slot],
                beside_y if way else beside_x,
            )
            copy.start()
            first_copies[q, way, slot] = copy
            pending.append(copy)
        project_own(q, 3)

    def second(q):
        h, where = chunks[q][0], slot_rows(q)
        for way in range(2):
            first_copies[q, way, 0].wait_recv()
            t = 1 if way else 2
            total = pair_sum(q, t, way) + first_in[h, way, 0, where].astype(F32)
            second_out[h, way, where] = total.astype(BF16)
            copy = remote(
                second_out.at[h, way, where],
                second_in.at[h, way, where],
                second_send.at[q, way],
                second_recv.at[q, way],
                beside_x if way else beside_y,
            )
            copy.start()
            second_copies[q, way] = copy
            pending.append(copy)

    def finish(q):
        h, where = chunks[q][0], slot_rows(q)
        pair_copies[q, 3].wait_recv()
        for way in range(2):
            first_copies[q, way, 1].wait_recv()
            total = pair_sum(q, 3, way) + first_in[h, way, 1, where].astype(F32)
            second_copies[q, way].wait_recv()
            out_ref[h, parts(q)[way]] = (total + second_in[h, way, where].astype(F32)).astype(BF16)

    project(0)
    first(0)
    project(1)
    first(1)
    project(2)
    second(0)
    first(2)
    project(3)
    second(1)
    first(3)
    finish(0)
    second(2)
    finish(1)
    second(3)
    finish(2)
    finish(3)

    @pl.when(z < PAIRS - 1)
    def _():
        rims[0, 0].wait_send()
        rims[1, 0].wait_send()

    @pl.when(z > 0)
    def _():
        rims[0, 1].wait_send()
        rims[1, 1].wait_send()

    for copy in pending:
        copy.wait_send()


def fused(features, short_weight, long_filter, skip_gain, out_weight):
    rows, channels = long_filter.shape[2:]
    middle = 2 * rows
    streams = jnp.transpose(features[:, 0], (0, 2, 1, 3))
    taps = jnp.transpose(short_weight, (1, 0, 2))
    forward, inverse = odd_tables(middle)
    blocked = (2, channels // LANES, rows, LANES)
    in_vmem = pl.BlockSpec(memory_space=pltpu.VMEM)
    in_hbm = pl.BlockSpec(memory_space=pl.ANY)
    vmem = pltpu.VMEM
    dma = pltpu.SemaphoreType.DMA
    out = pl.pallas_call(
        kernel,
        out_shape=pltpu.VMEM((2, rows, channels), BF16),
        in_specs=[in_hbm] * 7,
        out_specs=in_vmem,
        scratch_shapes=[
            vmem(streams.shape, BF16),
            vmem(taps.shape, BF16),
            vmem(blocked, BF16),
            vmem((1, channels), F32),
            vmem(out_weight.shape, BF16),
            vmem(forward.shape, BF16),
            vmem(inverse.shape, BF16),
            vmem((2, 2, 2 * RIM, channels), BF16),
            vmem((2, 2, 2 * RIM, channels), BF16),
            vmem((2, 3, RIM + rows, channels), F32),
            vmem(blocked, BF16),
            vmem((2, rows, channels), F32),
            vmem((2, *blocked), BF16),
            vmem(blocked, BF16),
            vmem(blocked, BF16),
            vmem((2, 4, 2 * middle, LANES), F32),
            vmem((4, 2 * middle, LANES), F32),
            vmem((2, 2 * middle, 2 * LANES), BF16),
            vmem((2, 2 * middle, LANES), F32),
            vmem((2, 4, rows, channels), F32),
            vmem((2, rows, channels), BF16),
            vmem((2, 4, rows, channels), BF16),
            vmem((2, 4, rows, channels), BF16),
            vmem((2, 2, 2, rows // 2, channels), BF16),
            vmem((2, 2, 2, rows // 2, channels), BF16),
            vmem((2, 2, rows // 2, channels), BF16),
            vmem((2, 2, rows // 2, channels), BF16),
            dma((6,)),
            dma((2, channels // LANES)),
            dma((2, 2)),
            dma((2, 2)),
            dma((2, 2, 3)),
            dma((2, 2, 3)),
            dma((4, 3)),
            dma((4, 3)),
            dma((4, 4)),
            dma((4, 4)),
            dma((4, 2, 2)),
            dma((4, 2, 2)),
            dma((4, 2)),
            dma((4, 2)),
        ],
        compiler_params=pltpu.CompilerParams(
            collective_id=0, has_side_effects=True, vmem_limit_bytes=62 * 1024 * 1024
        ),
        name="hyena",
    )(
        streams,
        taps,
        long_filter[:, 0],
        skip_gain.reshape(1, channels),
        out_weight,
        jnp.asarray(forward),
        jnp.asarray(inverse),
    )
    return out[:, None]


def from_behind(value, axis, steps):
    count = lax.axis_size(axis)
    initial, last = (max(0, -steps), min(count, count - steps))
    return lax.ppermute(value, axis, [(source, source + steps) for source in range(initial, last)])


def transform_tables(length):
    period = 2 * length
    indices = jnp.arange(period, dtype=jnp.int32)
    phases = indices[:, None] * indices[None, :] % period
    angles = phases.astype(jnp.float32) * (2.0 * math.pi / period)
    cosine = jnp.cos(angles)
    sine_table = jnp.sin(angles)
    forward_full = jnp.concatenate([cosine, -sine_table], axis=0)
    forward_data = forward_full[:, :length]
    inverse = jnp.concatenate([cosine[:length], -sine_table[:length]], axis=1) / period
    return (forward_full, forward_data, inverse)


def complex_product(first, second):
    middle = first.shape[-2] // 2
    real_a = first[..., :middle, :]
    imag_a = first[..., middle:, :]
    real_b = second[..., :middle, :]
    imag_b = second[..., middle:, :]
    return jnp.concatenate(
        [real_a * real_b - imag_a * imag_b, real_a * imag_b + imag_a * real_b], axis=-2
    )


def featurize(tokens, before, kernel):
    extended = jnp.concatenate([before, tokens], axis=0).astype(jnp.float32)
    length = tokens.shape[0]
    margin_rows = kernel.shape[0] - 1
    summed = jnp.zeros(tokens.shape, jnp.float32)
    for offset in range(kernel.shape[0]):
        summed = (
            summed
            + kernel[offset].astype(jnp.float32)
            * extended[margin_rows - offset : margin_rows - offset + length]
        )
    return summed


def ordered(blocks):
    return jnp.concatenate([blocks[0], jnp.flip(blocks[1], axis=0)], axis=0)


def local(features, short_weight, long_filter, skip_gain, out_weight):
    pair_count = lax.axis_size("ctx")
    blocks_all = 2 * pair_count
    position = lax.axis_index("ctx")
    length = features.shape[2]
    margin_rows = short_weight.shape[0] - 1
    trailing = features[:, 0, length - margin_rows :]
    from_before = from_behind(trailing[0], "ctx", 1)
    from_after = from_behind(trailing[1], "ctx", -1)
    second_rim = jnp.where(position == pair_count - 1, trailing[0], from_after)
    first_feat = featurize(features[0, 0], from_before, short_weight)
    second_feat = featurize(features[1, 0], second_rim, short_weight)
    featured = jnp.stack([first_feat, second_feat], axis=0)
    queries = featured[:, :, 0]
    gated_keys = (featured[:, :, 1] * featured[:, :, 2]).astype(jnp.bfloat16)
    forward_full, forward_data, inverse = transform_tables(length)
    precise = lax.Precision.HIGHEST
    moved_gated, moved_filter = (
        lax.all_to_all(gated_keys[:, None], "ctx", split_axis=3, concat_axis=1, tiled=True),
        lax.all_to_all(long_filter, "ctx", split_axis=3, concat_axis=1, tiled=True),
    )
    ordered_gated = ordered(moved_gated).astype(jnp.float32)
    lag_order = ordered(moved_filter)
    padded = jnp.concatenate(
        [jnp.zeros((1,) + lag_order.shape[1:], lag_order.dtype), lag_order], axis=0
    )
    segments = jnp.concatenate([padded[1:], padded[:-1]], axis=1).astype(jnp.float32)
    responses = jnp.einsum("fm,kmc->kfc", forward_full, segments, precision=precise)
    spectra = jnp.einsum("fn,knc->kfc", forward_data, ordered_gated, precision=precise)
    sources = jnp.arange(blocks_all, dtype=jnp.int32)

    def one_target(target):
        distance = target - sources
        picked = jnp.take(responses, jnp.maximum(distance, 0), axis=0)
        products = complex_product(picked, spectra)
        summed = jnp.sum(jnp.where((distance >= 0)[:, None, None], products, 0.0), axis=0)
        return jnp.dot(inverse, summed, precision=precise)

    group_size = math.gcd(blocks_all, 8)
    grouped = sources.reshape(blocks_all // group_size, group_size)
    outputs = lax.map(jax.vmap(one_target), grouped).reshape(
        (blocks_all, length, responses.shape[-1])
    )
    blocks = jnp.stack([outputs[:pair_count], jnp.flip(outputs[pair_count:], axis=0)], axis=0)
    returned = lax.all_to_all(blocks, "ctx", split_axis=1, concat_axis=3, tiled=True)
    convolved = returned[:, 0]
    activated = (queries * (convolved + skip_gain * gated_keys.astype(jnp.float32))).astype(
        jnp.bfloat16
    )
    token_rows = activated.reshape(2 * length, activated.shape[-1])
    channels = token_rows.shape[1]
    owned = lax.psum_scatter(
        lax.dot_general(
            out_weight, token_rows, (((0,), (1,)), ((), ())), preferred_element_type=jnp.float32
        ).astype(jnp.bfloat16),
        "ch",
        scatter_dimension=0,
        tiled=True,
    ).astype(jnp.float32)
    result = owned.T
    return result.astype(jnp.bfloat16).reshape(2, 1, length, channels)


def solution(mesh):
    in_specs = (
        P(None, "ctx", None, None, "ch"),
        P(None, None, "ch"),
        P(None, "ctx", None, "ch"),
        P("ch"),
        P("ch", None),
    )
    out_specs = P(None, "ctx", None, "ch")
    shape = dict(mesh.shape)
    suits = shape == {"ctx": PAIRS, "ch": 8}
    body = fused if suits else local
    return jax.shard_map(body, mesh=mesh, in_specs=in_specs, out_specs=out_specs, check_vma=False)
```

```python
import math

import jax
import jax.numpy as jnp
import ml_dtypes
import numpy as np
from jax import lax
from jax.experimental import pallas as pl
from jax.experimental.pallas import tpu as pltpu
from jax.sharding import PartitionSpec as P

F32 = jnp.float32
BF16 = jnp.bfloat16
MESH = pl.DeviceIdType.MESH
RIM = 8
STRIP = 64
LANES = 128
PAIRS = 4


def halves(values):
    high = values.astype(ml_dtypes.bfloat16)
    low = (values - high.astype(np.float64)).astype(ml_dtypes.bfloat16)
    return np.stack([high, low])


def odd_tables(length):
    k = np.arange(length)[:, None]
    t = np.arange(length)[None, :]
    angles = ((2 * k + 1) * t % (4 * length)) * (np.pi / (2 * length))
    forward = np.concatenate([np.cos(angles), -np.sin(angles)], axis=0)
    return halves(forward), halves(forward.T / length)


def dot(a, b):
    return jnp.dot(a, b, preferred_element_type=F32)


def kernel(
    x_hbm,
    taps_hbm,
    filter_hbm,
    skip_hbm,
    weight_hbm,
    forward_hbm,
    inverse_hbm,
    out_ref,
    x_ref,
    taps_ref,
    filter_ref,
    skip_ref,
    weight,
    forward,
    inverse,
    rim_out,
    halo,
    wide,
    gated,
    queries,
    moved,
    convolved,
    back,
    filter_spec,
    key_spec,
    summed_spec,
    early,
    own,
    act,
    pair_out,
    pair_in,
    first_out,
    first_in,
    second_out,
    second_in,
    local_sem,
    filter_sem,
    halo_send,
    halo_recv,
    move_send,
    move_recv,
    back_send,
    back_recv,
    pair_send,
    pair_recv,
    first_send,
    first_recv,
    second_send,
    second_recv,
):
    rows = gated.shape[2]
    channels = weight.shape[0]
    taps = taps_ref.shape[1]
    middle = forward.shape[2]
    z = lax.axis_index("ctx")
    ch = lax.axis_index("ch")
    core, x, y = ch % 2, ch // 2 % 2, ch // 4

    def ch_of(yy, xx, cc):
        return yy * 4 + xx * 2 + cc

    partner = (z, ch_of(y, x, 1 - core))
    beside_x = (z, ch_of(y, 1 - x, core))
    beside_y = (z, ch_of(1 - y, x, core))

    sources = (x_hbm, taps_hbm, skip_hbm, forward_hbm, inverse_hbm, weight_hbm)
    places = (x_ref, taps_ref, skip_ref, forward, inverse, weight)
    loads = [
        pltpu.make_async_copy(source, target, local_sem.at[i])
        for i, (source, target) in enumerate(zip(sources, places))
    ]
    filter_loads = [
        pltpu.make_async_copy(
            filter_hbm.at[h, :, pl.ds(c * LANES, LANES)], filter_ref.at[h, c], filter_sem.at[h, c]
        )
        for h in range(2)
        for c in range(channels // LANES)
    ]
    for load in (loads[0], *filter_loads, loads[1], loads[2]):
        load.start()

    barrier = pltpu.get_barrier_semaphore()
    peers = [((z + o) % PAIRS, ch) for o in range(1, PAIRS)] + [partner, beside_x, beside_y]
    for peer in peers:
        pl.semaphore_signal(barrier, inc=1, device_id=peer, device_id_type=MESH)
    pl.semaphore_wait(barrier, len(peers))

    for load in loads[3:]:
        load.start()
    pending = []

    def remote(src, dst, send, recv, device):
        return pltpu.make_async_remote_copy(
            src_ref=src, dst_ref=dst, send_sem=send, recv_sem=recv, device_id=device, device_id_type=MESH
        )

    def keep(kind, source, h):
        moved[kind, h, block_of(h, z)] = source[h, z]

    def block_of(h, owner):
        return owner if h == 0 else PAIRS - 1 - owner

    def scatter(kind, source, h):
        copies = []
        for o in (2, 1, 3):
            target = (z + o) % PAIRS
            copy = remote(
                source.at[h, target],
                moved.at[kind, h, block_of(h, z)],
                move_send.at[kind, h, o - 1],
                move_recv.at[kind, h, o - 1],
                (target, ch),
            )
            copy.start()
            copies.append(copy)
        pending.extend(copies)
        return copies

    filter_copies, key_copies = [None, None], [None, None]
    loads[0].wait()

    def widen(h):
        for s in range(3):
            wide[h, s, RIM:] = x_ref[h, s].astype(F32)

    tails = [[x_ref[h, s, rows - 2 * RIM :].astype(F32)[RIM:] for s in range(3)] for h in range(2)]
    rims = {}
    for kind, streams in ((0, (1, 2)), (1, (0, 0))):
        for h in range(2):
            rim_out[kind, h] = jnp.concatenate([tails[h][s] for s in streams], axis=0).astype(BF16)
            rims[kind, h] = remote(
                rim_out.at[kind, h],
                halo.at[kind, h],
                halo_send.at[kind, h],
                halo_recv.at[kind, h],
                ((z + (1 if h == 0 else 3)) % PAIRS, ch),
            )

    def send_rims(kind):
        @pl.when(z < PAIRS - 1)
        def _():
            rims[kind, 0].start()

        @pl.when(z > 0)
        def _():
            rims[kind, 1].start()

    def take_rim(kind, h):
        has = z > 0 if h == 0 else z < PAIRS - 1

        @pl.when(has)
        def _():
            rims[kind, h].wait_recv()

        @pl.when(jnp.logical_not(has))
        def _():
            halo[kind, h] = jnp.zeros(halo.shape[2:], BF16) if h == 0 else rim_out[kind, 0]

        both = halo[kind, h].astype(F32)
        for m, s in enumerate((1, 2) if kind == 0 else (0,)):
            wide[h, s, :RIM] = both[m * RIM : (m + 1) * RIM]

    send_rims(0)
    for load in filter_loads:
        load.wait()
    filter_copies[0] = scatter(0, filter_ref, 0)
    send_rims(1)
    widen(0)
    widen(1)

    loads[1].wait()
    tap_rows = [taps_ref[s].astype(F32) for s in range(3)]

    def taps_of(h, s, cols):
        total = None
        for i in range(taps):
            tap = tap_rows[s][i : i + 1, cols]
            term = tap * wide[h, s, pl.ds(RIM - i, rows), cols]
            total = term if total is None else total + term
        return total

    columns = [slice(a, a + LANES) for a in range(0, channels, LANES)]

    def make_keys(h):
        for c, cols in enumerate(columns):
            gated[h, c] = (taps_of(h, 1, cols) * taps_of(h, 2, cols)).astype(BF16)

    def make_queries(h):
        for cols in columns:
            queries[h, :, cols] = taps_of(h, 0, cols)

    take_rim(0, 0)
    make_keys(0)
    key_copies[0] = scatter(1, gated, 0)
    keep(1, gated, 0)
    filter_copies[1] = scatter(0, filter_ref, 1)
    keep(0, filter_ref, 0)
    keep(0, filter_ref, 1)
    take_rim(0, 1)
    make_keys(1)
    key_copies[1] = scatter(1, gated, 1)
    keep(1, gated, 1)
    for h in range(2):
        take_rim(1, h)
        make_queries(h)
    loads[3].wait()

    signs = (1 - 2 * (lax.broadcasted_iota(jnp.int32, (middle, LANES), 0) % 2)).astype(F32)

    def spectrum(kind, h):
        data = jnp.concatenate(
            [jnp.concatenate([moved[kind, h, 2 * m], moved[kind, h, 2 * m + 1]], axis=0) for m in range(2)], axis=1
        )
        return dot(forward[0], data) + dot(forward[1], data)

    def filter_spectra(h):
        for copy in filter_copies[h]:
            copy.wait_recv()
        both = spectrum(0, h)
        for m in range(2):
            filter_spec[0, 2 * h + m] = both[:, m * LANES : (m + 1) * LANES]
        for b in (2 * h, 2 * h + 1):
            if b == 0:
                filter_spec[1, 0] = filter_spec[0, 0]
            else:
                filter_spec[1, b, :middle] = filter_spec[0, b, :middle] - signs * filter_spec[0, b - 1, middle:]
                filter_spec[1, b, middle:] = filter_spec[0, b, middle:] + signs * filter_spec[0, b - 1, :middle]

    def key_spectra(h):
        for copy in key_copies[h]:
            copy.wait_recv()
        both = spectrum(1, h)
        for m in range(2):
            key_spec[2 * h + m] = both[:, m * LANES : (m + 1) * LANES]

    def pair_products(i, sources, re_rows, im_rows):
        real, imag = None, None
        for j in sources:
            ra, ia = filter_spec[1, i - j, re_rows], filter_spec[1, i - j, im_rows]
            rb, ib = key_spec[j, re_rows], key_spec[j, im_rows]
            re, im = ra * rb - ia * ib, ra * ib + ia * rb
            real = re if real is None else real + re
            imag = im if imag is None else imag + im
        return real, imag

    strips = [
        (slice(start, start + STRIP), slice(middle + start, middle + start + STRIP))
        for start in range(0, middle, STRIP)
    ]

    def early_products():
        for m in range(2):
            for re_rows, im_rows in strips:
                early[m, re_rows], early[m, im_rows] = pair_products(2 + m, (0, 1), re_rows, im_rows)

    def products(h):
        for m in range(2):
            i = 2 * h + m
            cols = slice(m * LANES, (m + 1) * LANES)
            for re_rows, im_rows in strips:
                sums = pair_products(i, range(2 * h, i + 1), re_rows, im_rows)
                for where, value in zip((re_rows, im_rows), sums):
                    if h == 1:
                        value = value + early[m, where]
                    high = value.astype(BF16)
                    summed_spec[0, where, cols] = high
                    summed_spec[1, where, cols] = (value - high.astype(F32)).astype(BF16)

    chunks = [(h, first_row, rows // 2) for h in range(2) for first_row in (0, rows // 2)]
    back_copies = {}

    def send_back(q):
        h, first_row, count = chunks[q]
        copies = []
        for o in (2, 1, 3):
            target = (z + o) % PAIRS
            copy = remote(
                convolved.at[h, block_of(h, target), pl.ds(first_row, count)],
                back.at[h, z, pl.ds(first_row, count)],
                back_send.at[q, o - 1],
                back_recv.at[q, o - 1],
                (target, ch),
            )
            copy.start()
            copies.append(copy)
        back[h, z, pl.ds(first_row, count)] = convolved[h, block_of(h, z), pl.ds(first_row, count)]
        pending.extend(copies)
        back_copies[q] = copies

    def convolve(h):
        products(h)
        high, low = summed_spec[0], summed_spec[1]
        result = dot(inverse[0], high) + dot(inverse[0], low) + dot(inverse[1], high)
        result = result.astype(BF16)
        for block in range(PAIRS):
            m, part = divmod(block, 2)
            convolved[h, block] = result[part * rows : (part + 1) * rows, m * LANES : (m + 1) * LANES]

    filter_spectra(0)
    key_spectra(0)
    loads[4].wait()
    convolve(0)
    send_back(0)
    send_back(1)
    filter_spectra(1)
    early_products()
    key_spectra(1)
    convolve(1)
    send_back(2)
    send_back(3)
    loads[5].wait()
    loads[2].wait()

    steps = [(1, 1), (0, 1), (1, 0), (0, 0)]
    pair_copies = {}

    def parts(q):
        h, first_row, count = chunks[q]
        half = count // 2
        return slice(first_row, first_row + half), slice(first_row + half, first_row + count)

    def slot_rows(q):
        return pl.ds(chunks[q][1] // 2, chunks[q][2] // 2)

    def weights_for(step, cc):
        yy = 1 - y if step[0] else y
        xx = 1 - x if step[1] else x
        return weight[:, pl.ds(pl.multiple_of(ch_of(yy, xx, cc) * channels, channels), channels)]

    def project(q):
        h, first_row, count = chunks[q]
        span = slice(first_row, first_row + count)
        for copy in back_copies[q]:
            copy.wait_recv()
        for c, cols in enumerate(columns):
            summed = back[h, c, span].astype(F32) + skip_ref[:, cols] * gated[h, c, span].astype(F32)
            act[h, span, cols] = (queries[h, span, cols] * summed).astype(BF16)
        rows_in = act[h, span]
        for t, step in enumerate(steps):
            pair_out[h, t, span] = dot(rows_in, weights_for(step, 1 - core)).astype(BF16)
            copy = remote(
                pair_out.at[h, t, pl.ds(first_row, count)],
                pair_in.at[h, t, pl.ds(first_row, count)],
                pair_send.at[q, t],
                pair_recv.at[q, t],
                partner,
            )
            copy.start()
            pair_copies[q, t] = copy
            pending.append(copy)

    def project_own(q, t):
        h, first_row, count = chunks[q]
        span = slice(first_row, first_row + count)
        own[h, t, span] = dot(act[h, span], weights_for(steps[t], core))

    first_copies, second_copies = {}, {}

    def pair_sum(q, t, way):
        h, part = chunks[q][0], parts(q)[way]
        return own[h, t, part] + pair_in[h, t, part].astype(F32)

    def first(q):
        h, where = chunks[q][0], slot_rows(q)
        for t, way, slot in ((0, 0, 0), (0, 1, 0), (1, 0, 1), (2, 1, 1)):
            if (t, way) != (0, 1):
                project_own(q, t)
                pair_copies[q, t].wait_recv()
            first_out[h, way, slot, where] = pair_sum(q, t, way).astype(BF16)
            copy = remote(
                first_out.at[h, way, slot, where],
                first_in.at[h, way, slot, where],
                first_send.at[q, way, slot],
                first_recv.at[q, way, slot],
                beside_y if way else beside_x,
            )
            copy.start()
            first_copies[q, way, slot] = copy
            pending.append(copy)
        project_own(q, 3)

    def second(q):
        h, where = chunks[q][0], slot_rows(q)
        for way in range(2):
            first_copies[q, way, 0].wait_recv()
            t = 1 if way else 2
            total = pair_sum(q, t, way) + first_in[h, way, 0, where].astype(F32)
            second_out[h, way, where] = total.astype(BF16)
            copy = remote(
                second_out.at[h, way, where],
                second_in.at[h, way, where],
                second_send.at[q, way],
                second_recv.at[q, way],
                beside_x if way else beside_y,
            )
            copy.start()
            second_copies[q, way] = copy
            pending.append(copy)

    def finish(q):
        h, where = chunks[q][0], slot_rows(q)
        pair_copies[q, 3].wait_recv()
        for way in range(2):
            first_copies[q, way, 1].wait_recv()
            total = pair_sum(q, 3, way) + first_in[h, way, 1, where].astype(F32)
            second_copies[q, way].wait_recv()
            out_ref[h, parts(q)[way]] = (total + second_in[h, way, where].astype(F32)).astype(BF16)

    project(0)
    first(0)
    project(1)
    first(1)
    project(2)
    second(0)
    first(2)
    project(3)
    second(1)
    first(3)
    finish(0)
    second(2)
    finish(1)
    second(3)
    finish(2)
    finish(3)

    @pl.when(z < PAIRS - 1)
    def _():
        rims[0, 0].wait_send()
        rims[1, 0].wait_send()

    @pl.when(z > 0)
    def _():
        rims[0, 1].wait_send()
        rims[1, 1].wait_send()

    for copy in pending:
        copy.wait_send()


def fused(features, short_weight, long_filter, skip_gain, out_weight):
    rows, channels = long_filter.shape[2:]
    middle = 2 * rows
    streams = jnp.transpose(features[:, 0], (0, 2, 1, 3))
    taps = jnp.transpose(short_weight, (1, 0, 2))
    forward, inverse = odd_tables(middle)
    blocked = (2, channels // LANES, rows, LANES)
    in_vmem = pl.BlockSpec(memory_space=pltpu.VMEM)
    in_hbm = pl.BlockSpec(memory_space=pl.ANY)
    vmem = pltpu.VMEM
    dma = pltpu.SemaphoreType.DMA
    out = pl.pallas_call(
        kernel,
        out_shape=pltpu.VMEM((2, rows, channels), BF16),
        in_specs=[in_hbm] * 7,
        out_specs=in_vmem,
        scratch_shapes=[
            vmem(streams.shape, BF16),
            vmem(taps.shape, BF16),
            vmem(blocked, BF16),
            vmem((1, channels), F32),
            vmem(out_weight.shape, BF16),
            vmem(forward.shape, BF16),
            vmem(inverse.shape, BF16),
            vmem((2, 2, 2 * RIM, channels), BF16),
            vmem((2, 2, 2 * RIM, channels), BF16),
            vmem((2, 3, RIM + rows, channels), F32),
            vmem(blocked, BF16),
            vmem((2, rows, channels), F32),
            vmem((2, *blocked), BF16),
            vmem(blocked, BF16),
            vmem(blocked, BF16),
            vmem((2, 4, 2 * middle, LANES), F32),
            vmem((4, 2 * middle, LANES), F32),
            vmem((2, 2 * middle, 2 * LANES), BF16),
            vmem((2, 2 * middle, LANES), F32),
            vmem((2, 4, rows, channels), F32),
            vmem((2, rows, channels), BF16),
            vmem((2, 4, rows, channels), BF16),
            vmem((2, 4, rows, channels), BF16),
            vmem((2, 2, 2, rows // 2, channels), BF16),
            vmem((2, 2, 2, rows // 2, channels), BF16),
            vmem((2, 2, rows // 2, channels), BF16),
            vmem((2, 2, rows // 2, channels), BF16),
            dma((6,)),
            dma((2, channels // LANES)),
            dma((2, 2)),
            dma((2, 2)),
            dma((2, 2, 3)),
            dma((2, 2, 3)),
            dma((4, 3)),
            dma((4, 3)),
            dma((4, 4)),
            dma((4, 4)),
            dma((4, 2, 2)),
            dma((4, 2, 2)),
            dma((4, 2)),
            dma((4, 2)),
        ],
        compiler_params=pltpu.CompilerParams(
            collective_id=0, has_side_effects=True, vmem_limit_bytes=62 * 1024 * 1024
        ),
        name="hyena",
    )(
        streams,
        taps,
        long_filter[:, 0],
        skip_gain.reshape(1, channels),
        out_weight,
        jnp.asarray(forward),
        jnp.asarray(inverse),
    )
    return out[:, None]


def from_behind(value, axis, steps):
    count = lax.axis_size(axis)
    initial, last = (max(0, -steps), min(count, count - steps))
    return lax.ppermute(value, axis, [(source, source + steps) for source in range(initial, last)])


def transform_tables(length):
    period = 2 * length
    indices = jnp.arange(period, dtype=jnp.int32)
    phases = indices[:, None] * indices[None, :] % period
    angles = phases.astype(jnp.float32) * (2.0 * math.pi / period)
    cosine = jnp.cos(angles)
    sine_table = jnp.sin(angles)
    forward_full = jnp.concatenate([cosine, -sine_table], axis=0)
    forward_data = forward_full[:, :length]
    inverse = jnp.concatenate([cosine[:length], -sine_table[:length]], axis=1) / period
    return (forward_full, forward_data, inverse)


def complex_product(first, second):
    middle = first.shape[-2] // 2
    real_a = first[..., :middle, :]
    imag_a = first[..., middle:, :]
    real_b = second[..., :middle, :]
    imag_b = second[..., middle:, :]
    return jnp.concatenate(
        [real_a * real_b - imag_a * imag_b, real_a * imag_b + imag_a * real_b], axis=-2
    )


def featurize(tokens, before, kernel):
    extended = jnp.concatenate([before, tokens], axis=0).astype(jnp.float32)
    length = tokens.shape[0]
    margin_rows = kernel.shape[0] - 1
    summed = jnp.zeros(tokens.shape, jnp.float32)
    for offset in range(kernel.shape[0]):
        summed = (
            summed
            + kernel[offset].astype(jnp.float32)
            * extended[margin_rows - offset : margin_rows - offset + length]
        )
    return summed


def ordered(blocks):
    return jnp.concatenate([blocks[0], jnp.flip(blocks[1], axis=0)], axis=0)


def local(features, short_weight, long_filter, skip_gain, out_weight):
    pair_count = lax.axis_size("ctx")
    blocks_all = 2 * pair_count
    position = lax.axis_index("ctx")
    length = features.shape[2]
    margin_rows = short_weight.shape[0] - 1
    trailing = features[:, 0, length - margin_rows :]
    from_before = from_behind(trailing[0], "ctx", 1)
    from_after = from_behind(trailing[1], "ctx", -1)
    second_rim = jnp.where(position == pair_count - 1, trailing[0], from_after)
    first_feat = featurize(features[0, 0], from_before, short_weight)
    second_feat = featurize(features[1, 0], second_rim, short_weight)
    featured = jnp.stack([first_feat, second_feat], axis=0)
    queries = featured[:, :, 0]
    gated_keys = (featured[:, :, 1] * featured[:, :, 2]).astype(jnp.bfloat16)
    forward_full, forward_data, inverse = transform_tables(length)
    precise = lax.Precision.HIGHEST
    moved_gated, moved_filter = (
        lax.all_to_all(gated_keys[:, None], "ctx", split_axis=3, concat_axis=1, tiled=True),
        lax.all_to_all(long_filter, "ctx", split_axis=3, concat_axis=1, tiled=True),
    )
    ordered_gated = ordered(moved_gated).astype(jnp.float32)
    lag_order = ordered(moved_filter)
    padded = jnp.concatenate(
        [jnp.zeros((1,) + lag_order.shape[1:], lag_order.dtype), lag_order], axis=0
    )
    segments = jnp.concatenate([padded[1:], padded[:-1]], axis=1).astype(jnp.float32)
    responses = jnp.einsum("fm,kmc->kfc", forward_full, segments, precision=precise)
    spectra = jnp.einsum("fn,knc->kfc", forward_data, ordered_gated, precision=precise)
    sources = jnp.arange(blocks_all, dtype=jnp.int32)

    def one_target(target):
        distance = target - sources
        picked = jnp.take(responses, jnp.maximum(distance, 0), axis=0)
        products = complex_product(picked, spectra)
        summed = jnp.sum(jnp.where((distance >= 0)[:, None, None], products, 0.0), axis=0)
        return jnp.dot(inverse, summed, precision=precise)

    group_size = math.gcd(blocks_all, 8)
    grouped = sources.reshape(blocks_all // group_size, group_size)
    outputs = lax.map(jax.vmap(one_target), grouped).reshape(
        (blocks_all, length, responses.shape[-1])
    )
    blocks = jnp.stack([outputs[:pair_count], jnp.flip(outputs[pair_count:], axis=0)], axis=0)
    returned = lax.all_to_all(blocks, "ctx", split_axis=1, concat_axis=3, tiled=True)
    convolved = returned[:, 0]
    activated = (queries * (convolved + skip_gain * gated_keys.astype(jnp.float32))).astype(
        jnp.bfloat16
    )
    token_rows = activated.reshape(2 * length, activated.shape[-1])
    channels = token_rows.shape[1]
    owned = lax.psum_scatter(
        lax.dot_general(
            out_weight, token_rows, (((0,), (1,)), ((), ())), preferred_element_type=jnp.float32
        ).astype(jnp.bfloat16),
        "ch",
        scatter_dimension=0,
        tiled=True,
    ).astype(jnp.float32)
    result = owned.T
    return result.astype(jnp.bfloat16).reshape(2, 1, length, channels)


def solution(mesh):
    in_specs = (
        P(None, "ctx", None, None, "ch"),
        P(None, None, "ch"),
        P(None, "ctx", None, "ch"),
        P("ch"),
        P("ch", None),
    )
    out_specs = P(None, "ctx", None, "ch")
    shape = dict(mesh.shape)
    suits = shape == {"ctx": PAIRS, "ch": 8}
    body = fused if suits else local
    return jax.shard_map(body, mesh=mesh, in_specs=in_specs, out_specs=out_specs, check_vma=False)
```
